32 devices in a mesh: groups: 2 (over x), cols: 4 (over y, core), rows: 4 (over z).
Axes of the slice: x: 2, y: 2, z: 4, core: 2. Of those that a mesh axis runs over, the one named last changes fastest.
Arguments:
- camera_tokens: bfloat16 [1024, 6144], P(('groups', 'rows'), 'cols'), parts along dimension 0, may hold values from -150 to 150, as said below
- norm_gain: float32 [6144], P('cols'), may hold values from 0.25 to 1.75
- query_weight: bfloat16 [6144, 6144], P('cols', 'rows'), may hold values from -0.078125 to 0.078125
- key_weight: bfloat16 [6144, 6144], P('cols', 'rows'), may hold values from -0.078125 to 0.078125
- value_weight: bfloat16 [6144, 6144], P('cols', 'rows'), may hold values from -0.078125 to 0.078125
- query_gain: float32 [6144], P('rows'), may hold values from 0.5 to 14, as said below
- key_gain: float32 [6144], P('rows'), may hold values from 0.5 to 14, as said below
- out_weight: bfloat16 [6144, 6144], P('rows', 'cols'), may hold values from -0.078125 to 0.078125
- up_weight: bfloat16 [6144, 24576], P('cols', 'rows'), may hold values from -0.078125 to 0.078125
- up_bias: float32 [24576], P('rows'), may hold values from -3 to 3
- down_weight: bfloat16 [24576, 6144], P('rows', 'cols'), may hold values from -0.0390625 to 0.0390625
- down_bias: float32 [6144], P('cols'), may hold values from -3 to 3
- join_gain: float32 [6144], P('cols'), may hold values from 0.25 to 1.75
- join_query: bfloat16 [6144, 6144], P('cols', 'rows'), may hold values from -0.078125 to 0.078125
- join_key: bfloat16 [6144, 6144], P('cols', 'rows'), may hold values from -0.078125 to 0.078125
- join_value: bfloat16 [6144, 6144], P('cols', 'rows'), may hold values from -0.078125 to 0.078125
- join_query_gain: float32 [6144], P('rows'), may hold values from 0.5 to 14, as said below
- join_key_gain: float32 [6144], P('rows'), may hold values from 0.5 to 14, as said below
- join_out: bfloat16 [6144, 6144], P('rows', 'cols'), may hold values from -0.078125 to 0.078125
Outputs:
- joined_tokens: bfloat16 [1024, 6144], P(('groups', 'rows'), 'cols'), parts along dimension 0
The draws below stay inside these ranges and needn't reach their ends.
There are 2 independent parts, one for each index of `groups`. The reference program is written for one: setup_inputs(seed, part) draws one part's arguments, and reference() takes and returns one part's arrays. A program takes and returns all parts, laid end to end along the dimension named above; an argument that names none is the same for every part. Nothing has to cross between parts.
Inputs may be any that keep to these rules, and one draw needn't show every extreme that they name: `camera_tokens`: real valued tokens. `query_gain`: Positive. `key_gain`: Positive. `join_query_gain`: Positive. `join_key_gain`: Positive.
All inputs are finite; a program needn't handle non-finite values.
Results may differ from the reference program's by a relative error of at most 0.012.
Values may be sent and summed in bfloat16 or wider, within the bound.
No kernel may reach another device: no remote copies, remote signals or barrier semaphores. Data moves between devices by JAX's collectives and lax.ppermute only.
A program may use at most 192 MiB of HBM per device.

```python
import math
import jax
import jax.numpy as jnp
from jax import lax

HEADS = 48
HEAD_DIM = 128
FF = 24576
CAMERAS = 8
TOK_CAM = 64
D = 6144
TOKENS = 512


def head_scales(key):
    subkeys = jax.random.split(key, 2)
    per_head = jnp.exp(jax.random.uniform(subkeys[0], (HEADS, 1), jnp.float32, math.log(1.2), math.log(3.5)))
    jitter = jax.random.uniform(subkeys[1], (HEADS, HEAD_DIM), jnp.float32, 0.8, 1.25)
    return (per_head * jitter).reshape(HEADS * HEAD_DIM)


def draw_query_gain(key, part):
    return head_scales(jax.random.fold_in(key, 11))


def draw_key_gain(key, part):
    return head_scales(jax.random.fold_in(key, 23))


def draw_join_query_gain(key, part):
    return head_scales(jax.random.fold_in(key, 37))


def draw_join_key_gain(key, part):
    return head_scales(jax.random.fold_in(key, 41))


def draw_camera_tokens(key, part):
    subkeys = jax.random.split(jax.random.fold_in(key, 5), 3)
    width = HEADS * HEAD_DIM
    gaussian = jax.random.truncated_normal(subkeys[0], -4.0, 4.0, (TOKENS, width), jnp.float32)
    rising = 3.0 ** (jnp.arange(width, dtype=jnp.float32) / width)
    row_scale = jnp.exp(jax.random.uniform(subkeys[1], (TOKENS, 1), jnp.float32, math.log(0.5), math.log(2.0)))
    col_scale = jnp.exp(jax.random.uniform(subkeys[2], (1, width), jnp.float32, math.log(0.6), math.log(1.6))) * rising
    return (gaussian * row_scale * col_scale).astype(jnp.bfloat16)


def levels(own_key, shape, shards, low, top_value):
    loudness = 1.0
    for dim, shards_of in shards:
        steps = jax.random.uniform(jax.random.fold_in(jax.random.fold_in(own_key, 6), dim), (shards_of,), jnp.float32, low / len(shards), top_value / len(shards))
        loudness = loudness * jnp.repeat(jnp.exp(steps), shape[dim] // shards_of).reshape((-1,) + (1,) * (len(shape) - 1 - dim))
    return loudness


def noise(own_key, extent, scale, most, cuts=(), kind=jnp.bfloat16):
    drawn = scale * jax.random.normal(own_key, extent, jnp.float32)
    if cuts:
        drawn = drawn * levels(own_key, extent, cuts, -0.22, 0.18)
    return jnp.clip(drawn, -most, most).astype(kind)


def setup_inputs(seed: int = 0, part: int = 0) -> dict:
    arg_keys = jax.random.split(jax.random.key(seed), 20)
    part_keys = jax.random.split(jax.random.fold_in(arg_keys[19], part), 20)
    return {
        "camera_tokens": draw_camera_tokens(jax.random.fold_in(jax.random.fold_in(arg_keys[19], part), 71), part),
        "norm_gain": jnp.clip(1.0 + 0.15 * jax.random.normal(arg_keys[1], (D,), jnp.float32), 0.25, 1.75),
        "query_weight": noise(arg_keys[2], (D, D), D ** -0.5, 0.078125, ((0, 4), (1, 4))),
        "key_weight": noise(arg_keys[3], (D, D), D ** -0.5, 0.078125, ((0, 4), (1, 4))),
        "value_weight": noise(arg_keys[4], (D, D), D ** -0.5, 0.078125, ((0, 4), (1, 4))),
        "query_gain": draw_query_gain(jax.random.fold_in(arg_keys[19], 71), part),
        "key_gain": draw_key_gain(jax.random.fold_in(arg_keys[19], 71), part),
        "out_weight": noise(arg_keys[7], (D, D), D ** -0.5, 0.078125, ((0, 4), (1, 4))),
        "up_weight": noise(arg_keys[8], (D, FF), D ** -0.5, 0.078125, ((0, 4), (1, 4))),
        "up_bias": noise(arg_keys[9], (FF,), 0.5, 3.0, ((0, 4),), jnp.float32),
        "down_weight": noise(arg_keys[10], (FF, D), FF ** -0.5, 0.0390625, ((0, 4), (1, 4))),
        "down_bias": noise(arg_keys[11], (D,), 0.5, 3.0, ((0, 4),), jnp.float32),
        "join_gain": jnp.clip(1.0 + 0.15 * jax.random.normal(arg_keys[12], (D,), jnp.float32), 0.25, 1.75),
        "join_query": noise(arg_keys[13], (D, D), D ** -0.5, 0.078125, ((0, 4), (1, 4))),
        "join_key": noise(arg_keys[14], (D, D), D ** -0.5, 0.078125, ((0, 4), (1, 4))),
        "join_value": noise(arg_keys[15], (D, D), D ** -0.5, 0.078125, ((0, 4), (1, 4))),
        "join_query_gain": draw_join_query_gain(jax.random.fold_in(arg_keys[19], 71), part),
        "join_key_gain": draw_join_key_gain(jax.random.fold_in(arg_keys[19], 71), part),
        "join_out": noise(arg_keys[18], (D, D), D ** -0.5, 0.078125, ((0, 4), (1, 4))),
    }


EPS = 1e-06

def layer_norm(values, scales):
    row_mean = lax.optimization_barrier(jnp.mean(values, -1, keepdims=True))
    row_var = lax.optimization_barrier(jnp.mean(values * values, -1, keepdims=True)) - row_mean * row_mean
    return ((values - row_mean) * lax.rsqrt(row_var + EPS) * scales).astype(jnp.bfloat16)

def head_norm(values, scales):
    row_count = values.shape[0]
    grouped = values.reshape(row_count, -1, HEAD_DIM)
    row_mean = lax.optimization_barrier(jnp.mean(grouped, -1, keepdims=True))
    row_var = lax.optimization_barrier(jnp.mean(grouped * grouped, -1, keepdims=True)) - row_mean * row_mean
    normed = (grouped - row_mean) * lax.rsqrt(row_var + EPS)
    return (normed.reshape(row_count, -1) * scales).astype(jnp.bfloat16)

def attend(queries, key_rows, val_rows):
    inv_root = 1.0 / math.sqrt(HEAD_DIM)
    scores = jnp.einsum('bqhd,bkhd->bhqk', queries.astype(jnp.float32), key_rows.astype(jnp.float32)) * inv_root
    row_max = lax.optimization_barrier(jnp.max(scores, -1, keepdims=True))
    weights = jnp.exp(scores - row_max)
    row_sum = lax.optimization_barrier(jnp.sum(weights, -1))
    rounded = lax.optimization_barrier(weights.astype(jnp.bfloat16)).astype(jnp.float32)
    blended = jnp.einsum('bhqk,bkhd->bqhd', rounded, val_rows.astype(jnp.float32))
    return blended / jnp.transpose(row_sum, (0, 2, 1))[..., None]

def reference(camera_tokens, norm_gain, query_weight, key_weight, value_weight, query_gain, key_gain, out_weight, up_weight, up_bias, down_weight, down_bias, join_gain, join_query, join_key, join_value, join_query_gain, join_key_gain, join_out):
    start_f32 = camera_tokens.astype(jnp.float32)
    normed = layer_norm(start_f32, norm_gain)
    query_raw = jnp.dot(normed, query_weight, preferred_element_type=jnp.float32)
    key_raw = jnp.dot(normed, key_weight, preferred_element_type=jnp.float32)
    value_raw = jnp.dot(normed, value_weight, preferred_element_type=jnp.float32)
    up_raw = jnp.dot(normed, up_weight, preferred_element_type=jnp.float32)
    query_normed = head_norm(query_raw, query_gain)
    key_normed = head_norm(key_raw, key_gain)
    value_rounded = value_raw.astype(jnp.bfloat16)
    cam_shape = (CAMERAS, TOK_CAM, HEADS, HEAD_DIM)
    attended = attend(query_normed.reshape(cam_shape), key_normed.reshape(cam_shape), value_rounded.reshape(cam_shape))
    attended = attended.reshape(TOKENS, D).astype(jnp.bfloat16)
    hidden = jax.nn.gelu(up_raw + up_bias, approximate=False).astype(jnp.bfloat16)
    mixed = jnp.dot(attended, out_weight, preferred_element_type=jnp.float32) + jnp.dot(hidden, down_weight, preferred_element_type=jnp.float32)
    camera_out = (start_f32 + mixed + down_bias).astype(jnp.bfloat16)
    layer_f32 = camera_out.astype(jnp.float32)
    join_normed = layer_norm(layer_f32, join_gain)
    join_q = head_norm(jnp.dot(join_normed, join_query, preferred_element_type=jnp.float32), join_query_gain)
    join_k = head_norm(jnp.dot(join_normed, join_key, preferred_element_type=jnp.float32), join_key_gain)
    join_v = jnp.dot(join_normed, join_value, preferred_element_type=jnp.float32).astype(jnp.bfloat16)
    all_shape = (1, TOKENS, HEADS, HEAD_DIM)
    join_attended = attend(join_q.reshape(all_shape), join_k.reshape(all_shape), join_v.reshape(all_shape))
    join_attended = join_attended.reshape(TOKENS, D).astype(jnp.bfloat16)
    return (layer_f32 + jnp.dot(join_attended, join_out, preferred_element_type=jnp.float32)).astype(jnp.bfloat16)
```

```python
import math

import jax
import jax.numpy as jnp
from jax import lax
from jax.experimental import pallas as pl
from jax.experimental.pallas import tpu as pltpu
from jax.sharding import PartitionSpec as P

HEAD_DIM = 128
TOK_CAM = 64
D = 6144


EPS = 1e-06


def partner_2(array, axis, bit):
    return lax.ppermute(array, axis, [(i, i ^ 1 << bit) for i in range(lax.axis_size(axis))])


def normalize(values, scales, moments):
    row_mean = moments[0] / D
    row_var = moments[1] / D - row_mean * row_mean
    return ((values - row_mean[:, None]) * lax.rsqrt(row_var[:, None] + EPS) * scales).astype(
        jnp.bfloat16
    )


def shard_moments(values):
    return lax.psum((jnp.sum(values, 1), jnp.sum(values * values, 1)), "cols")


def head_norm(values, scales):
    row_count = values.shape[0]
    grouped = values.reshape(row_count, -1, HEAD_DIM)
    row_mean = jnp.mean(grouped, -1, keepdims=True)
    row_var = jnp.mean(grouped * grouped, -1, keepdims=True) - row_mean * row_mean
    normed = (grouped - row_mean) * lax.rsqrt(row_var + EPS)
    return (normed.reshape(row_count, -1) * scales).astype(jnp.bfloat16)


def attend(queries, key_rows, val_rows):
    inv_root = 1.0 / math.sqrt(HEAD_DIM)
    scores = (
        jnp.einsum("bqhd,bkhd->bhqk", queries, key_rows, preferred_element_type=jnp.float32)
        * inv_root
    )
    row_max = jnp.max(scores, -1, keepdims=True)
    weights = jnp.exp(scores - row_max)
    row_sum = jnp.sum(weights, -1)
    blended = jnp.einsum(
        "bhqk,bkhd->bqhd",
        weights.astype(jnp.bfloat16),
        val_rows,
        preferred_element_type=jnp.float32,
    )
    return blended / jnp.transpose(row_sum, (0, 2, 1))[..., None]


def to_heads(matrix, blocks):
    return matrix.reshape(blocks, -1, matrix.shape[1] // HEAD_DIM, HEAD_DIM)


def camera_attention(queries, key_rows, val_rows):
    local_rows = queries.shape[0]
    if local_rows >= TOK_CAM:
        blocks = local_rows // TOK_CAM
        result = attend(
            to_heads(queries, blocks), to_heads(key_rows, blocks), to_heads(val_rows, blocks)
        )
    else:
        cam_span = TOK_CAM // local_rows
        position = lax.axis_index("cols")
        key_value = jnp.stack((key_rows, val_rows))
        for which_bit in range(cam_span.bit_length() - 1):
            partner = partner_2(key_value, "cols", which_bit)
            is_lower = position >> which_bit & 1 == 0
            key_value = jnp.where(
                is_lower,
                jnp.concatenate((key_value, partner), 1),
                jnp.concatenate((partner, key_value), 1),
            )
        result = attend(to_heads(queries, 1), to_heads(key_value[0], 1), to_heads(key_value[1], 1))
    return result.reshape(local_rows, -1).astype(jnp.bfloat16)


def generic_body(
    camera_tokens,
    norm_gain,
    query_weight,
    key_weight,
    value_weight,
    query_gain,
    key_gain,
    out_weight,
    up_weight,
    up_bias,
    down_weight,
    down_bias,
    join_gain,
    join_query,
    join_key,
    join_value,
    join_query_gain,
    join_key_gain,
    join_out,
):
    own_rows = camera_tokens.shape[0]
    all_rows = own_rows * lax.axis_size("rows")
    col_rows = all_rows // lax.axis_size("cols")
    attn_width = query_weight.shape[1]
    start_f32 = camera_tokens.astype(jnp.float32)
    normed_all = lax.all_gather(
        normalize(start_f32, norm_gain, shard_moments(start_f32)), "rows", axis=0, tiled=True
    )
    joint_weight = jnp.concatenate((query_weight, key_weight, value_weight, up_weight), 1)
    joint = lax.psum_scatter(
        jnp.dot(normed_all, joint_weight, preferred_element_type=jnp.float32),
        "cols",
        scatter_dimension=0,
        tiled=True,
    )
    up_sum = joint[:, 3 * attn_width :]
    hidden = jax.nn.gelu(up_sum + up_bias, approximate=False).astype(jnp.bfloat16)
    attended = camera_attention(
        head_norm(joint[:, :attn_width], query_gain),
        head_norm(joint[:, attn_width : 2 * attn_width], key_gain),
        joint[:, 2 * attn_width : 3 * attn_width].astype(jnp.bfloat16),
    )
    attn_all, hidden_all = (
        lax.all_gather(attended, "cols", axis=0, tiled=True),
        lax.all_gather(hidden, "cols", axis=0, tiled=True),
    )
    mixed = lax.psum_scatter(
        jnp.dot(attn_all, out_weight, preferred_element_type=jnp.float32)
        + jnp.dot(hidden_all, down_weight, preferred_element_type=jnp.float32),
        "rows",
        scatter_dimension=0,
        tiled=True,
    )
    layer_own = (start_f32 + mixed + down_bias).astype(jnp.bfloat16)
    layer_f32 = layer_own.astype(jnp.float32)
    join_in = lax.all_gather(
        normalize(layer_f32, join_gain, shard_moments(layer_f32)), "rows", axis=0, tiled=True
    )
    join_weight = jnp.concatenate((join_query, join_key, join_value), 1)
    join_joint = lax.psum_scatter(
        jnp.dot(join_in, join_weight, preferred_element_type=jnp.float32),
        "cols",
        scatter_dimension=0,
        tiled=True,
    )
    join_q = head_norm(join_joint[:, :attn_width], join_query_gain)
    join_k = head_norm(join_joint[:, attn_width : 2 * attn_width], join_key_gain)
    join_v = join_joint[:, 2 * attn_width :].astype(jnp.bfloat16)
    heads_here = attn_width // HEAD_DIM
    query_heads = join_q.reshape(col_rows, heads_here, HEAD_DIM)
    inv_root = 1.0 / math.sqrt(HEAD_DIM)
    run_max = jnp.full((heads_here, col_rows), -jnp.inf, jnp.float32)
    run_sum = jnp.zeros((heads_here, col_rows), jnp.float32)
    accum = jnp.zeros((col_rows, heads_here, HEAD_DIM), jnp.float32)
    key_part = lax.all_gather(join_k, "cols", axis=0, tiled=True)
    val_part = lax.all_gather(join_v, "cols", axis=0, tiled=True)
    row_count = key_part.shape[0]
    key_heads = key_part.reshape(row_count, heads_here, HEAD_DIM)
    val_heads = val_part.reshape(row_count, heads_here, HEAD_DIM)
    scores = (
        jnp.einsum("qhd,khd->hqk", query_heads, key_heads, preferred_element_type=jnp.float32)
        * inv_root
    )
    new_max = jnp.max(scores, -1)
    factor = jnp.exp(run_max - new_max)
    weights = jnp.exp(scores - new_max[..., None])
    run_sum = run_sum * factor + jnp.sum(weights, -1)
    accum = accum * jnp.transpose(factor)[..., None] + jnp.einsum(
        "hqk,khd->qhd", weights.astype(jnp.bfloat16), val_heads, preferred_element_type=jnp.float32
    )
    run_max, run_sum, accum = (new_max, run_sum, accum)
    joined_attn = (
        (accum / jnp.transpose(run_sum)[..., None])
        .reshape(col_rows, attn_width)
        .astype(jnp.bfloat16)
    )
    joined_all = lax.all_gather(joined_attn, "cols", axis=0, tiled=True)
    result = lax.psum_scatter(
        jnp.dot(joined_all, join_out, preferred_element_type=jnp.float32),
        "rows",
        scatter_dimension=0,
        tiled=True,
    )
    return (layer_own.astype(jnp.float32) + result).astype(jnp.bfloat16)


VMEM_BYTES = 60 * 1024 * 1024


def flip(array, mask):
    size = lax.axis_size("cols")
    return lax.ppermute(array, "cols", [(i, i ^ mask) for i in range(size)])


def core_swap(array):
    return flip(array, 1)


def y_swap(array):
    return flip(array, 2)


def row_shift(array, shift):
    size = lax.axis_size("rows")
    return lax.ppermute(array, "rows", [(i, (i + shift) % size) for i in range(size)])


def compiler_params():
    return pltpu.CompilerParams(vmem_limit_bytes=VMEM_BYTES)


def project(tokens, weights, width, sub, order, out_type, add=None, add_order=None):
    rows, depth = tokens.shape
    count = len(order)
    block = width // sub
    many = len(weights)
    wide = many * block
    scalars = jnp.stack(list(order) + list(add_order or ())).astype(jnp.int32)

    def kernel(scalars_ref, tokens_ref, *refs):
        out_ref = refs[-1]
        for i in range(many):
            part = jnp.dot(tokens_ref[...], refs[i][...], preferred_element_type=jnp.float32)
            if add is not None:
                part = part + refs[many][:, i * block : (i + 1) * block].astype(jnp.float32)
            out_ref[:, i * block : (i + 1) * block] = part.astype(out_type)

    in_specs = [pl.BlockSpec((rows, depth), lambda s, sc: (0, 0))]
    in_specs += [
        pl.BlockSpec((depth, block), lambda s, sc: (0, sc[s // sub] * sub + s % sub))
        for _ in weights
    ]
    operands = [tokens, *weights]
    if add is not None:
        in_specs.append(
            pl.BlockSpec((rows, wide), lambda s, sc: (0, sc[count + s // sub] * sub + s % sub))
        )
        operands.append(add)
    steps = count * sub
    return pl.pallas_call(
        kernel,
        out_shape=jax.ShapeDtypeStruct((rows, steps * wide), out_type),
        grid_spec=pltpu.PrefetchScalarGridSpec(
            num_scalar_prefetch=1,
            grid=(steps,),
            in_specs=in_specs,
            out_specs=pl.BlockSpec((rows, wide), lambda s, sc: (0, s)),
        ),
        compiler_params=compiler_params(),
        cost_estimate=pl.CostEstimate(
            flops=2 * rows * depth * steps * wide,
            bytes_accessed=2 * depth * steps * wide + 2 * rows * (depth + steps * wide),
            transcendentals=0,
        ),
    )(scalars, *operands)


def contract(parts, weight, sub, order, start=None):
    rows, width = parts[0].shape
    count = len(parts)
    out_width = weight.shape[1]
    block = width // sub
    scalars = jnp.stack(list(order)).astype(jnp.int32)

    def kernel(scalars_ref, weight_ref, *refs):
        out_ref = refs[-1]
        step = pl.program_id(0)

        @pl.when(step == 0)
        def _():
            if start is None:
                out_ref[...] = jnp.zeros_like(out_ref)
            else:
                out_ref[...] = refs[count][...]

        for i in range(count):

            @pl.when(step // sub == i)
            def _():
                out_ref[...] += jnp.dot(
                    refs[i][...], weight_ref[...], preferred_element_type=jnp.float32
                )

    def part_spec(i):
        return pl.BlockSpec((rows, block), lambda s, sc: (0, jnp.clip(s - i * sub, 0, sub - 1)))

    in_specs = [
        pl.BlockSpec((block, out_width), lambda s, sc: (sc[s // sub] * sub + s % sub, 0))
    ]
    in_specs += [part_spec(i) for i in range(count)]
    operands = [weight, *parts]
    if start is not None:
        in_specs.append(pl.BlockSpec((rows, out_width), lambda s, sc: (0, 0)))
        operands.append(start)
    return pl.pallas_call(
        kernel,
        out_shape=jax.ShapeDtypeStruct((rows, out_width), jnp.float32),
        grid_spec=pltpu.PrefetchScalarGridSpec(
            num_scalar_prefetch=1,
            grid=(count * sub,),
            in_specs=in_specs,
            out_specs=pl.BlockSpec((rows, out_width), lambda s, sc: (0, 0)),
        ),
        compiler_params=compiler_params(),
        cost_estimate=pl.CostEstimate(
            flops=2 * rows * width * count * out_width,
            bytes_accessed=2 * width * count * out_width + 8 * rows * out_width,
            transcendentals=0,
        ),
    )(scalars, *operands)


def unit_norm(values, scales):
    row_mean = jnp.mean(values, -1, keepdims=True)
    row_var = jnp.mean(values * values, -1, keepdims=True) - row_mean * row_mean
    return ((values - row_mean) * lax.rsqrt(row_var + EPS) * scales).astype(jnp.bfloat16)


def softmax_blend(query, key, value, keep=None):
    scores = lax.dot_general(
        query, key, (((1,), (1,)), ((), ())), preferred_element_type=jnp.float32
    ) * (1.0 / math.sqrt(HEAD_DIM))
    if keep is not None:
        scores = jnp.where(keep, scores, -jnp.inf)
    weights = jnp.exp(scores - jnp.max(scores, -1, keepdims=True))
    row_sum = jnp.sum(weights, -1, keepdims=True)
    blended = jnp.dot(weights.astype(jnp.bfloat16), value, preferred_element_type=jnp.float32)
    return (blended / row_sum).astype(jnp.bfloat16)


def camera_blend(own, arrived, query_scale, key_scale):
    rows, wide = own.shape
    width = wide // 3
    heads = width // HEAD_DIM

    def kernel(own_ref, arrived_ref, query_scale_ref, key_scale_ref, out_ref):
        row_cam = lax.broadcasted_iota(jnp.int32, (rows, rows), 0) // TOK_CAM
        col_cam = lax.broadcasted_iota(jnp.int32, (rows, rows), 1) // TOK_CAM
        same = row_cam == col_cam
        for h in range(heads):

            def raw(which):
                at = pl.ds(which * width + h * HEAD_DIM, HEAD_DIM)
                return own_ref[:, at] + arrived_ref[:, at].astype(jnp.float32)

            at = pl.ds(h * HEAD_DIM, HEAD_DIM)
            out_ref[:, at] = softmax_blend(
                unit_norm(raw(0), query_scale_ref[:, at]),
                unit_norm(raw(1), key_scale_ref[:, at]),
                raw(2).astype(jnp.bfloat16),
                same,
            )

    return pl.pallas_call(
        kernel,
        out_shape=jax.ShapeDtypeStruct((rows, width), jnp.bfloat16),
        compiler_params=compiler_params(),
        cost_estimate=pl.CostEstimate(
            flops=4 * rows * rows * width,
            bytes_accessed=6 * rows * wide,
            transcendentals=rows * rows * heads,
        ),
    )(own, arrived, query_scale, key_scale)


def head_parts(own, arrived, query_scale, key_scale):
    rows, wide = own.shape
    width = wide // 3
    heads = width // HEAD_DIM

    def kernel(own_ref, arrived_ref, query_scale_ref, key_scale_ref, out_ref):
        for which in range(3):
            for h in range(heads):
                at = pl.ds(which * width + h * HEAD_DIM, HEAD_DIM)
                scale_at = pl.ds(h * HEAD_DIM, HEAD_DIM)
                raw = own_ref[:, at] + arrived_ref[:, at].astype(jnp.float32)
                if which == 0:
                    raw = unit_norm(raw, query_scale_ref[:, scale_at])
                elif which == 1:
                    raw = unit_norm(raw, key_scale_ref[:, scale_at])
                out_ref[:, at] = raw.astype(jnp.bfloat16)

    return pl.pallas_call(
        kernel,
        out_shape=jax.ShapeDtypeStruct((rows, wide), jnp.bfloat16),
        compiler_params=compiler_params(),
        cost_estimate=pl.CostEstimate(
            flops=10 * rows * wide, bytes_accessed=8 * rows * wide, transcendentals=0
        ),
    )(own, arrived, query_scale, key_scale)


def join_blend(parts):
    rows, wide = parts.shape
    heads = wide // 3 // HEAD_DIM

    def kernel(query_ref, key_ref, value_ref, out_ref):
        out_ref[...] = softmax_blend(query_ref[...], key_ref[...], value_ref[...])

    def spec(which):
        return pl.BlockSpec((rows, HEAD_DIM), lambda h: (0, which * heads + h))

    return pl.pallas_call(
        kernel,
        out_shape=jax.ShapeDtypeStruct((rows, wide // 3), jnp.bfloat16),
        grid=(heads,),
        in_specs=[spec(0), spec(1), spec(2)],
        out_specs=pl.BlockSpec((rows, HEAD_DIM), lambda h: (0, h)),
        compiler_params=compiler_params(),
        cost_estimate=pl.CostEstimate(
            flops=4 * rows * rows * heads * HEAD_DIM,
            bytes_accessed=2 * rows * wide,
            transcendentals=rows * rows * heads,
        ),
    )(parts, parts, parts)


def all_moments(values):
    pair = jnp.stack((jnp.sum(values, 1), jnp.sum(values * values, 1)))
    return (pair + flip(pair, 1)) + (flip(pair, 2) + flip(pair, 3))


def gather_rows(own):
    half = own.shape[0] // 2
    before, after = row_shift(own, 1), row_shift(own, -1)
    away = jnp.concatenate((row_shift(before[:half], 1), row_shift(after[half:], -1)))
    return [own, before, after, away]


def scatter_rows(own, before, after, away):
    half = own.shape[0] // 2

    def send(array, shift):
        return row_shift(array.astype(jnp.bfloat16), shift).astype(jnp.float32)

    to_after = send(away[:half], 1)
    to_before = send(away[half:], -1)
    from_before = jnp.concatenate((send(after[:half] + to_after, 1), send(after[half:], 1)))
    from_after = jnp.concatenate((send(before[:half], -1), send(before[half:] + to_before, -1)))
    return own + from_before + from_after


def fast_body(
    camera_tokens,
    norm_gain,
    query_weight,
    key_weight,
    value_weight,
    query_gain,
    key_gain,
    out_weight,
    up_weight,
    up_bias,
    down_weight,
    down_bias,
    join_gain,
    join_query,
    join_key,
    join_value,
    join_query_gain,
    join_key_gain,
    join_out,
):
    own_rows = camera_tokens.shape[0]
    position = lax.axis_index("cols")
    core, side = position & 1, position >> 1
    mine = 2 * core + side
    across = 2 * core + 1 - side
    near = 2 * (1 - core) + side
    far = 2 * (1 - core) + 1 - side
    head_width = query_weight.shape[1] // 4
    unit_width = up_weight.shape[1] // 4

    def quarter(vector):
        width = vector.shape[0] // 4
        return lax.dynamic_slice(vector, (mine * width,), (width,))[None]

    def spread(tokens, weights, width, sub):
        for_core = project(
            tokens, weights, width, sub, (2 * (1 - core), 2 * (1 - core) + 1), jnp.bfloat16
        )
        arrived = core_swap(for_core)
        for_side = project(
            tokens, weights, width, sub, (across,), jnp.bfloat16, arrived, (1 - side,)
        )
        from_side = y_swap(for_side)
        kept = project(tokens, weights, width, sub, (mine,), jnp.float32, arrived, (side,))
        return kept, from_side

    def collect(own):
        own_across = y_swap(own)
        return own, core_swap(own), own_across, core_swap(own_across)

    spans = [(i, TOK_CAM) for i in range(0, own_rows, TOK_CAM)]
    cuts = []
    for at, size in spans[:-1]:
        cuts.append((at, 0, size))
    last = spans[-1][0]
    cuts += [(last, 0, TOK_CAM // 2), (last, TOK_CAM // 2, TOK_CAM // 2)]

    start_f32 = camera_tokens.astype(jnp.float32)
    normed = normalize(start_f32, norm_gain, all_moments(start_f32))
    shards = {at: gather_rows(normed[at : at + size]) for at, size in spans}

    query_scale, key_scale = quarter(query_gain), quarter(key_gain)
    blended_out = {}
    for at, size in spans:
        tokens = jnp.concatenate(shards[at])
        kept, from_side = spread(tokens, (query_weight, key_weight, value_weight), head_width, 1)
        blended = collect(camera_blend(kept, from_side, query_scale, key_scale))
        blended_out[at] = contract(blended, out_weight, 1, (mine, near, across, far))

    bias = quarter(up_bias)
    join_query_scale, join_key_scale = quarter(join_query_gain), quarter(join_key_gain)
    layer_parts, join_parts = [], []
    for at, low, size in cuts:
        tokens = jnp.concatenate([shard[low : low + size] for shard in shards[at]])
        kept, from_side = spread(tokens, (up_weight,), unit_width, 2)
        hidden = jax.nn.gelu(
            kept + from_side.astype(jnp.float32) + bias, approximate=False
        ).astype(jnp.bfloat16)
        own, own_near, own_across, own_far = collect(hidden)
        begun = blended_out[at].reshape(4, -1, blended_out[at].shape[1])
        begun = begun[:, low : low + size].reshape(4 * size, -1)
        mixed = contract((own, own_near), down_weight, 2, (mine, near), begun)
        mixed = contract((own_across, own_far), down_weight, 2, (across, far), mixed)
        summed = scatter_rows(*jnp.split(mixed, 4))
        rows = slice(at + low, at + low + size)
        layer = (start_f32[rows] + summed + down_bias).astype(jnp.bfloat16)
        layer_parts.append(layer)
        layer_f32 = layer.astype(jnp.float32)
        layer_normed = normalize(layer_f32, join_gain, all_moments(layer_f32))
        tokens = jnp.concatenate(gather_rows(layer_normed))
        kept, from_side = spread(tokens, (join_query, join_key, join_value), head_width, 1)
        join_parts.append(head_parts(kept, from_side, join_query_scale, join_key_scale))

    blended = join_blend(jnp.concatenate(join_parts))
    pieces, at = [], 0
    for _, _, size in cuts:
        pieces.append(blended[at : at + 4 * size].reshape(4, size, -1))
        at += 4 * size
    blended = jnp.concatenate(pieces, 1).reshape(4 * own_rows, -1)
    result = contract(collect(blended), join_out, 1, (mine, near, across, far))
    summed = scatter_rows(*jnp.split(result, 4))
    layer_own = jnp.concatenate(layer_parts)
    return (layer_own.astype(jnp.float32) + summed).astype(jnp.bfloat16)


def layer(*arrays):
    own_rows, heads_width = arrays[0].shape[0], arrays[2].shape[1]
    fits = lax.axis_size("cols") == 4 and lax.axis_size("rows") == 4
    fits = fits and own_rows % TOK_CAM == 0 and heads_width % (4 * HEAD_DIM) == 0
    return (fast_body if fits else generic_body)(*arrays)


def solution(mesh):
    in_specs = (
        P(("groups", "rows"), "cols"),
        P("cols"),
        P("cols", "rows"),
        P("cols", "rows"),
        P("cols", "rows"),
        P("rows"),
        P("rows"),
        P("rows", "cols"),
        P("cols", "rows"),
        P("rows"),
        P("rows", "cols"),
        P("cols"),
        P("cols"),
        P("cols", "rows"),
        P("cols", "rows"),
        P("cols", "rows"),
        P("rows"),
        P("rows"),
        P("rows", "cols"),
    )
    out_specs = P(("groups", "rows"), "cols")
    return jax.shard_map(layer, mesh=mesh, in_specs=in_specs, out_specs=out_specs, check_vma=False)
```

```python
import math

import jax
import jax.numpy as jnp
from jax import lax
from jax.experimental import pallas as pl
from jax.experimental.pallas import tpu as pltpu
from jax.sharding import PartitionSpec as P

HEAD_DIM = 128
TOK_CAM = 64
D = 6144


EPS = 1e-06


def partner_2(array, axis, bit):
    return lax.ppermute(array, axis, [(i, i ^ 1 << bit) for i in range(lax.axis_size(axis))])


def normalize(values, scales, moments):
    row_mean = moments[0] / D
    row_var = moments[1] / D - row_mean * row_mean
    return ((values - row_mean[:, None]) * lax.rsqrt(row_var[:, None] + EPS) * scales).astype(
        jnp.bfloat16
    )


def shard_moments(values):
    return lax.psum((jnp.sum(values, 1), jnp.sum(values * values, 1)), "cols")


def head_norm(values, scales):
    row_count = values.shape[0]
    grouped = values.reshape(row_count, -1, HEAD_DIM)
    row_mean = jnp.mean(grouped, -1, keepdims=True)
    row_var = jnp.mean(grouped * grouped, -1, keepdims=True) - row_mean * row_mean
    normed = (grouped - row_mean) * lax.rsqrt(row_var + EPS)
    return (normed.reshape(row_count, -1) * scales).astype(jnp.bfloat16)


def attend(queries, key_rows, val_rows):
    inv_root = 1.0 / math.sqrt(HEAD_DIM)
    scores = (
        jnp.einsum("bqhd,bkhd->bhqk", queries, key_rows, preferred_element_type=jnp.float32)
        * inv_root
    )
    row_max = jnp.max(scores, -1, keepdims=True)
    weights = jnp.exp(scores - row_max)
    row_sum = jnp.sum(weights, -1)
    blended = jnp.einsum(
        "bhqk,bkhd->bqhd",
        weights.astype(jnp.bfloat16),
        val_rows,
        preferred_element_type=jnp.float32,
    )
    return blended / jnp.transpose(row_sum, (0, 2, 1))[..., None]


def to_heads(matrix, blocks):
    return matrix.reshape(blocks, -1, matrix.shape[1] // HEAD_DIM, HEAD_DIM)


def camera_attention(queries, key_rows, val_rows):
    local_rows = queries.shape[0]
    if local_rows >= TOK_CAM:
        blocks = local_rows // TOK_CAM
        result = attend(
            to_heads(queries, blocks), to_heads(key_rows, blocks), to_heads(val_rows, blocks)
        )
    else:
        cam_span = TOK_CAM // local_rows
        position = lax.axis_index("cols")
        key_value = jnp.stack((key_rows, val_rows))
        for which_bit in range(cam_span.bit_length() - 1):
            partner = partner_2(key_value, "cols", which_bit)
            is_lower = position >> which_bit & 1 == 0
            key_value = jnp.where(
                is_lower,
                jnp.concatenate((key_value, partner), 1),
                jnp.concatenate((partner, key_value), 1),
            )
        result = attend(to_heads(queries, 1), to_heads(key_value[0], 1), to_heads(key_value[1], 1))
    return result.reshape(local_rows, -1).astype(jnp.bfloat16)


def generic_body(
    camera_tokens,
    norm_gain,
    query_weight,
    key_weight,
    value_weight,
    query_gain,
    key_gain,
    out_weight,
    up_weight,
    up_bias,
    down_weight,
    down_bias,
    join_gain,
    join_query,
    join_key,
    join_value,
    join_query_gain,
    join_key_gain,
    join_out,
):
    own_rows = camera_tokens.shape[0]
    all_rows = own_rows * lax.axis_size("rows")
    col_rows = all_rows // lax.axis_size("cols")
    attn_width = query_weight.shape[1]
    start_f32 = camera_tokens.astype(jnp.float32)
    normed_all = lax.all_gather(
        normalize(start_f32, norm_gain, shard_moments(start_f32)), "rows", axis=0, tiled=True
    )
    joint_weight = jnp.concatenate((query_weight, key_weight, value_weight, up_weight), 1)
    joint = lax.psum_scatter(
        jnp.dot(normed_all, joint_weight, preferred_element_type=jnp.float32),
        "cols",
        scatter_dimension=0,
        tiled=True,
    )
    up_sum = joint[:, 3 * attn_width :]
    hidden = jax.nn.gelu(up_sum + up_bias, approximate=False).astype(jnp.bfloat16)
    attended = camera_attention(
        head_norm(joint[:, :attn_width], query_gain),
        head_norm(joint[:, attn_width : 2 * attn_width], key_gain),
        joint[:, 2 * attn_width : 3 * attn_width].astype(jnp.bfloat16),
    )
    attn_all, hidden_all = (
        lax.all_gather(attended, "cols", axis=0, tiled=True),
        lax.all_gather(hidden, "cols", axis=0, tiled=True),
    )
    mixed = lax.psum_scatter(
        jnp.dot(attn_all, out_weight, preferred_element_type=jnp.float32)
        + jnp.dot(hidden_all, down_weight, preferred_element_type=jnp.float32),
        "rows",
        scatter_dimension=0,
        tiled=True,
    )
    layer_own = (start_f32 + mixed + down_bias).astype(jnp.bfloat16)
    layer_f32 = layer_own.astype(jnp.float32)
    join_in = lax.all_gather(
        normalize(layer_f32, join_gain, shard_moments(layer_f32)), "rows", axis=0, tiled=True
    )
    join_weight = jnp.concatenate((join_query, join_key, join_value), 1)
    join_joint = lax.psum_scatter(
        jnp.dot(join_in, join_weight, preferred_element_type=jnp.float32),
        "cols",
        scatter_dimension=0,
        tiled=True,
    )
    join_q = head_norm(join_joint[:, :attn_width], join_query_gain)
    join_k = head_norm(join_joint[:, attn_width : 2 * attn_width], join_key_gain)
    join_v = join_joint[:, 2 * attn_width :].astype(jnp.bfloat16)
    heads_here = attn_width // HEAD_DIM
    query_heads = join_q.reshape(col_rows, heads_here, HEAD_DIM)
    inv_root = 1.0 / math.sqrt(HEAD_DIM)
    run_max = jnp.full((heads_here, col_rows), -jnp.inf, jnp.float32)
    run_sum = jnp.zeros((heads_here, col_rows), jnp.float32)
    accum = jnp.zeros((col_rows, heads_here, HEAD_DIM), jnp.float32)
    key_part = lax.all_gather(join_k, "cols", axis=0, tiled=True)
    val_part = lax.all_gather(join_v, "cols", axis=0, tiled=True)
    row_count = key_part.shape[0]
    key_heads = key_part.reshape(row_count, heads_here, HEAD_DIM)
    val_heads = val_part.reshape(row_count, heads_here, HEAD_DIM)
    scores = (
        jnp.einsum("qhd,khd->hqk", query_heads, key_heads, preferred_element_type=jnp.float32)
        * inv_root
    )
    new_max = jnp.max(scores, -1)
    factor = jnp.exp(run_max - new_max)
    weights = jnp.exp(scores - new_max[..., None])
    run_sum = run_sum * factor + jnp.sum(weights, -1)
    accum = accum * jnp.transpose(factor)[..., None] + jnp.einsum(
        "hqk,khd->qhd", weights.astype(jnp.bfloat16), val_heads, preferred_element_type=jnp.float32
    )
    run_max, run_sum, accum = (new_max, run_sum, accum)
    joined_attn = (
        (accum / jnp.transpose(run_sum)[..., None])
        .reshape(col_rows, attn_width)
        .astype(jnp.bfloat16)
    )
    joined_all = lax.all_gather(joined_attn, "cols", axis=0, tiled=True)
    result = lax.psum_scatter(
        jnp.dot(joined_all, join_out, preferred_element_type=jnp.float32),
        "rows",
        scatter_dimension=0,
        tiled=True,
    )
    return (layer_own.astype(jnp.float32) + result).astype(jnp.bfloat16)


VMEM_BYTES = 48 * 1024 * 1024


def flip(array, mask):
    size = lax.axis_size("cols")
    return lax.ppermute(array, "cols", [(i, i ^ mask) for i in range(size)])


def core_swap(array):
    return flip(array, 1)


def y_swap(array):
    return flip(array, 2)


def row_shift(array, shift):
    size = lax.axis_size("rows")
    return lax.ppermute(array, "rows", [(i, (i + shift) % size) for i in range(size)])


class Runner:
    def __init__(self, position):
        self.position = position
        self.last = None

    def __call__(self, kernel, grid, operands, in_specs, out_shape, out_spec, flops, scratch=()):
        in_specs = list(in_specs)
        operands = list(operands)
        count = len(operands)
        if self.last is not None:
            operands.append(self.last)
            in_specs.append(pl.BlockSpec(memory_space=pl.ANY))
        total = len(operands)

        def inner(position_ref, *refs):
            kernel(position_ref, *refs[:count], *refs[total:])

        self.last = pl.pallas_call(
            inner,
            out_shape=out_shape,
            grid_spec=pltpu.PrefetchScalarGridSpec(
                num_scalar_prefetch=1,
                grid=grid,
                in_specs=in_specs,
                out_specs=out_spec,
                scratch_shapes=scratch,
            ),
            compiler_params=pltpu.CompilerParams(vmem_limit_bytes=VMEM_BYTES),
            cost_estimate=pl.CostEstimate(flops=1, bytes_accessed=1, transcendentals=0),
        )(self.position, *operands)
        return self.last


def whole(array):
    return pl.BlockSpec(array.shape, lambda s, pos: (0,) * array.ndim)


def mine_of(pos):
    return 2 * pos[0] + pos[1]


def across_of(pos):
    return 2 * pos[0] + 1 - pos[1]


def dot_f32(a, b):
    return jnp.dot(a, b, preferred_element_type=jnp.float32)


def project_send(run, tokens, weights, width, sub):
    rows, depth = tokens.shape
    block = width // sub
    wide = len(weights) * block

    def kernel(pos, tokens_ref, *refs):
        for i in range(len(weights)):
            refs[-1][:, i * block : (i + 1) * block] = dot_f32(
                tokens_ref[...], refs[i][...]
            ).astype(jnp.bfloat16)

    spec = pl.BlockSpec((depth, block), lambda s, pos: (0, 2 * (1 - pos[0]) * sub + s))
    return run(
        kernel,
        (2 * sub,),
        (tokens, *weights),
        (whole(tokens), *[spec] * len(weights)),
        jax.ShapeDtypeStruct((rows, 2 * sub * wide), jnp.bfloat16),
        pl.BlockSpec((rows, wide), lambda s, pos: (0, s)),
        rows * depth * 2 * sub * wide,
    )


def project_across(run, tokens, weights, width, sub, arrived):
    rows, depth = tokens.shape
    block = width // sub
    wide = len(weights) * block

    def kernel(pos, tokens_ref, *refs):
        for i in range(len(weights)):
            at = slice(i * block, (i + 1) * block)
            part = dot_f32(tokens_ref[...], refs[i][...])
            part = part + refs[-2][:, at].astype(jnp.float32)
            refs[-1][:, at] = part.astype(jnp.bfloat16)

    spec = pl.BlockSpec((depth, block), lambda s, pos: (0, across_of(pos) * sub + s))
    return run(
        kernel,
        (sub,),
        (tokens, *weights, arrived),
        (
            whole(tokens),
            *[spec] * len(weights),
            pl.BlockSpec((rows, wide), lambda s, pos: (0, (1 - pos[1]) * sub + s)),
        ),
        jax.ShapeDtypeStruct((rows, sub * wide), jnp.bfloat16),
        pl.BlockSpec((rows, wide), lambda s, pos: (0, s)),
        rows * depth * sub * wide,
    )


def project_hidden(run, tokens, weight, bias, width, sub, arrived, from_side):
    rows, depth = tokens.shape
    block = width // sub

    def kernel(pos, tokens_ref, weight_ref, bias_ref, arrived_ref, side_ref, out_ref):
        total = dot_f32(tokens_ref[...], weight_ref[...])
        total = total + arrived_ref[...].astype(jnp.float32) + side_ref[...].astype(jnp.float32)
        total = total + bias_ref[...]
        out_ref[...] = (total * (1.0 + lax.erf(total * math.sqrt(0.5))) * 0.5).astype(jnp.bfloat16)

    return run(
        kernel,
        (sub,),
        (tokens, weight, bias, arrived, from_side),
        (
            whole(tokens),
            pl.BlockSpec((depth, block), lambda s, pos: (0, mine_of(pos) * sub + s)),
            pl.BlockSpec((1, block), lambda s, pos: (0, mine_of(pos) * sub + s)),
            pl.BlockSpec((rows, block), lambda s, pos: (0, pos[1] * sub + s)),
            pl.BlockSpec((rows, block), lambda s, pos: (0, s)),
        ),
        jax.ShapeDtypeStruct((rows, width), jnp.bfloat16),
        pl.BlockSpec((rows, block), lambda s, pos: (0, s)),
        rows * depth * width,
    )


def unit_norm(values, scales):
    row_mean = jnp.mean(values, -1, keepdims=True)
    row_var = jnp.mean(values * values, -1, keepdims=True) - row_mean * row_mean
    return ((values - row_mean) * lax.rsqrt(row_var + EPS) * scales).astype(jnp.bfloat16)


def softmax_blend(query, key, value, keep=None):
    scores = lax.dot_general(
        query, key, (((1,), (1,)), ((), ())), preferred_element_type=jnp.float32
    ) * (1.0 / math.sqrt(HEAD_DIM))
    if keep is not None:
        scores = jnp.where(keep, scores, -jnp.inf)
    weights = jnp.exp(scores - jnp.max(scores, -1, keepdims=True))
    row_sum = jnp.sum(weights, -1, keepdims=True)
    blended = dot_f32(weights.astype(jnp.bfloat16), value)
    return (blended / row_sum).astype(jnp.bfloat16)


def project_heads(run, tokens, weights, scales, width, arrived, from_side, attend_camera):
    rows, depth = tokens.shape
    heads = width // HEAD_DIM
    out_width = width if attend_camera else 3 * width

    def kernel(pos, tokens_ref, *refs):
        weight_refs, scale_refs = refs[:3], refs[3:5]
        arrived_ref, side_ref, out_ref = refs[5:]
        raws = []
        for i in range(3):
            at = slice(i * width, (i + 1) * width)
            raw = dot_f32(tokens_ref[...], weight_refs[i][...])
            raw = raw + arrived_ref[:, at].astype(jnp.float32)
            raws.append(raw + side_ref[:, at].astype(jnp.float32))
        if attend_camera:
            row_cam = lax.broadcasted_iota(jnp.int32, (rows, rows), 0) // TOK_CAM
            col_cam = lax.broadcasted_iota(jnp.int32, (rows, rows), 1) // TOK_CAM
            same = row_cam == col_cam
        for h in range(heads):
            at = slice(h * HEAD_DIM, (h + 1) * HEAD_DIM)
            query = unit_norm(raws[0][:, at], scale_refs[0][:, at])
            key = unit_norm(raws[1][:, at], scale_refs[1][:, at])
            value = raws[2][:, at].astype(jnp.bfloat16)
            if attend_camera:
                out_ref[:, at] = softmax_blend(query, key, value, same)
            else:
                out_ref[:, at] = query
                out_ref[:, width + h * HEAD_DIM : width + (h + 1) * HEAD_DIM] = key
                out_ref[:, 2 * width + h * HEAD_DIM : 2 * width + (h + 1) * HEAD_DIM] = value

    weight_spec = pl.BlockSpec((depth, width), lambda s, pos: (0, mine_of(pos)))
    scale_spec = pl.BlockSpec((1, width), lambda s, pos: (0, mine_of(pos)))
    return run(
        kernel,
        (1,),
        (tokens, *weights, *scales, arrived, from_side),
        (
            whole(tokens),
            *[weight_spec] * 3,
            *[scale_spec] * 2,
            pl.BlockSpec((rows, 3 * width), lambda s, pos: (0, pos[1])),
            whole(from_side),
        ),
        jax.ShapeDtypeStruct((rows, out_width), jnp.bfloat16),
        pl.BlockSpec((rows, out_width), lambda s, pos: (0, 0)),
        3 * rows * depth * width,
    )


def contract(run, parts, weight, sub, first=0, start=None):
    rows, width = parts[0].shape
    count = len(parts)
    out_width = weight.shape[1]
    block = width // sub

    def kernel(pos, weight_ref, *refs):
        out_ref = refs[-1]
        step = pl.program_id(0)
        for i in range(count):

            @pl.when(step // sub == i)
            def _(i=i):
                term = dot_f32(refs[i][...], weight_ref[...])
                if i > 0:
                    out_ref[...] += term
                elif sub == 1:
                    out_ref[...] = term if start is None else term + refs[count][...]
                else:

                    @pl.when(step == 0)
                    def _():
                        out_ref[...] = term if start is None else term + refs[count][...]

                    @pl.when(step > 0)
                    def _():
                        out_ref[...] += term

    def weight_block(s, pos):
        i = s // sub + first
        return (2 * (pos[0] ^ (i & 1)) + (pos[1] ^ (i >> 1))) * sub + s % sub, 0

    def part_spec(i):
        return pl.BlockSpec((rows, block), lambda s, pos: (0, jnp.clip(s - i * sub, 0, sub - 1)))

    operands = [weight, *parts]
    in_specs = [pl.BlockSpec((block, out_width), weight_block)]
    in_specs += [part_spec(i) for i in range(count)]
    if start is not None:
        operands.append(start)
        in_specs.append(whole(start))
    return run(
        kernel,
        (count * sub,),
        operands,
        in_specs,
        jax.ShapeDtypeStruct((rows, out_width), jnp.float32),
        pl.BlockSpec((rows, out_width), lambda s, pos: (0, 0)),
        rows * width * count * out_width,
    )


def join_blend(run, parts):
    rows = sum(part.shape[0] for part in parts)
    heads = parts[0].shape[1] // 3 // HEAD_DIM
    count = len(parts)

    def kernel(pos, *refs):
        query, key, value = (
            jnp.concatenate([ref[...] for ref in refs[i * count : (i + 1) * count]])
            for i in range(3)
        )
        refs[-1][...] = softmax_blend(query, key, value)

    def specs(which):
        return [
            pl.BlockSpec((part.shape[0], HEAD_DIM), lambda h, pos: (0, which * heads + h))
            for part in parts
        ]

    return run(
        kernel,
        (heads,),
        (*parts, *parts, *parts),
        (*specs(0), *specs(1), *specs(2)),
        jax.ShapeDtypeStruct((rows, heads * HEAD_DIM), jnp.bfloat16),
        pl.BlockSpec((rows, HEAD_DIM), lambda h, pos: (0, h)),
        2 * rows * rows * heads * HEAD_DIM,
    )


def all_moments(values):
    pair = jnp.stack((jnp.sum(values, 1), jnp.sum(values * values, 1)))
    return (pair + flip(pair, 1)) + (flip(pair, 2) + flip(pair, 3))


def gather_rows(own):
    return jnp.concatenate((own, row_shift(own, 1), row_shift(own, -1), row_shift(own, 2)))


def scatter_rows(terms):
    own, before, after, away = jnp.split(terms, 4)

    def send(array, shift):
        return row_shift(array.astype(jnp.bfloat16), shift).astype(jnp.float32)

    return own + send(after, 1) + send(before, -1) + send(away, 2)


def scatter_rows_long(terms):
    own, before, after, away = jnp.split(terms, 4)
    half = own.shape[0] // 2

    def send(array, shift):
        return row_shift(array.astype(jnp.bfloat16), shift).astype(jnp.float32)

    to_after = send(away[:half], 1)
    to_before = send(away[half:], -1)
    from_before = jnp.concatenate((send(after[:half] + to_after, 1), send(after[half:], 1)))
    from_after = jnp.concatenate((send(before[:half], -1), send(before[half:] + to_before, -1)))
    return own + from_before + from_after


def fast_body(
    camera_tokens,
    norm_gain,
    query_weight,
    key_weight,
    value_weight,
    query_gain,
    key_gain,
    out_weight,
    up_weight,
    up_bias,
    down_weight,
    down_bias,
    join_gain,
    join_query,
    join_key,
    join_value,
    join_query_gain,
    join_key_gain,
    join_out,
):
    own_rows = camera_tokens.shape[0]
    index = lax.axis_index("cols")
    run = Runner(jnp.stack((index & 1, index >> 1)).astype(jnp.int32))
    head_width = query_weight.shape[1] // 4
    unit_width = up_weight.shape[1] // 4
    sub = 3 if unit_width % (3 * 256) == 0 else 1
    heads_in = (query_weight, key_weight, value_weight)
    join_in = (join_query, join_key, join_value)
    scales = (query_gain[None], key_gain[None])
    join_scales = (join_query_gain[None], join_key_gain[None])
    bias = up_bias[None]
    spans = range(0, own_rows, TOK_CAM)
    last = len(spans) - 1

    start_f32 = camera_tokens.astype(jnp.float32)
    normed = normalize(start_f32, norm_gain, all_moments(start_f32))
    tokens = [gather_rows(normed[at : at + TOK_CAM]) for at in spans]

    def collect(own):
        own_across = y_swap(own)
        return own, core_swap(own), own_across, core_swap(own_across)

    def heads_begin(i):
        sent = core_swap(project_send(run, tokens[i], heads_in, head_width, 1))
        heads_arrived.append(sent)

    def units_begin(i):
        sent = core_swap(project_send(run, tokens[i], (up_weight,), unit_width, sub))
        units_arrived.append(sent)

    def heads_cross(i):
        heads_side.append(
            y_swap(project_across(run, tokens[i], heads_in, head_width, 1, heads_arrived[i]))
        )

    def units_cross(i):
        units_side.append(
            y_swap(
                project_across(run, tokens[i], (up_weight,), unit_width, sub, units_arrived[i])
            )
        )

    def heads_end(i):
        own = project_heads(
            run, tokens[i], heads_in, scales, head_width, heads_arrived[i], heads_side[i], True
        )
        blended.append(collect(own))

    def units_end(i):
        own = project_hidden(
            run, tokens[i], up_weight, bias, unit_width, sub, units_arrived[i], units_side[i]
        )
        hidden.append(collect(own))

    def out_terms(i):
        return contract(run, blended[i], out_weight, 1)

    def camera_end(i, mixed):
        summed = scatter_rows(mixed)
        rows = slice(spans[i], spans[i] + TOK_CAM)
        layer = (start_f32[rows] + summed + down_bias).astype(jnp.bfloat16)
        layers.append(layer)
        layer_f32 = layer.astype(jnp.float32)
        join_tokens.append(gather_rows(normalize(layer_f32, join_gain, all_moments(layer_f32))))

    def join_begin(i):
        arrived = core_swap(project_send(run, join_tokens[i], join_in, head_width, 1))
        side = y_swap(project_across(run, join_tokens[i], join_in, head_width, 1, arrived))
        join_sums.append((arrived, side))

    def join_end(i):
        join_parts.append(
            project_heads(
                run, join_tokens[i], join_in, join_scales, head_width, *join_sums[i], False
            )
        )

    heads_arrived, units_arrived, heads_side, units_side = [], [], [], []
    blended, hidden, layers, join_tokens, join_sums, join_parts = [], [], [], [], [], []
    for i in range(len(spans)):
        heads_begin(i)
        units_begin(i)
        heads_cross(i)
        if i > 0:
            heads_end(i - 1)
        units_cross(i)
        if i > 0:
            units_end(i - 1)
    heads_end(last)
    for i in range(last):
        mixed = contract(run, hidden[i], down_weight, 2, 0, out_terms(i))
        if i == last - 1:
            units_end(last)
        camera_end(i, mixed)
    if last == 0:
        units_end(last)
    mixed = contract(run, hidden[last][:2], down_weight, 2, 0, out_terms(last))
    mixed = contract(run, hidden[last][2:], down_weight, 2, 2, mixed)
    camera_end(last, mixed)
    for i in range(len(spans)):
        join_begin(i)
        if i > 0:
            join_end(i - 1)
    join_end(last)

    joined = join_blend(run, join_parts)
    joined = joined.reshape(len(spans), 4, TOK_CAM, head_width).swapaxes(0, 1)
    joined = joined.reshape(4 * own_rows, head_width)
    summed = scatter_rows_long(contract(run, collect(joined), join_out, 1))
    layer_own = jnp.concatenate(layers)
    return (layer_own.astype(jnp.float32) + summed).astype(jnp.bfloat16)


def layer(*arrays):
    own_rows, heads_width = arrays[0].shape[0], arrays[2].shape[1]
    fits = lax.axis_size("cols") == 4 and lax.axis_size("rows") == 4
    fits = fits and own_rows % TOK_CAM == 0 and heads_width % (4 * HEAD_DIM) == 0
    return (fast_body if fits else generic_body)(*arrays)


def solution(mesh):
    in_specs = (
        P(("groups", "rows"), "cols"),
        P("cols"),
        P("cols", "rows"),
        P("cols", "rows"),
        P("cols", "rows"),
        P("rows"),
        P("rows"),
        P("rows", "cols"),
        P("cols", "rows"),
        P("rows"),
        P("rows", "cols"),
        P("cols"),
        P("cols"),
        P("cols", "rows"),
        P("cols", "rows"),
        P("cols", "rows"),
        P("rows"),
        P("rows"),
        P("rows", "cols"),
    )
    out_specs = P(("groups", "rows"), "cols")
    return jax.shard_map(layer, mesh=mesh, in_specs=in_specs, out_specs=out_specs, check_vma=False)
```

```python
import math

import jax
import jax.numpy as jnp
from jax import lax
from jax.experimental import pallas as pl
from jax.experimental.pallas import tpu as pltpu
from jax.sharding import PartitionSpec as P

HEAD_DIM = 128
TOK_CAM = 64
D = 6144


EPS = 1e-06


def partner_2(array, axis, bit):
    return lax.ppermute(array, axis, [(i, i ^ 1 << bit) for i in range(lax.axis_size(axis))])


def normalize(values, scales, moments):
    row_mean = moments[0] / D
    row_var = moments[1] / D - row_mean * row_mean
    return ((values - row_mean[:, None]) * lax.rsqrt(row_var[:, None] + EPS) * scales).astype(
        jnp.bfloat16
    )


def shard_moments(values):
    return lax.psum((jnp.sum(values, 1), jnp.sum(values * values, 1)), "cols")


def head_norm(values, scales):
    row_count = values.shape[0]
    grouped = values.reshape(row_count, -1, HEAD_DIM)
    row_mean = jnp.mean(grouped, -1, keepdims=True)
    row_var = jnp.mean(grouped * grouped, -1, keepdims=True) - row_mean * row_mean
    normed = (grouped - row_mean) * lax.rsqrt(row_var + EPS)
    return (normed.reshape(row_count, -1) * scales).astype(jnp.bfloat16)


def attend(queries, key_rows, val_rows):
    inv_root = 1.0 / math.sqrt(HEAD_DIM)
    scores = (
        jnp.einsum("bqhd,bkhd->bhqk", queries, key_rows, preferred_element_type=jnp.float32)
        * inv_root
    )
    row_max = jnp.max(scores, -1, keepdims=True)
    weights = jnp.exp(scores - row_max)
    row_sum = jnp.sum(weights, -1)
    blended = jnp.einsum(
        "bhqk,bkhd->bqhd",
        weights.astype(jnp.bfloat16),
        val_rows,
        preferred_element_type=jnp.float32,
    )
    return blended / jnp.transpose(row_sum, (0, 2, 1))[..., None]


def to_heads(matrix, blocks):
    return matrix.reshape(blocks, -1, matrix.shape[1] // HEAD_DIM, HEAD_DIM)


def camera_attention(queries, key_rows, val_rows):
    local_rows = queries.shape[0]
    if local_rows >= TOK_CAM:
        blocks = local_rows // TOK_CAM
        result = attend(
            to_heads(queries, blocks), to_heads(key_rows, blocks), to_heads(val_rows, blocks)
        )
    else:
        cam_span = TOK_CAM // local_rows
        position = lax.axis_index("cols")
        key_value = jnp.stack((key_rows, val_rows))
        for which_bit in range(cam_span.bit_length() - 1):
            partner = partner_2(key_value, "cols", which_bit)
            is_lower = position >> which_bit & 1 == 0
            key_value = jnp.where(
                is_lower,
                jnp.concatenate((key_value, partner), 1),
                jnp.concatenate((partner, key_value), 1),
            )
        result = attend(to_heads(queries, 1), to_heads(key_value[0], 1), to_heads(key_value[1], 1))
    return result.reshape(local_rows, -1).astype(jnp.bfloat16)


def generic_body(
    camera_tokens,
    norm_gain,
    query_weight,
    key_weight,
    value_weight,
    query_gain,
    key_gain,
    out_weight,
    up_weight,
    up_bias,
    down_weight,
    down_bias,
    join_gain,
    join_query,
    join_key,
    join_value,
    join_query_gain,
    join_key_gain,
    join_out,
):
    own_rows = camera_tokens.shape[0]
    all_rows = own_rows * lax.axis_size("rows")
    col_rows = all_rows // lax.axis_size("cols")
    attn_width = query_weight.shape[1]
    start_f32 = camera_tokens.astype(jnp.float32)
    normed_all = lax.all_gather(
        normalize(start_f32, norm_gain, shard_moments(start_f32)), "rows", axis=0, tiled=True
    )
    joint_weight = jnp.concatenate((query_weight, key_weight, value_weight, up_weight), 1)
    joint = lax.psum_scatter(
        jnp.dot(normed_all, joint_weight, preferred_element_type=jnp.float32),
        "cols",
        scatter_dimension=0,
        tiled=True,
    )
    up_sum = joint[:, 3 * attn_width :]
    hidden = jax.nn.gelu(up_sum + up_bias, approximate=False).astype(jnp.bfloat16)
    attended = camera_attention(
        head_norm(joint[:, :attn_width], query_gain),
        head_norm(joint[:, attn_width : 2 * attn_width], key_gain),
        joint[:, 2 * attn_width : 3 * attn_width].astype(jnp.bfloat16),
    )
    attn_all, hidden_all = (
        lax.all_gather(attended, "cols", axis=0, tiled=True),
        lax.all_gather(hidden, "cols", axis=0, tiled=True),
    )
    mixed = lax.psum_scatter(
        jnp.dot(attn_all, out_weight, preferred_element_type=jnp.float32)
        + jnp.dot(hidden_all, down_weight, preferred_element_type=jnp.float32),
        "rows",
        scatter_dimension=0,
        tiled=True,
    )
    layer_own = (start_f32 + mixed + down_bias).astype(jnp.bfloat16)
    layer_f32 = layer_own.astype(jnp.float32)
    join_in = lax.all_gather(
        normalize(layer_f32, join_gain, shard_moments(layer_f32)), "rows", axis=0, tiled=True
    )
    join_weight = jnp.concatenate((join_query, join_key, join_value), 1)
    join_joint = lax.psum_scatter(
        jnp.dot(join_in, join_weight, preferred_element_type=jnp.float32),
        "cols",
        scatter_dimension=0,
        tiled=True,
    )
    join_q = head_norm(join_joint[:, :attn_width], join_query_gain)
    join_k = head_norm(join_joint[:, attn_width : 2 * attn_width], join_key_gain)
    join_v = join_joint[:, 2 * attn_width :].astype(jnp.bfloat16)
    heads_here = attn_width // HEAD_DIM
    query_heads = join_q.reshape(col_rows, heads_here, HEAD_DIM)
    inv_root = 1.0 / math.sqrt(HEAD_DIM)
    run_max = jnp.full((heads_here, col_rows), -jnp.inf, jnp.float32)
    run_sum = jnp.zeros((heads_here, col_rows), jnp.float32)
    accum = jnp.zeros((col_rows, heads_here, HEAD_DIM), jnp.float32)
    key_part = lax.all_gather(join_k, "cols", axis=0, tiled=True)
    val_part = lax.all_gather(join_v, "cols", axis=0, tiled=True)
    row_count = key_part.shape[0]
    key_heads = key_part.reshape(row_count, heads_here, HEAD_DIM)
    val_heads = val_part.reshape(row_count, heads_here, HEAD_DIM)
    scores = (
        jnp.einsum("qhd,khd->hqk", query_heads, key_heads, preferred_element_type=jnp.float32)
        * inv_root
    )
    new_max = jnp.max(scores, -1)
    factor = jnp.exp(run_max - new_max)
    weights = jnp.exp(scores - new_max[..., None])
    run_sum = run_sum * factor + jnp.sum(weights, -1)
    accum = accum * jnp.transpose(factor)[..., None] + jnp.einsum(
        "hqk,khd->qhd", weights.astype(jnp.bfloat16), val_heads, preferred_element_type=jnp.float32
    )
    run_max, run_sum, accum = (new_max, run_sum, accum)
    joined_attn = (
        (accum / jnp.transpose(run_sum)[..., None])
        .reshape(col_rows, attn_width)
        .astype(jnp.bfloat16)
    )
    joined_all = lax.all_gather(joined_attn, "cols", axis=0, tiled=True)
    result = lax.psum_scatter(
        jnp.dot(joined_all, join_out, preferred_element_type=jnp.float32),
        "rows",
        scatter_dimension=0,
        tiled=True,
    )
    return (layer_own.astype(jnp.float32) + result).astype(jnp.bfloat16)


VMEM_BYTES = 48 * 1024 * 1024


def flip(array, mask):
    size = lax.axis_size("cols")
    return lax.ppermute(array, "cols", [(i, i ^ mask) for i in range(size)])


def core_swap(array):
    return flip(array, 1)


def y_swap(array):
    return flip(array, 2)


def row_shift(array, shift):
    size = lax.axis_size("rows")
    return lax.ppermute(array, "rows", [(i, (i + shift) % size) for i in range(size)])


class Runner:
    def __init__(self, position):
        self.position = position

    def __call__(self, kernel, grid, operands, in_specs, out_shape, out_spec):
        return pl.pallas_call(
            kernel,
            out_shape=out_shape,
            grid_spec=pltpu.PrefetchScalarGridSpec(
                num_scalar_prefetch=1, grid=grid, in_specs=list(in_specs), out_specs=out_spec
            ),
            compiler_params=pltpu.CompilerParams(vmem_limit_bytes=VMEM_BYTES),
            cost_estimate=pl.CostEstimate(flops=1, bytes_accessed=1, transcendentals=0),
        )(self.position, *operands)


def joined_rows(refs, at=slice(None)):
    return jnp.concatenate([ref[:, at] for ref in refs])


def store_rows(refs, at, values):
    piece = values.shape[0] // len(refs)
    for j, ref in enumerate(refs):
        ref[:, at] = values[j * piece : (j + 1) * piece].astype(ref.dtype)


def whole(array):
    return pl.BlockSpec(array.shape, lambda s, pos: (0,) * array.ndim)


def mine_of(pos):
    return 2 * pos[0] + pos[1]


def across_of(pos):
    return 2 * pos[0] + 1 - pos[1]


def dot_f32(a, b):
    return jnp.dot(a, b, preferred_element_type=jnp.float32)


def project_send(run, tokens, weights, width, sub):
    rows, depth = tokens.shape
    block = width // sub
    wide = len(weights) * block

    def kernel(pos, tokens_ref, *refs):
        for i in range(len(weights)):
            refs[-1][:, i * block : (i + 1) * block] = dot_f32(
                tokens_ref[...], refs[i][...]
            ).astype(jnp.bfloat16)

    spec = pl.BlockSpec((depth, block), lambda s, pos: (0, 2 * (1 - pos[0]) * sub + s))
    return run(
        kernel,
        (2 * sub,),
        (tokens, *weights),
        (whole(tokens), *[spec] * len(weights)),
        jax.ShapeDtypeStruct((rows, 2 * sub * wide), jnp.bfloat16),
        pl.BlockSpec((rows, wide), lambda s, pos: (0, s)),
    )


def project_across(run, tokens, weights, width, sub, arrived, pieces=1):
    rows, depth = tokens.shape
    block = width // sub
    wide = len(weights) * block

    def kernel(pos, tokens_ref, *refs):
        for i in range(len(weights)):
            at = slice(i * block, (i + 1) * block)
            part = dot_f32(tokens_ref[...], refs[i][...])
            part = part + refs[len(weights)][:, at].astype(jnp.float32)
            store_rows(refs[len(weights) + 1 :], at, part)

    spec = pl.BlockSpec((depth, block), lambda s, pos: (0, across_of(pos) * sub + s))
    return run(
        kernel,
        (sub,),
        (tokens, *weights, arrived),
        (
            whole(tokens),
            *[spec] * len(weights),
            pl.BlockSpec((rows, wide), lambda s, pos: (0, (1 - pos[1]) * sub + s)),
        ),
        (jax.ShapeDtypeStruct((rows // pieces, sub * wide), jnp.bfloat16),) * pieces,
        (pl.BlockSpec((rows // pieces, wide), lambda s, pos: (0, s)),) * pieces,
    )


def project_hidden(run, tokens, weight, bias, width, sub, arrived, from_side, pieces=1):
    rows, depth = tokens.shape
    block = width // sub
    sides = len(from_side)

    def kernel(pos, tokens_ref, weight_ref, bias_ref, arrived_ref, *refs):
        total = dot_f32(tokens_ref[...], weight_ref[...])
        total = total + arrived_ref[...].astype(jnp.float32)
        total = total + joined_rows(refs[:sides]).astype(jnp.float32)
        total = total + bias_ref[...]
        unit = total * (1.0 + lax.erf(total * math.sqrt(0.5))) * 0.5
        store_rows(refs[sides:], slice(None), unit)

    return run(
        kernel,
        (sub,),
        (tokens, weight, bias, arrived, *from_side),
        (
            whole(tokens),
            pl.BlockSpec((depth, block), lambda s, pos: (0, mine_of(pos) * sub + s)),
            pl.BlockSpec((1, block), lambda s, pos: (0, mine_of(pos) * sub + s)),
            pl.BlockSpec((rows, block), lambda s, pos: (0, pos[1] * sub + s)),
            *[pl.BlockSpec((rows // sides, block), lambda s, pos: (0, s))] * sides,
        ),
        (jax.ShapeDtypeStruct((rows // pieces, width), jnp.bfloat16),) * pieces,
        (pl.BlockSpec((rows // pieces, block), lambda s, pos: (0, s)),) * pieces,
    )


def unit_norm(values, scales):
    row_mean = jnp.mean(values, -1, keepdims=True)
    row_var = jnp.mean(values * values, -1, keepdims=True) - row_mean * row_mean
    return ((values - row_mean) * lax.rsqrt(row_var + EPS) * scales).astype(jnp.bfloat16)


def softmax_blend(query, key, value, keep=None):
    scores = lax.dot_general(
        query, key, (((1,), (1,)), ((), ())), preferred_element_type=jnp.float32
    ) * (1.0 / math.sqrt(HEAD_DIM))
    if keep is not None:
        scores = jnp.where(keep, scores, -jnp.inf)
    weights = jnp.exp(scores - jnp.max(scores, -1, keepdims=True))
    row_sum = jnp.sum(weights, -1, keepdims=True)
    blended = dot_f32(weights.astype(jnp.bfloat16), value)
    return (blended / row_sum).astype(jnp.bfloat16)


def project_heads(run, tokens, weights, scales, width, arrived, from_side, attend_camera):
    rows, depth = tokens.shape
    heads = width // HEAD_DIM
    out_width = width if attend_camera else 3 * width

    def kernel(pos, tokens_ref, *refs):
        weight_refs, scale_refs = refs[:3], refs[3:5]
        arrived_ref, side_ref, out_ref = refs[5:]
        raws = []
        for i in range(3):
            at = slice(i * width, (i + 1) * width)
            raw = dot_f32(tokens_ref[...], weight_refs[i][...])
            raw = raw + arrived_ref[:, at].astype(jnp.float32)
            raws.append(raw + side_ref[:, at].astype(jnp.float32))
        if attend_camera:
            row_cam = lax.broadcasted_iota(jnp.int32, (rows, rows), 0) // TOK_CAM
            col_cam = lax.broadcasted_iota(jnp.int32, (rows, rows), 1) // TOK_CAM
            same = row_cam == col_cam
        for h in range(heads):
            at = slice(h * HEAD_DIM, (h + 1) * HEAD_DIM)
            query = unit_norm(raws[0][:, at], scale_refs[0][:, at])
            key = unit_norm(raws[1][:, at], scale_refs[1][:, at])
            value = raws[2][:, at].astype(jnp.bfloat16)
            if attend_camera:
                out_ref[:, at] = softmax_blend(query, key, value, same)
            else:
                out_ref[:, at] = query
                out_ref[:, width + h * HEAD_DIM : width + (h + 1) * HEAD_DIM] = key
                out_ref[:, 2 * width + h * HEAD_DIM : 2 * width + (h + 1) * HEAD_DIM] = value

    weight_spec = pl.BlockSpec((depth, width), lambda s, pos: (0, mine_of(pos)))
    scale_spec = pl.BlockSpec((1, width), lambda s, pos: (0, mine_of(pos)))
    return run(
        kernel,
        (1,),
        (tokens, *weights, *scales, arrived, from_side),
        (
            whole(tokens),
            *[weight_spec] * 3,
            *[scale_spec] * 2,
            pl.BlockSpec((rows, 3 * width), lambda s, pos: (0, pos[1])),
            whole(from_side),
        ),
        jax.ShapeDtypeStruct((rows, out_width), jnp.bfloat16),
        pl.BlockSpec((rows, out_width), lambda s, pos: (0, 0)),
    )


def contract(run, parts, weight, sub, first=0, start=None):
    rows = sum(piece.shape[0] for piece in parts[0])
    width = parts[0][0].shape[1]
    count, pieces = len(parts), len(parts[0])
    out_width = weight.shape[1]
    block = width // sub

    def kernel(pos, weight_ref, *refs):
        out_ref = refs[-1]
        step = pl.program_id(0)
        for i in range(count):

            @pl.when(step // sub == i)
            def _(i=i):
                part = joined_rows(refs[i * pieces : (i + 1) * pieces])
                term = dot_f32(part, weight_ref[...])
                if i > 0:
                    out_ref[...] += term
                elif sub == 1:
                    out_ref[...] = term if start is None else term + refs[-2][...]
                else:

                    @pl.when(step == 0)
                    def _():
                        out_ref[...] = term if start is None else term + refs[-2][...]

                    @pl.when(step > 0)
                    def _():
                        out_ref[...] += term

    def weight_block(s, pos):
        i = s // sub + first
        return (2 * (pos[0] ^ (i & 1)) + (pos[1] ^ (i >> 1))) * sub + s % sub, 0

    def part_spec(i):
        return pl.BlockSpec(
            (rows // pieces, block), lambda s, pos: (0, jnp.clip(s - i * sub, 0, sub - 1))
        )

    operands = [weight, *[piece for part in parts for piece in part]]
    in_specs = [pl.BlockSpec((block, out_width), weight_block)]
    in_specs += [part_spec(i) for i in range(count) for _ in range(pieces)]
    if start is not None:
        operands.append(start)
        in_specs.append(whole(start))
    return run(
        kernel,
        (count * sub,),
        operands,
        in_specs,
        jax.ShapeDtypeStruct((rows, out_width), jnp.float32),
        pl.BlockSpec((rows, out_width), lambda s, pos: (0, 0)),
    )


def join_blend(run, parts):
    rows = sum(part.shape[0] for part in parts)
    heads = parts[0].shape[1] // 3 // HEAD_DIM
    count = len(parts)

    def kernel(pos, *refs):
        query, key, value = (
            jnp.concatenate([ref[...] for ref in refs[i * count : (i + 1) * count]])
            for i in range(3)
        )
        refs[-1][...] = softmax_blend(query, key, value)

    def specs(which):
        return [
            pl.BlockSpec((part.shape[0], HEAD_DIM), lambda h, pos: (0, which * heads + h))
            for part in parts
        ]

    return run(
        kernel,
        (heads,),
        (*parts, *parts, *parts),
        (*specs(0), *specs(1), *specs(2)),
        jax.ShapeDtypeStruct((rows, heads * HEAD_DIM), jnp.bfloat16),
        pl.BlockSpec((rows, HEAD_DIM), lambda h, pos: (0, h)),
    )


def moment_pair(values):
    return jnp.stack((jnp.sum(values, 1), jnp.sum(values * values, 1)))


def moment_flips(pair):
    return pair, flip(pair, 1), flip(pair, 2), flip(pair, 3)


def moment_sum(pairs):
    return (pairs[0] + pairs[1]) + (pairs[2] + pairs[3])


def sent(array, shift):
    return row_shift(array.astype(jnp.bfloat16), shift)


def sync(*values):
    return lax.optimization_barrier(values)


def scatter_rows_long(terms):
    own, before, after, away = jnp.split(terms, 4)
    half = own.shape[0] // 2

    def send(array, shift):
        return row_shift(array.astype(jnp.bfloat16), shift).astype(jnp.float32)

    to_after = send(away[:half], 1)
    to_before = send(away[half:], -1)
    from_before = jnp.concatenate((send(after[:half] + to_after, 1), send(after[half:], 1)))
    from_after = jnp.concatenate((send(before[:half], -1), send(before[half:] + to_before, -1)))
    return own + from_before + from_after


def fast_body(
    camera_tokens,
    norm_gain,
    query_weight,
    key_weight,
    value_weight,
    query_gain,
    key_gain,
    out_weight,
    up_weight,
    up_bias,
    down_weight,
    down_bias,
    join_gain,
    join_query,
    join_key,
    join_value,
    join_query_gain,
    join_key_gain,
    join_out,
):
    half = TOK_CAM
    index = lax.axis_index("cols")
    run = Runner(jnp.stack((index & 1, index >> 1)).astype(jnp.int32))
    head_width = query_weight.shape[1] // 4
    unit_width = up_weight.shape[1] // 4
    sub = 3 if unit_width % (3 * 256) == 0 else 1
    heads_in = (query_weight, key_weight, value_weight)
    join_in = (join_query, join_key, join_value)
    scales = (query_gain[None], key_gain[None])
    join_scales = (join_query_gain[None], join_key_gain[None])
    bias = up_bias[None]

    def heads_send(tokens, weights):
        return project_send(run, tokens, weights, head_width, 1)

    def heads_across(tokens, weights, arrived):
        return project_across(run, tokens, weights, head_width, 1, arrived)[0]

    def units_send(tokens):
        return project_send(run, tokens, (up_weight,), unit_width, sub)

    def units_across(tokens, arrived, pieces):
        return project_across(run, tokens, (up_weight,), unit_width, sub, arrived, pieces)

    def units_end(tokens, arrived, side, pieces):
        return project_hidden(
            run, tokens, up_weight, bias, unit_width, sub, arrived, side, pieces
        )

    def layer_end(start, own, *arrived):
        total = own
        for term in arrived:
            total = total + term.astype(jnp.float32)
        return (start + total + down_bias).astype(jnp.bfloat16)

    start_f32 = camera_tokens.astype(jnp.float32)
    pairs = sync(*moment_flips(moment_pair(start_f32)))
    normed = normalize(start_f32, norm_gain, moment_sum(pairs))
    own_a, own_b = normed[:half], normed[half:]
    gathered = sync(own_b, own_a, sent(own_a, 1), sent(own_a, -1), sent(own_a, 2))
    own_b, tok_a = gathered[0], jnp.concatenate(gathered[1:])

    b_before = sent(own_b, 1)
    qs_a = heads_send(tok_a, heads_in)
    tok_a, own_b, b_before, qs_a = sync(tok_a, own_b, b_before, qs_a)

    b_after, qc_a = sent(own_b, -1), core_swap(qs_a)
    us_a = units_send(tok_a)
    tok_a, own_b, b_after, qc_a, us_a = sync(tok_a, own_b, b_after, qc_a, us_a)

    uc_a = core_swap(us_a)
    qx_a = heads_across(tok_a, heads_in, qc_a)
    tok_a, own_b, qc_a, uc_a, qx_a = sync(tok_a, own_b, qc_a, uc_a, qx_a)

    qy_a, b_away = y_swap(qx_a), sent(own_b, 2)
    (ux_a,) = units_across(tok_a, uc_a, 1)
    tok_a, qc_a, uc_a, ux_a, qy_a, own_b, b_before, b_after, b_away = sync(
        tok_a, qc_a, uc_a, ux_a, qy_a, own_b, b_before, b_after, b_away
    )

    uy_a = y_swap(ux_a)
    tok_b = jnp.concatenate((own_b, b_before, b_after, b_away))
    qs_b = heads_send(tok_b, heads_in)
    us_b = units_send(tok_b)
    at_a = project_heads(run, tok_a, heads_in, scales, head_width, qc_a, qy_a, True)
    tok_a, tok_b, qs_b, us_b, at_a, uc_a, uy_a = sync(
        tok_a, tok_b, qs_b, us_b, at_a, uc_a, uy_a
    )

    at_ya, at_ca, qc_b, uc_b = y_swap(at_a), core_swap(at_a), core_swap(qs_b), core_swap(us_b)
    (hd_a,) = units_end(tok_a, uc_a, (uy_a,), 1)
    tok_b, at_a, at_ya, at_ca, qc_b, uc_b, hd_a = sync(
        tok_b, at_a, at_ya, at_ca, qc_b, uc_b, hd_a
    )

    hd_ya, hd_ca, at_fa = y_swap(hd_a), core_swap(hd_a), core_swap(at_ya)
    qx_b = heads_across(tok_b, heads_in, qc_b)
    ux_b = units_across(tok_b, uc_b, 2)
    tok_b, at_a, at_ya, at_ca, at_fa, hd_a, hd_ya, hd_ca, qc_b, uc_b, qx_b, *ux_b = sync(
        tok_b, at_a, at_ya, at_ca, at_fa, hd_a, hd_ya, hd_ca, qc_b, uc_b, qx_b, *ux_b
    )

    qy_b, hd_fa = y_swap(qx_b), core_swap(hd_ya)
    mixed_a = contract(run, ((at_a,), (at_ca,), (at_ya,), (at_fa,)), out_weight, 1)
    mixed_a = contract(run, ((hd_a,), (hd_ca,)), down_weight, 2, 0, mixed_a)
    tok_b, hd_ya, hd_fa, mixed_a, qc_b, qy_b, uc_b, ux_b0, ux_b1 = sync(
        tok_b, hd_ya, hd_fa, mixed_a, qc_b, qy_b, uc_b, *ux_b
    )

    uy_b0 = y_swap(ux_b0)
    mixed_a = contract(run, ((hd_ya,), (hd_fa,)), down_weight, 2, 2, mixed_a)
    tok_b, mixed_a, qc_b, qy_b, uc_b, uy_b0, ux_b1 = sync(
        tok_b, mixed_a, qc_b, qy_b, uc_b, uy_b0, ux_b1
    )

    uy_b1 = y_swap(ux_b1)
    mine_a, before_a, after_a, away_a = jnp.split(mixed_a, 4)
    from_before, from_after = sent(after_a, 1), sent(before_a, -1)
    at_b = project_heads(run, tok_b, heads_in, scales, head_width, qc_b, qy_b, True)
    tok_b, uc_b, uy_b0, uy_b1, at_b, mine_a, away_a, from_before, from_after = sync(
        tok_b, uc_b, uy_b0, uy_b1, at_b, mine_a, away_a.astype(jnp.bfloat16), from_before, from_after
    )

    at_yb, at_cb, from_away = y_swap(at_b), core_swap(at_b), sent(away_a, 2)
    hd_b = units_end(tok_b, uc_b, (uy_b0, uy_b1), 2)
    at_b, at_yb, at_cb, hd_b0, hd_b1, mine_a, from_before, from_after, from_away = sync(
        at_b, at_yb, at_cb, *hd_b, mine_a, from_before, from_after, from_away
    )

    hd_yb0, at_fb = y_swap(hd_b0), core_swap(at_yb)
    layer_a = layer_end(start_f32[:half], mine_a, from_before, from_after, from_away)
    pairs = moment_flips(moment_pair(layer_a.astype(jnp.float32)))
    at_b, at_yb, at_cb, at_fb, hd_b0, hd_b1, hd_yb0, layer_a, *pairs = sync(
        at_b, at_yb, at_cb, at_fb, hd_b0, hd_b1, hd_yb0, layer_a, *pairs
    )

    hd_yb1, hd_cb0, hd_cb1 = y_swap(hd_b1), core_swap(hd_b0), core_swap(hd_b1)
    join_a = normalize(layer_a.astype(jnp.float32), join_gain, moment_sum(pairs))
    ja_before, ja_after = sent(join_a, 1), sent(join_a, -1)
    mixed_b = contract(run, ((at_b,), (at_cb,), (at_yb,), (at_fb,)), out_weight, 1)
    hd_b0, hd_b1, hd_cb0, hd_cb1, hd_yb0, hd_yb1, mixed_b, join_a, ja_before, ja_after = sync(
        hd_b0, hd_b1, hd_cb0, hd_cb1, hd_yb0, hd_yb1, mixed_b, join_a, ja_before, ja_after
    )

    hd_fb0, hd_fb1, ja_away = core_swap(hd_yb0), core_swap(hd_yb1), sent(join_a, 2)
    mixed_b = contract(run, ((hd_b0, hd_b1), (hd_cb0, hd_cb1)), down_weight, 2, 0, mixed_b)
    hd_yb0, hd_yb1, hd_fb0, hd_fb1, mixed_b, join_a, ja_before, ja_after, ja_away = sync(
        hd_yb0, hd_yb1, hd_fb0, hd_fb1, mixed_b, join_a, ja_before, ja_after, ja_away
    )

    mixed_b = contract(run, ((hd_yb0, hd_yb1), (hd_fb0, hd_fb1)), down_weight, 2, 2, mixed_b)
    mixed_b, join_a, ja_before, ja_after, ja_away = sync(
        mixed_b, join_a, ja_before, ja_after, ja_away
    )

    mine_b, before_b, after_b, away_b = jnp.split(mixed_b, 4)
    from_before, from_after = sent(after_b, 1), sent(before_b, -1)
    tok_ja = jnp.concatenate((join_a, ja_before, ja_after, ja_away))
    js_a = heads_send(tok_ja, join_in)
    tok_ja, js_a, mine_b, away_b, from_before, from_after = sync(
        tok_ja, js_a, mine_b, away_b.astype(jnp.bfloat16), from_before, from_after
    )

    from_away, jc_a = sent(away_b, 2), core_swap(js_a)
    tok_ja, jc_a, mine_b, from_before, from_after, from_away = sync(
        tok_ja, jc_a, mine_b, from_before, from_after, from_away
    )

    layer_b = layer_end(start_f32[half:], mine_b, from_before, from_after, from_away)
    pairs = moment_flips(moment_pair(layer_b.astype(jnp.float32)))
    jx_a = heads_across(tok_ja, join_in, jc_a)
    tok_ja, jc_a, jx_a, layer_b, *pairs = sync(tok_ja, jc_a, jx_a, layer_b, *pairs)

    join_b = normalize(layer_b.astype(jnp.float32), join_gain, moment_sum(pairs))
    jb_before, jb_after, jb_away = sent(join_b, 1), sent(join_b, -1), sent(join_b, 2)
    jy_a = y_swap(jx_a)
    tok_ja, jc_a, jy_a, join_b, jb_before, jb_after, jb_away = sync(
        tok_ja, jc_a, jy_a, join_b, jb_before, jb_after, jb_away
    )

    tok_jb = jnp.concatenate((join_b, jb_before, jb_after, jb_away))
    js_b = heads_send(tok_jb, join_in)
    tok_ja, jc_a, jy_a, tok_jb, js_b = sync(tok_ja, jc_a, jy_a, tok_jb, js_b)

    jc_b = core_swap(js_b)
    parts_a = project_heads(run, tok_ja, join_in, join_scales, head_width, jc_a, jy_a, False)
    tok_jb, jc_b, parts_a = sync(tok_jb, jc_b, parts_a)

    jy_b = y_swap(heads_across(tok_jb, join_in, jc_b))
    parts_b = project_heads(run, tok_jb, join_in, join_scales, head_width, jc_b, jy_b, False)

    joined = join_blend(run, (parts_a, parts_b))
    joined = joined.reshape(2, 4, half, head_width).swapaxes(0, 1).reshape(8 * half, head_width)
    jo_y, jo_c = y_swap(joined), core_swap(joined)
    jo_f = core_swap(jo_y)
    result = contract(run, ((joined,), (jo_c,), (jo_y,), (jo_f,)), join_out, 1)
    summed = scatter_rows_long(result)
    layer_own = jnp.concatenate((layer_a, layer_b))
    return (layer_own.astype(jnp.float32) + summed).astype(jnp.bfloat16)


def layer(*arrays):
    own_rows, heads_width = arrays[0].shape[0], arrays[2].shape[1]
    fits = lax.axis_size("cols") == 4 and lax.axis_size("rows") == 4
    fits = fits and own_rows == 2 * TOK_CAM and heads_width % (4 * HEAD_DIM) == 0
    return (fast_body if fits else generic_body)(*arrays)


def solution(mesh):
    in_specs = (
        P(("groups", "rows"), "cols"),
        P("cols"),
        P("cols", "rows"),
        P("cols", "rows"),
        P("cols", "rows"),
        P("rows"),
        P("rows"),
        P("rows", "cols"),
        P("cols", "rows"),
        P("rows"),
        P("rows", "cols"),
        P("cols"),
        P("cols"),
        P("cols", "rows"),
        P("cols", "rows"),
        P("cols", "rows"),
        P("rows"),
        P("rows"),
        P("rows", "cols"),
    )
    out_specs = P(("groups", "rows"), "cols")
    return jax.shard_map(layer, mesh=mesh, in_specs=in_specs, out_specs=out_specs, check_vma=False)
```

```python
import math

import jax
import jax.numpy as jnp
from jax import lax
from jax.experimental import pallas as pl
from jax.experimental.pallas import tpu as pltpu
from jax.sharding import PartitionSpec as P

HEAD_DIM = 128
TOK_CAM = 64
D = 6144


EPS = 1e-06


def partner_2(array, axis, bit):
    return lax.ppermute(array, axis, [(i, i ^ 1 << bit) for i in range(lax.axis_size(axis))])


def normalize(values, scales, moments):
    row_mean = moments[0] / D
    row_var = moments[1] / D - row_mean * row_mean
    return ((values - row_mean[:, None]) * lax.rsqrt(row_var[:, None] + EPS) * scales).astype(
        jnp.bfloat16
    )


def shard_moments(values):
    return lax.psum((jnp.sum(values, 1), jnp.sum(values * values, 1)), "cols")


def head_norm(values, scales):
    row_count = values.shape[0]
    grouped = values.reshape(row_count, -1, HEAD_DIM)
    row_mean = jnp.mean(grouped, -1, keepdims=True)
    row_var = jnp.mean(grouped * grouped, -1, keepdims=True) - row_mean * row_mean
    normed = (grouped - row_mean) * lax.rsqrt(row_var + EPS)
    return (normed.reshape(row_count, -1) * scales).astype(jnp.bfloat16)


def attend(queries, key_rows, val_rows):
    inv_root = 1.0 / math.sqrt(HEAD_DIM)
    scores = (
        jnp.einsum("bqhd,bkhd->bhqk", queries, key_rows, preferred_element_type=jnp.float32)
        * inv_root
    )
    row_max = jnp.max(scores, -1, keepdims=True)
    weights = jnp.exp(scores - row_max)
    row_sum = jnp.sum(weights, -1)
    blended = jnp.einsum(
        "bhqk,bkhd->bqhd",
        weights.astype(jnp.bfloat16),
        val_rows,
        preferred_element_type=jnp.float32,
    )
    return blended / jnp.transpose(row_sum, (0, 2, 1))[..., None]


def to_heads(matrix, blocks):
    return matrix.reshape(blocks, -1, matrix.shape[1] // HEAD_DIM, HEAD_DIM)


def camera_attention(queries, key_rows, val_rows):
    local_rows = queries.shape[0]
    if local_rows >= TOK_CAM:
        blocks = local_rows // TOK_CAM
        result = attend(
            to_heads(queries, blocks), to_heads(key_rows, blocks), to_heads(val_rows, blocks)
        )
    else:
        cam_span = TOK_CAM // local_rows
        position = lax.axis_index("cols")
        key_value = jnp.stack((key_rows, val_rows))
        for which_bit in range(cam_span.bit_length() - 1):
            partner = partner_2(key_value, "cols", which_bit)
            is_lower = position >> which_bit & 1 == 0
            key_value = jnp.where(
                is_lower,
                jnp.concatenate((key_value, partner), 1),
                jnp.concatenate((partner, key_value), 1),
            )
        result = attend(to_heads(queries, 1), to_heads(key_value[0], 1), to_heads(key_value[1], 1))
    return result.reshape(local_rows, -1).astype(jnp.bfloat16)


def generic_body(
    camera_tokens,
    norm_gain,
    query_weight,
    key_weight,
    value_weight,
    query_gain,
    key_gain,
    out_weight,
    up_weight,
    up_bias,
    down_weight,
    down_bias,
    join_gain,
    join_query,
    join_key,
    join_value,
    join_query_gain,
    join_key_gain,
    join_out,
):
    own_rows = camera_tokens.shape[0]
    all_rows = own_rows * lax.axis_size("rows")
    col_rows = all_rows // lax.axis_size("cols")
    attn_width = query_weight.shape[1]
    start_f32 = camera_tokens.astype(jnp.float32)
    normed_all = lax.all_gather(
        normalize(start_f32, norm_gain, shard_moments(start_f32)), "rows", axis=0, tiled=True
    )
    joint_weight = jnp.concatenate((query_weight, key_weight, value_weight, up_weight), 1)
    joint = lax.psum_scatter(
        jnp.dot(normed_all, joint_weight, preferred_element_type=jnp.float32),
        "cols",
        scatter_dimension=0,
        tiled=True,
    )
    up_sum = joint[:, 3 * attn_width :]
    hidden = jax.nn.gelu(up_sum + up_bias, approximate=False).astype(jnp.bfloat16)
    attended = camera_attention(
        head_norm(joint[:, :attn_width], query_gain),
        head_norm(joint[:, attn_width : 2 * attn_width], key_gain),
        joint[:, 2 * attn_width : 3 * attn_width].astype(jnp.bfloat16),
    )
    attn_all, hidden_all = (
        lax.all_gather(attended, "cols", axis=0, tiled=True),
        lax.all_gather(hidden, "cols", axis=0, tiled=True),
    )
    mixed = lax.psum_scatter(
        jnp.dot(attn_all, out_weight, preferred_element_type=jnp.float32)
        + jnp.dot(hidden_all, down_weight, preferred_element_type=jnp.float32),
        "rows",
        scatter_dimension=0,
        tiled=True,
    )
    layer_own = (start_f32 + mixed + down_bias).astype(jnp.bfloat16)
    layer_f32 = layer_own.astype(jnp.float32)
    join_in = lax.all_gather(
        normalize(layer_f32, join_gain, shard_moments(layer_f32)), "rows", axis=0, tiled=True
    )
    join_weight = jnp.concatenate((join_query, join_key, join_value), 1)
    join_joint = lax.psum_scatter(
        jnp.dot(join_in, join_weight, preferred_element_type=jnp.float32),
        "cols",
        scatter_dimension=0,
        tiled=True,
    )
    join_q = head_norm(join_joint[:, :attn_width], join_query_gain)
    join_k = head_norm(join_joint[:, attn_width : 2 * attn_width], join_key_gain)
    join_v = join_joint[:, 2 * attn_width :].astype(jnp.bfloat16)
    heads_here = attn_width // HEAD_DIM
    query_heads = join_q.reshape(col_rows, heads_here, HEAD_DIM)
    inv_root = 1.0 / math.sqrt(HEAD_DIM)
    run_max = jnp.full((heads_here, col_rows), -jnp.inf, jnp.float32)
    run_sum = jnp.zeros((heads_here, col_rows), jnp.float32)
    accum = jnp.zeros((col_rows, heads_here, HEAD_DIM), jnp.float32)
    key_part = lax.all_gather(join_k, "cols", axis=0, tiled=True)
    val_part = lax.all_gather(join_v, "cols", axis=0, tiled=True)
    row_count = key_part.shape[0]
    key_heads = key_part.reshape(row_count, heads_here, HEAD_DIM)
    val_heads = val_part.reshape(row_count, heads_here, HEAD_DIM)
    scores = (
        jnp.einsum("qhd,khd->hqk", query_heads, key_heads, preferred_element_type=jnp.float32)
        * inv_root
    )
    new_max = jnp.max(scores, -1)
    factor = jnp.exp(run_max - new_max)
    weights = jnp.exp(scores - new_max[..., None])
    run_sum = run_sum * factor + jnp.sum(weights, -1)
    accum = accum * jnp.transpose(factor)[..., None] + jnp.einsum(
        "hqk,khd->qhd", weights.astype(jnp.bfloat16), val_heads, preferred_element_type=jnp.float32
    )
    run_max, run_sum, accum = (new_max, run_sum, accum)
    joined_attn = (
        (accum / jnp.transpose(run_sum)[..., None])
        .reshape(col_rows, attn_width)
        .astype(jnp.bfloat16)
    )
    joined_all = lax.all_gather(joined_attn, "cols", axis=0, tiled=True)
    result = lax.psum_scatter(
        jnp.dot(joined_all, join_out, preferred_element_type=jnp.float32),
        "rows",
        scatter_dimension=0,
        tiled=True,
    )
    return (layer_own.astype(jnp.float32) + result).astype(jnp.bfloat16)


VMEM_BYTES = 48 * 1024 * 1024


def flip(array, mask):
    size = lax.axis_size("cols")
    return lax.ppermute(array, "cols", [(i, i ^ mask) for i in range(size)])


def core_swap(array):
    return flip(array, 1)


def y_swap(array):
    return flip(array, 2)


def row_shift(array, shift):
    size = lax.axis_size("rows")
    return lax.ppermute(array, "rows", [(i, (i + shift) % size) for i in range(size)])


class Runner:
    def __init__(self, position):
        self.position = position

    def __call__(self, kernel, grid, operands, in_specs, out_shape, out_spec):
        return pl.pallas_call(
            kernel,
            out_shape=out_shape,
            grid_spec=pltpu.PrefetchScalarGridSpec(
                num_scalar_prefetch=1, grid=grid, in_specs=list(in_specs), out_specs=out_spec
            ),
            compiler_params=pltpu.CompilerParams(vmem_limit_bytes=VMEM_BYTES),
            cost_estimate=pl.CostEstimate(flops=1, bytes_accessed=1, transcendentals=0),
        )(self.position, *operands)


def joined_rows(refs, at=slice(None)):
    return jnp.concatenate([ref[:, at] for ref in refs])


def store_rows(refs, at, values):
    piece = values.shape[0] // len(refs)
    for j, ref in enumerate(refs):
        ref[:, at] = values[j * piece : (j + 1) * piece].astype(ref.dtype)


def whole(array):
    return pl.BlockSpec(array.shape, lambda s, pos: (0,) * array.ndim)


def mine_of(pos):
    return 2 * pos[0] + pos[1]


def across_of(pos):
    return 2 * pos[0] + 1 - pos[1]


def dot_f32(a, b):
    return jnp.dot(a, b, preferred_element_type=jnp.float32)


def project_send(run, tokens, weights, width, sub):
    rows, depth = tokens.shape
    block = width // sub
    wide = len(weights) * block

    def kernel(pos, tokens_ref, *refs):
        for i in range(len(weights)):
            refs[-1][:, i * block : (i + 1) * block] = dot_f32(
                tokens_ref[...], refs[i][...]
            ).astype(jnp.bfloat16)

    spec = pl.BlockSpec((depth, block), lambda s, pos: (0, 2 * (1 - pos[0]) * sub + s))
    return run(
        kernel,
        (2 * sub,),
        (tokens, *weights),
        (whole(tokens), *[spec] * len(weights)),
        jax.ShapeDtypeStruct((rows, 2 * sub * wide), jnp.bfloat16),
        pl.BlockSpec((rows, wide), lambda s, pos: (0, s)),
    )


def project_across(run, tokens, weights, width, sub, arrived, pieces=1):
    rows, depth = tokens.shape
    block = width // sub
    wide = len(weights) * block

    def kernel(pos, tokens_ref, *refs):
        for i in range(len(weights)):
            at = slice(i * block, (i + 1) * block)
            part = dot_f32(tokens_ref[...], refs[i][...])
            part = part + refs[len(weights)][:, at].astype(jnp.float32)
            store_rows(refs[len(weights) + 1 :], at, part)

    spec = pl.BlockSpec((depth, block), lambda s, pos: (0, across_of(pos) * sub + s))
    return run(
        kernel,
        (sub,),
        (tokens, *weights, arrived),
        (
            whole(tokens),
            *[spec] * len(weights),
            pl.BlockSpec((rows, wide), lambda s, pos: (0, (1 - pos[1]) * sub + s)),
        ),
        (jax.ShapeDtypeStruct((rows // pieces, sub * wide), jnp.bfloat16),) * pieces,
        (pl.BlockSpec((rows // pieces, wide), lambda s, pos: (0, s)),) * pieces,
    )


def project_hidden(run, tokens, weight, bias, width, sub, arrived, from_side, pieces=1):
    rows, depth = tokens.shape
    block = width // sub
    sides = len(from_side)

    def kernel(pos, tokens_ref, weight_ref, bias_ref, arrived_ref, *refs):
        total = dot_f32(tokens_ref[...], weight_ref[...])
        total = total + arrived_ref[...].astype(jnp.float32)
        total = total + joined_rows(refs[:sides]).astype(jnp.float32)
        total = total + bias_ref[...]
        unit = total * (1.0 + lax.erf(total * math.sqrt(0.5))) * 0.5
        store_rows(refs[sides:], slice(None), unit)

    return run(
        kernel,
        (sub,),
        (tokens, weight, bias, arrived, *from_side),
        (
            whole(tokens),
            pl.BlockSpec((depth, block), lambda s, pos: (0, mine_of(pos) * sub + s)),
            pl.BlockSpec((1, block), lambda s, pos: (0, mine_of(pos) * sub + s)),
            pl.BlockSpec((rows, block), lambda s, pos: (0, pos[1] * sub + s)),
            *[pl.BlockSpec((rows // sides, block), lambda s, pos: (0, s))] * sides,
        ),
        (jax.ShapeDtypeStruct((rows // pieces, width), jnp.bfloat16),) * pieces,
        (pl.BlockSpec((rows // pieces, block), lambda s, pos: (0, s)),) * pieces,
    )


def unit_norm(values, scales):
    row_mean = jnp.mean(values, -1, keepdims=True)
    row_var = jnp.mean(values * values, -1, keepdims=True) - row_mean * row_mean
    return ((values - row_mean) * lax.rsqrt(row_var + EPS) * scales).astype(jnp.bfloat16)


def softmax_blend(query, key, value, keep=None):
    scores = lax.dot_general(
        query, key, (((1,), (1,)), ((), ())), preferred_element_type=jnp.float32
    ) * (1.0 / math.sqrt(HEAD_DIM))
    if keep is not None:
        scores = jnp.where(keep, scores, -jnp.inf)
    weights = jnp.exp(scores - jnp.max(scores, -1, keepdims=True))
    row_sum = jnp.sum(weights, -1, keepdims=True)
    blended = dot_f32(weights.astype(jnp.bfloat16), value)
    return (blended / row_sum).astype(jnp.bfloat16)


def project_heads(run, tokens, weights, scales, width, arrived, from_side, attend_camera):
    rows, depth = tokens.shape
    heads = width // HEAD_DIM
    out_width = width if attend_camera else 3 * width

    def kernel(pos, tokens_ref, *refs):
        weight_refs, scale_refs = refs[:3], refs[3:5]
        arrived_ref, *side_refs, out_ref = refs[5:]
        raws = []
        for i in range(3):
            at = slice(i * width, (i + 1) * width)
            raw = dot_f32(tokens_ref[...], weight_refs[i][...])
            raw = raw + arrived_ref[:, at].astype(jnp.float32)
            raws.append(raw + joined_rows(side_refs, at).astype(jnp.float32))
        if attend_camera:
            row_cam = lax.broadcasted_iota(jnp.int32, (rows, rows), 0) // TOK_CAM
            col_cam = lax.broadcasted_iota(jnp.int32, (rows, rows), 1) // TOK_CAM
            same = row_cam == col_cam
        for h in range(heads):
            at = slice(h * HEAD_DIM, (h + 1) * HEAD_DIM)
            query = unit_norm(raws[0][:, at], scale_refs[0][:, at])
            key = unit_norm(raws[1][:, at], scale_refs[1][:, at])
            value = raws[2][:, at].astype(jnp.bfloat16)
            if attend_camera:
                out_ref[:, at] = softmax_blend(query, key, value, same)
            else:
                out_ref[:, at] = query
                out_ref[:, width + h * HEAD_DIM : width + (h + 1) * HEAD_DIM] = key
                out_ref[:, 2 * width + h * HEAD_DIM : 2 * width + (h + 1) * HEAD_DIM] = value

    weight_spec = pl.BlockSpec((depth, width), lambda s, pos: (0, mine_of(pos)))
    scale_spec = pl.BlockSpec((1, width), lambda s, pos: (0, mine_of(pos)))
    return run(
        kernel,
        (1,),
        (tokens, *weights, *scales, arrived, *from_side),
        (
            whole(tokens),
            *[weight_spec] * 3,
            *[scale_spec] * 2,
            pl.BlockSpec((rows, 3 * width), lambda s, pos: (0, pos[1])),
            *[whole(piece) for piece in from_side],
        ),
        jax.ShapeDtypeStruct((rows, out_width), jnp.bfloat16),
        pl.BlockSpec((rows, out_width), lambda s, pos: (0, 0)),
    )


def contract(run, parts, weight, sub, first=0, start=None):
    rows = sum(piece.shape[0] for piece in parts[0])
    width = parts[0][0].shape[1]
    count, pieces = len(parts), len(parts[0])
    out_width = weight.shape[1]
    block = width // sub

    def kernel(pos, weight_ref, *refs):
        out_ref = refs[-1]
        step = pl.program_id(0)
        for i in range(count):

            @pl.when(step // sub == i)
            def _(i=i):
                part = joined_rows(refs[i * pieces : (i + 1) * pieces])
                term = dot_f32(part, weight_ref[...])
                if i > 0:
                    out_ref[...] += term
                elif sub == 1:
                    out_ref[...] = term if start is None else term + refs[-2][...]
                else:

                    @pl.when(step == 0)
                    def _():
                        out_ref[...] = term if start is None else term + refs[-2][...]

                    @pl.when(step > 0)
                    def _():
                        out_ref[...] += term

    def weight_block(s, pos):
        i = s // sub + first
        return (2 * (pos[0] ^ (i & 1)) + (pos[1] ^ (i >> 1))) * sub + s % sub, 0

    def part_spec(i):
        return pl.BlockSpec(
            (rows // pieces, block), lambda s, pos: (0, jnp.clip(s - i * sub, 0, sub - 1))
        )

    operands = [weight, *[piece for part in parts for piece in part]]
    in_specs = [pl.BlockSpec((block, out_width), weight_block)]
    in_specs += [part_spec(i) for i in range(count) for _ in range(pieces)]
    if start is not None:
        operands.append(start)
        in_specs.append(whole(start))
    return run(
        kernel,
        (count * sub,),
        operands,
        in_specs,
        jax.ShapeDtypeStruct((rows, out_width), jnp.float32),
        pl.BlockSpec((rows, out_width), lambda s, pos: (0, 0)),
    )


def join_blend(run, parts):
    rows = sum(part.shape[0] for part in parts)
    heads = parts[0].shape[1] // 3 // HEAD_DIM
    count = len(parts)

    def kernel(pos, *refs):
        query, key, value = (
            jnp.concatenate([ref[...] for ref in refs[i * count : (i + 1) * count]])
            for i in range(3)
        )
        refs[-1][...] = softmax_blend(query, key, value)

    def specs(which):
        return [
            pl.BlockSpec((part.shape[0], HEAD_DIM), lambda h, pos: (0, which * heads + h))
            for part in parts
        ]

    return run(
        kernel,
        (heads,),
        (*parts, *parts, *parts),
        (*specs(0), *specs(1), *specs(2)),
        jax.ShapeDtypeStruct((rows, heads * HEAD_DIM), jnp.bfloat16),
        pl.BlockSpec((rows, HEAD_DIM), lambda h, pos: (0, h)),
    )


def moment_pair(values):
    return jnp.stack((jnp.sum(values, 1), jnp.sum(values * values, 1)))


def moment_flips(pair):
    return pair, flip(pair, 1), flip(pair, 2), flip(pair, 3)


def moment_sum(pairs):
    return (pairs[0] + pairs[1]) + (pairs[2] + pairs[3])


def sent(array, shift):
    return row_shift(array.astype(jnp.bfloat16), shift)


def moment_shards(total):
    return total, row_shift(total, 1), row_shift(total, -1), row_shift(total, 2)


def normed_shards(shards, scales, totals):
    return jnp.concatenate(
        [normalize(x.astype(jnp.float32), scales, m) for x, m in zip(shards, totals)]
    )


def sync(*values):
    return lax.optimization_barrier(values)


def scatter_rows_long(terms):
    own, before, after, away = jnp.split(terms, 4)
    half = own.shape[0] // 2

    def send(array, shift):
        return row_shift(array.astype(jnp.bfloat16), shift).astype(jnp.float32)

    to_after = send(away[:half], 1)
    to_before = send(away[half:], -1)
    from_before = jnp.concatenate((send(after[:half] + to_after, 1), send(after[half:], 1)))
    from_after = jnp.concatenate((send(before[:half], -1), send(before[half:] + to_before, -1)))
    return own + from_before + from_after


def fast_body(
    camera_tokens,
    norm_gain,
    query_weight,
    key_weight,
    value_weight,
    query_gain,
    key_gain,
    out_weight,
    up_weight,
    up_bias,
    down_weight,
    down_bias,
    join_gain,
    join_query,
    join_key,
    join_value,
    join_query_gain,
    join_key_gain,
    join_out,
):
    half = TOK_CAM
    index = lax.axis_index("cols")
    run = Runner(jnp.stack((index & 1, index >> 1)).astype(jnp.int32))
    head_width = query_weight.shape[1] // 4
    unit_width = up_weight.shape[1] // 4
    sub = 3 if unit_width % (3 * 256) == 0 else 1
    heads_in = (query_weight, key_weight, value_weight)
    join_in = (join_query, join_key, join_value)
    scales = (query_gain[None], key_gain[None])
    join_scales = (join_query_gain[None], join_key_gain[None])
    bias = up_bias[None]

    def heads_send(tokens, weights):
        return project_send(run, tokens, weights, head_width, 1)

    def heads_across(tokens, weights, arrived, pieces=1):
        return project_across(run, tokens, weights, head_width, 1, arrived, pieces)

    def heads_out(parts, first=0, start=None):
        return contract(run, [(part,) for part in parts], out_weight, 1, first, start)

    def units_down(parts, first, start):
        return contract(run, parts, down_weight, 2, first, start)

    def units_send(tokens):
        return project_send(run, tokens, (up_weight,), unit_width, sub)

    def units_across(tokens, arrived, pieces):
        return project_across(run, tokens, (up_weight,), unit_width, sub, arrived, pieces)

    def units_end(tokens, arrived, side, pieces):
        return project_hidden(
            run, tokens, up_weight, bias, unit_width, sub, arrived, side, pieces
        )

    def layer_end(start, own, *arrived):
        total = own
        for term in arrived:
            total = total + term.astype(jnp.float32)
        return (start + total + down_bias).astype(jnp.bfloat16)

    start_f32 = camera_tokens.astype(jnp.float32)
    own_a, own_b = camera_tokens[:half], camera_tokens[half:]
    pairs = moment_flips(moment_pair(start_f32))
    own_a, own_b, a_before, a_after, *pairs = sync(
        own_a, own_b, sent(own_a, 1), sent(own_a, -1), *pairs
    )

    totals = moment_shards(moment_sum(pairs))
    own_a, own_b, a_before, a_after, a_away, *totals = sync(
        own_a, own_b, a_before, a_after, sent(own_a, 2), *totals
    )
    totals_a = [total[:, :half] for total in totals]
    totals_b = [total[:, half:] for total in totals]

    b_before = sent(own_b, 1)
    tok_a = normed_shards((own_a, a_before, a_after, a_away), norm_gain, totals_a)
    qs_a = heads_send(tok_a, heads_in)
    tok_a, own_b, b_before, qs_a = sync(tok_a, own_b, b_before, qs_a)

    b_after, qc_a = sent(own_b, -1), core_swap(qs_a)
    us_a = units_send(tok_a)
    tok_a, own_b, b_after, qc_a, us_a = sync(tok_a, own_b, b_after, qc_a, us_a)

    uc_a = core_swap(us_a)
    (qx_a,) = heads_across(tok_a, heads_in, qc_a)
    tok_a, own_b, qc_a, uc_a, qx_a = sync(tok_a, own_b, qc_a, uc_a, qx_a)

    qy_a, b_away = y_swap(qx_a), sent(own_b, 2)
    (ux_a,) = units_across(tok_a, uc_a, 1)
    tok_a, qc_a, uc_a, ux_a, qy_a, own_b, b_before, b_after, b_away = sync(
        tok_a, qc_a, uc_a, ux_a, qy_a, own_b, b_before, b_after, b_away
    )

    uy_a = y_swap(ux_a)
    tok_b = normed_shards((own_b, b_before, b_after, b_away), norm_gain, totals_b)
    qs_b = heads_send(tok_b, heads_in)
    us_b = units_send(tok_b)
    at_a = project_heads(run, tok_a, heads_in, scales, head_width, qc_a, (qy_a,), True)
    tok_a, tok_b, qs_b, us_b, at_a, uc_a, uy_a = sync(
        tok_a, tok_b, qs_b, us_b, at_a, uc_a, uy_a
    )

    at_ya, at_ca, qc_b, uc_b = y_swap(at_a), core_swap(at_a), core_swap(qs_b), core_swap(us_b)
    (hd_a,) = units_end(tok_a, uc_a, (uy_a,), 1)
    tok_b, at_a, at_ya, at_ca, qc_b, uc_b, hd_a = sync(
        tok_b, at_a, at_ya, at_ca, qc_b, uc_b, hd_a
    )

    hd_ya, hd_ca, at_fa = y_swap(hd_a), core_swap(hd_a), core_swap(at_ya)
    (qx_b,) = heads_across(tok_b, heads_in, qc_b)
    ux_b = units_across(tok_b, uc_b, 2)
    mixed_a = units_down(((hd_a,),), 0, heads_out((at_a, at_ca, at_ya)))
    tok_b, at_fa, hd_ya, hd_ca, qc_b, uc_b, qx_b, mixed_a, *ux_b = sync(
        tok_b, at_fa, hd_ya, hd_ca, qc_b, uc_b, qx_b, mixed_a, *ux_b
    )

    qy_b, hd_fa = y_swap(qx_b), core_swap(hd_ya)
    mixed_a = units_down(((hd_ca,),), 1, heads_out((at_fa,), 3, mixed_a))
    mixed_a = units_down(((hd_ya,), (hd_fa,)), 2, mixed_a)
    tok_b, mixed_a, qc_b, qy_b, uc_b, ux_b0, ux_b1 = sync(
        tok_b, mixed_a, qc_b, qy_b, uc_b, *ux_b
    )

    uy_b0 = y_swap(ux_b0)
    mine_a, before_a, after_a, away_a = jnp.split(mixed_a, 4)
    from_before, from_after = sent(after_a, 1), sent(before_a, -1)
    at_b = project_heads(run, tok_b, heads_in, scales, head_width, qc_b, (qy_b,), True)
    at_yb = y_swap(at_b)
    tok_b, uc_b, uy_b0, ux_b1, at_b, at_yb, mine_a, away_a, from_before, from_after = sync(
        tok_b, uc_b, uy_b0, ux_b1, at_b, at_yb, mine_a, away_a.astype(jnp.bfloat16),
        from_before, from_after,
    )

    uy_b1, from_away, at_cb, at_fb = (
        y_swap(ux_b1), sent(away_a, 2), core_swap(at_b), core_swap(at_yb)
    )
    tok_b, uc_b, uy_b0, uy_b1, at_b, at_cb, at_yb, at_fb, mine_a, *arrived = sync(
        tok_b, uc_b, uy_b0, uy_b1, at_b, at_cb, at_yb, at_fb, mine_a,
        from_before, from_after, from_away,
    )

    layer_a = layer_end(start_f32[:half], mine_a, *arrived)
    pairs = moment_flips(moment_pair(layer_a.astype(jnp.float32)))
    hd_b = units_end(tok_b, uc_b, (uy_b0, uy_b1), 2)
    at_b, at_cb, at_yb, at_fb, hd_b0, hd_b1, layer_a, *pairs = sync(
        at_b, at_cb, at_yb, at_fb, *hd_b, layer_a, *pairs
    )

    hd_yb0, hd_cb0, hd_cb1 = y_swap(hd_b0), core_swap(hd_b0), core_swap(hd_b1)
    join_a = normalize(layer_a.astype(jnp.float32), join_gain, moment_sum(pairs))
    ja_before, ja_after = sent(join_a, 1), sent(join_a, -1)
    mixed_b = units_down(((hd_b0, hd_b1),), 0, heads_out((at_b, at_cb, at_yb, at_fb)))
    hd_b1, hd_cb0, hd_cb1, hd_yb0, mixed_b, layer_a, join_a, ja_before, ja_after = sync(
        hd_b1, hd_cb0, hd_cb1, hd_yb0, mixed_b, layer_a, join_a, ja_before, ja_after
    )

    hd_yb1, ja_away = y_swap(hd_b1), sent(join_a, 2)
    mixed_b = units_down(((hd_cb0, hd_cb1),), 1, mixed_b)
    hd_yb0, hd_yb1, mixed_b, join_a, ja_before, ja_after, ja_away = sync(
        hd_yb0, hd_yb1, mixed_b, join_a, ja_before, ja_after, ja_away
    )

    hd_fb0, hd_fb1 = core_swap(hd_yb0), core_swap(hd_yb1)
    mixed_b = units_down(((hd_yb0, hd_yb1), (hd_fb0, hd_fb1)), 2, mixed_b)
    mixed_b, join_a, ja_before, ja_after, ja_away = sync(
        mixed_b, join_a, ja_before, ja_after, ja_away
    )

    mine_b, before_b, after_b, away_b = jnp.split(mixed_b, 4)
    from_before, from_after = sent(after_b, 1), sent(before_b, -1)
    tok_ja = jnp.concatenate((join_a, ja_before, ja_after, ja_away))
    js_a = heads_send(tok_ja, join_in)
    tok_ja, js_a, mine_b, away_b, from_before, from_after = sync(
        tok_ja, js_a, mine_b, away_b.astype(jnp.bfloat16), from_before, from_after
    )

    from_away, jc_a = sent(away_b, 2), core_swap(js_a)
    jx_a = heads_across(tok_ja, join_in, jc_a, 2)
    tok_ja, jc_a, jx_a0, jx_a1, mine_b, *arrived = sync(
        tok_ja, jc_a, *jx_a, mine_b, from_before, from_after, from_away
    )

    layer_b = layer_end(start_f32[half:], mine_b, *arrived)
    pairs = moment_flips(moment_pair(layer_b.astype(jnp.float32)))
    jb_before, jb_after, jy_a0 = sent(layer_b, 1), sent(layer_b, -1), y_swap(jx_a0)
    tok_ja, jc_a, jy_a0, jx_a1, layer_b, jb_before, jb_after, *pairs = sync(
        tok_ja, jc_a, jy_a0, jx_a1, layer_b, jb_before, jb_after, *pairs
    )

    totals = moment_shards(moment_sum(pairs))
    jb_away, jy_a1 = sent(layer_b, 2), y_swap(jx_a1)
    tok_ja, jc_a, jy_a0, jy_a1, layer_b, jb_before, jb_after, jb_away, *totals = sync(
        tok_ja, jc_a, jy_a0, jy_a1, layer_b, jb_before, jb_after, jb_away, *totals
    )

    tok_jb = normed_shards((layer_b, jb_before, jb_after, jb_away), join_gain, totals)
    jc_b = core_swap(heads_send(tok_jb, join_in))
    (jx_b,) = heads_across(tok_jb, join_in, jc_b)
    tok_ja, jc_a, jy_a0, jy_a1, tok_jb, jc_b, jx_b = sync(
        tok_ja, jc_a, jy_a0, jy_a1, tok_jb, jc_b, jx_b
    )

    jy_b = y_swap(jx_b)
    parts_a = project_heads(
        run, tok_ja, join_in, join_scales, head_width, jc_a, (jy_a0, jy_a1), False
    )
    tok_jb, jc_b, jy_b, parts_a = sync(tok_jb, jc_b, jy_b, parts_a)

    parts_b = project_heads(run, tok_jb, join_in, join_scales, head_width, jc_b, (jy_b,), False)
    joined = join_blend(run, (parts_a, parts_b))
    joined = joined.reshape(2, 4, half, head_width).swapaxes(0, 1).reshape(8 * half, head_width)
    jo_y, jo_c = y_swap(joined), core_swap(joined)
    jo_f = core_swap(jo_y)
    result = contract(run, ((joined,), (jo_c,), (jo_y,), (jo_f,)), join_out, 1)
    summed = scatter_rows_long(result)
    layer_own = jnp.concatenate((layer_a, layer_b))
    return (layer_own.astype(jnp.float32) + summed).astype(jnp.bfloat16)


def layer(*arrays):
    own_rows, heads_width = arrays[0].shape[0], arrays[2].shape[1]
    fits = lax.axis_size("cols") == 4 and lax.axis_size("rows") == 4
    fits = fits and own_rows == 2 * TOK_CAM and heads_width % (4 * HEAD_DIM) == 0
    return (fast_body if fits else generic_body)(*arrays)


def solution(mesh):
    in_specs = (
        P(("groups", "rows"), "cols"),
        P("cols"),
        P("cols", "rows"),
        P("cols", "rows"),
        P("cols", "rows"),
        P("rows"),
        P("rows"),
        P("rows", "cols"),
        P("cols", "rows"),
        P("rows"),
        P("rows", "cols"),
        P("cols"),
        P("cols"),
        P("cols", "rows"),
        P("cols", "rows"),
        P("cols", "rows"),
        P("rows"),
        P("rows"),
        P("rows", "cols"),
    )
    out_specs = P(("groups", "rows"), "cols")
    return jax.shard_map(layer, mesh=mesh, in_specs=in_specs, out_specs=out_specs, check_vma=False)
```

```python
import math

import jax
import jax.numpy as jnp
from jax import lax
from jax.experimental import pallas as pl
from jax.experimental.pallas import tpu as pltpu
from jax.sharding import PartitionSpec as P

HEAD_DIM = 128
TOK_CAM = 64
D = 6144


EPS = 1e-06


def partner_2(array, axis, bit):
    return lax.ppermute(array, axis, [(i, i ^ 1 << bit) for i in range(lax.axis_size(axis))])


def normalize(values, scales, moments):
    row_mean = moments[0] / D
    row_var = moments[1] / D - row_mean * row_mean
    return ((values - row_mean[:, None]) * lax.rsqrt(row_var[:, None] + EPS) * scales).astype(
        jnp.bfloat16
    )


def shard_moments(values):
    return lax.psum((jnp.sum(values, 1), jnp.sum(values * values, 1)), "cols")


def head_norm(values, scales):
    row_count = values.shape[0]
    grouped = values.reshape(row_count, -1, HEAD_DIM)
    row_mean = jnp.mean(grouped, -1, keepdims=True)
    row_var = jnp.mean(grouped * grouped, -1, keepdims=True) - row_mean * row_mean
    normed = (grouped - row_mean) * lax.rsqrt(row_var + EPS)
    return (normed.reshape(row_count, -1) * scales).astype(jnp.bfloat16)


def attend(queries, key_rows, val_rows):
    inv_root = 1.0 / math.sqrt(HEAD_DIM)
    scores = (
        jnp.einsum("bqhd,bkhd->bhqk", queries, key_rows, preferred_element_type=jnp.float32)
        * inv_root
    )
    row_max = jnp.max(scores, -1, keepdims=True)
    weights = jnp.exp(scores - row_max)
    row_sum = jnp.sum(weights, -1)
    blended = jnp.einsum(
        "bhqk,bkhd->bqhd",
        weights.astype(jnp.bfloat16),
        val_rows,
        preferred_element_type=jnp.float32,
    )
    return blended / jnp.transpose(row_sum, (0, 2, 1))[..., None]


def to_heads(matrix, blocks):
    return matrix.reshape(blocks, -1, matrix.shape[1] // HEAD_DIM, HEAD_DIM)


def camera_attention(queries, key_rows, val_rows):
    local_rows = queries.shape[0]
    if local_rows >= TOK_CAM:
        blocks = local_rows // TOK_CAM
        result = attend(
            to_heads(queries, blocks), to_heads(key_rows, blocks), to_heads(val_rows, blocks)
        )
    else:
        cam_span = TOK_CAM // local_rows
        position = lax.axis_index("cols")
        key_value = jnp.stack((key_rows, val_rows))
        for which_bit in range(cam_span.bit_length() - 1):
            partner = partner_2(key_value, "cols", which_bit)
            is_lower = position >> which_bit & 1 == 0
            key_value = jnp.where(
                is_lower,
                jnp.concatenate((key_value, partner), 1),
                jnp.concatenate((partner, key_value), 1),
            )
        result = attend(to_heads(queries, 1), to_heads(key_value[0], 1), to_heads(key_value[1], 1))
    return result.reshape(local_rows, -1).astype(jnp.bfloat16)


def generic_body(
    camera_tokens,
    norm_gain,
    query_weight,
    key_weight,
    value_weight,
    query_gain,
    key_gain,
    out_weight,
    up_weight,
    up_bias,
    down_weight,
    down_bias,
    join_gain,
    join_query,
    join_key,
    join_value,
    join_query_gain,
    join_key_gain,
    join_out,
):
    own_rows = camera_tokens.shape[0]
    all_rows = own_rows * lax.axis_size("rows")
    col_rows = all_rows // lax.axis_size("cols")
    attn_width = query_weight.shape[1]
    start_f32 = camera_tokens.astype(jnp.float32)
    normed_all = lax.all_gather(
        normalize(start_f32, norm_gain, shard_moments(start_f32)), "rows", axis=0, tiled=True
    )
    joint_weight = jnp.concatenate((query_weight, key_weight, value_weight, up_weight), 1)
    joint = lax.psum_scatter(
        jnp.dot(normed_all, joint_weight, preferred_element_type=jnp.float32),
        "cols",
        scatter_dimension=0,
        tiled=True,
    )
    up_sum = joint[:, 3 * attn_width :]
    hidden = jax.nn.gelu(up_sum + up_bias, approximate=False).astype(jnp.bfloat16)
    attended = camera_attention(
        head_norm(joint[:, :attn_width], query_gain),
        head_norm(joint[:, attn_width : 2 * attn_width], key_gain),
        joint[:, 2 * attn_width : 3 * attn_width].astype(jnp.bfloat16),
    )
    attn_all, hidden_all = (
        lax.all_gather(attended, "cols", axis=0, tiled=True),
        lax.all_gather(hidden, "cols", axis=0, tiled=True),
    )
    mixed = lax.psum_scatter(
        jnp.dot(attn_all, out_weight, preferred_element_type=jnp.float32)
        + jnp.dot(hidden_all, down_weight, preferred_element_type=jnp.float32),
        "rows",
        scatter_dimension=0,
        tiled=True,
    )
    layer_own = (start_f32 + mixed + down_bias).astype(jnp.bfloat16)
    layer_f32 = layer_own.astype(jnp.float32)
    join_in = lax.all_gather(
        normalize(layer_f32, join_gain, shard_moments(layer_f32)), "rows", axis=0, tiled=True
    )
    join_weight = jnp.concatenate((join_query, join_key, join_value), 1)
    join_joint = lax.psum_scatter(
        jnp.dot(join_in, join_weight, preferred_element_type=jnp.float32),
        "cols",
        scatter_dimension=0,
        tiled=True,
    )
    join_q = head_norm(join_joint[:, :attn_width], join_query_gain)
    join_k = head_norm(join_joint[:, attn_width : 2 * attn_width], join_key_gain)
    join_v = join_joint[:, 2 * attn_width :].astype(jnp.bfloat16)
    heads_here = attn_width // HEAD_DIM
    query_heads = join_q.reshape(col_rows, heads_here, HEAD_DIM)
    inv_root = 1.0 / math.sqrt(HEAD_DIM)
    run_max = jnp.full((heads_here, col_rows), -jnp.inf, jnp.float32)
    run_sum = jnp.zeros((heads_here, col_rows), jnp.float32)
    accum = jnp.zeros((col_rows, heads_here, HEAD_DIM), jnp.float32)
    key_part = lax.all_gather(join_k, "cols", axis=0, tiled=True)
    val_part = lax.all_gather(join_v, "cols", axis=0, tiled=True)
    row_count = key_part.shape[0]
    key_heads = key_part.reshape(row_count, heads_here, HEAD_DIM)
    val_heads = val_part.reshape(row_count, heads_here, HEAD_DIM)
    scores = (
        jnp.einsum("qhd,khd->hqk", query_heads, key_heads, preferred_element_type=jnp.float32)
        * inv_root
    )
    new_max = jnp.max(scores, -1)
    factor = jnp.exp(run_max - new_max)
    weights = jnp.exp(scores - new_max[..., None])
    run_sum = run_sum * factor + jnp.sum(weights, -1)
    accum = accum * jnp.transpose(factor)[..., None] + jnp.einsum(
        "hqk,khd->qhd", weights.astype(jnp.bfloat16), val_heads, preferred_element_type=jnp.float32
    )
    run_max, run_sum, accum = (new_max, run_sum, accum)
    joined_attn = (
        (accum / jnp.transpose(run_sum)[..., None])
        .reshape(col_rows, attn_width)
        .astype(jnp.bfloat16)
    )
    joined_all = lax.all_gather(joined_attn, "cols", axis=0, tiled=True)
    result = lax.psum_scatter(
        jnp.dot(joined_all, join_out, preferred_element_type=jnp.float32),
        "rows",
        scatter_dimension=0,
        tiled=True,
    )
    return (layer_own.astype(jnp.float32) + result).astype(jnp.bfloat16)


VMEM_BYTES = 48 * 1024 * 1024


def flip(array, mask):
    size = lax.axis_size("cols")
    return lax.ppermute(array, "cols", [(i, i ^ mask) for i in range(size)])


def core_swap(array):
    return flip(array, 1)


def y_swap(array):
    return flip(array, 2)


def row_shift(array, shift):
    size = lax.axis_size("rows")
    return lax.ppermute(array, "rows", [(i, (i + shift) % size) for i in range(size)])


class Runner:
    def __init__(self, position):
        self.position = position

    def __call__(self, kernel, grid, operands, in_specs, out_shape, out_spec):
        return pl.pallas_call(
            kernel,
            out_shape=out_shape,
            grid_spec=pltpu.PrefetchScalarGridSpec(
                num_scalar_prefetch=1, grid=grid, in_specs=list(in_specs), out_specs=out_spec
            ),
            compiler_params=pltpu.CompilerParams(vmem_limit_bytes=VMEM_BYTES),
            cost_estimate=pl.CostEstimate(flops=1, bytes_accessed=1, transcendentals=0),
        )(self.position, *operands)


def joined_rows(refs, at=slice(None)):
    return jnp.concatenate([ref[:, at] for ref in refs])


def store_rows(refs, at, values):
    piece = values.shape[0] // len(refs)
    for j, ref in enumerate(refs):
        ref[:, at] = values[j * piece : (j + 1) * piece].astype(ref.dtype)


def whole(array):
    return pl.BlockSpec(array.shape, lambda s, pos: (0,) * array.ndim)


def mine_of(pos):
    return 2 * pos[0] + pos[1]


def across_of(pos):
    return 2 * pos[0] + 1 - pos[1]


def dot_f32(a, b):
    return jnp.dot(a, b, preferred_element_type=jnp.float32)


def project_send(run, tokens, weights, width, sub):
    rows, depth = tokens.shape
    block = width // sub
    wide = len(weights) * block

    def kernel(pos, tokens_ref, *refs):
        for i in range(len(weights)):
            refs[-1][:, i * block : (i + 1) * block] = dot_f32(
                tokens_ref[...], refs[i][...]
            ).astype(jnp.bfloat16)

    spec = pl.BlockSpec((depth, block), lambda s, pos: (0, 2 * (1 - pos[0]) * sub + s))
    return run(
        kernel,
        (2 * sub,),
        (tokens, *weights),
        (whole(tokens), *[spec] * len(weights)),
        jax.ShapeDtypeStruct((rows, 2 * sub * wide), jnp.bfloat16),
        pl.BlockSpec((rows, wide), lambda s, pos: (0, s)),
    )


def project_across(run, tokens, weights, width, sub, arrived, pieces=1):
    rows, depth = tokens.shape
    block = width // sub
    wide = len(weights) * block

    def kernel(pos, tokens_ref, *refs):
        for i in range(len(weights)):
            at = slice(i * block, (i + 1) * block)
            part = dot_f32(tokens_ref[...], refs[i][...])
            part = part + refs[len(weights)][:, at].astype(jnp.float32)
            store_rows(refs[len(weights) + 1 :], at, part)

    spec = pl.BlockSpec((depth, block), lambda s, pos: (0, across_of(pos) * sub + s))
    return run(
        kernel,
        (sub,),
        (tokens, *weights, arrived),
        (
            whole(tokens),
            *[spec] * len(weights),
            pl.BlockSpec((rows, wide), lambda s, pos: (0, (1 - pos[1]) * sub + s)),
        ),
        (jax.ShapeDtypeStruct((rows // pieces, sub * wide), jnp.bfloat16),) * pieces,
        (pl.BlockSpec((rows // pieces, wide), lambda s, pos: (0, s)),) * pieces,
    )


def project_hidden(run, tokens, weight, bias, width, sub, arrived, from_side, at=0):
    depth = tokens.shape[1]
    rows = from_side.shape[0]
    block = width // sub

    def kernel(pos, tokens_ref, weight_ref, bias_ref, arrived_ref, side_ref, out_ref):
        total = dot_f32(tokens_ref[...], weight_ref[...])
        total = total + arrived_ref[...].astype(jnp.float32) + side_ref[...].astype(jnp.float32)
        total = total + bias_ref[...]
        out_ref[...] = (total * (1.0 + lax.erf(total * math.sqrt(0.5))) * 0.5).astype(jnp.bfloat16)

    return run(
        kernel,
        (sub,),
        (tokens, weight, bias, arrived, from_side),
        (
            pl.BlockSpec((rows, depth), lambda s, pos: (at, 0)),
            pl.BlockSpec((depth, block), lambda s, pos: (0, mine_of(pos) * sub + s)),
            pl.BlockSpec((1, block), lambda s, pos: (0, mine_of(pos) * sub + s)),
            pl.BlockSpec((rows, block), lambda s, pos: (at, pos[1] * sub + s)),
            pl.BlockSpec((rows, block), lambda s, pos: (0, s)),
        ),
        jax.ShapeDtypeStruct((rows, width), jnp.bfloat16),
        pl.BlockSpec((rows, block), lambda s, pos: (0, s)),
    )


def project_keep(run, tokens, weights, width, arrived):
    rows, depth = tokens.shape
    wide = len(weights) * width

    def kernel(pos, tokens_ref, *refs):
        arrived_ref, out_ref = refs[len(weights) :]
        for i in range(len(weights)):
            at = slice(i * width, (i + 1) * width)
            part = dot_f32(tokens_ref[...], refs[i][...])
            out_ref[:, at] = part + arrived_ref[:, at].astype(jnp.float32)

    spec = pl.BlockSpec((depth, width), lambda s, pos: (0, mine_of(pos)))
    return run(
        kernel,
        (1,),
        (tokens, *weights, arrived),
        (
            whole(tokens),
            *[spec] * len(weights),
            pl.BlockSpec((rows, wide), lambda s, pos: (0, pos[1])),
        ),
        jax.ShapeDtypeStruct((rows, wide), jnp.float32),
        pl.BlockSpec((rows, wide), lambda s, pos: (0, 0)),
    )


def unit_norm(values, scales):
    row_mean = jnp.mean(values, -1, keepdims=True)
    row_var = jnp.mean(values * values, -1, keepdims=True) - row_mean * row_mean
    return ((values - row_mean) * lax.rsqrt(row_var + EPS) * scales).astype(jnp.bfloat16)


def softmax_blend(query, key, value, keep=None):
    scores = lax.dot_general(
        query, key, (((1,), (1,)), ((), ())), preferred_element_type=jnp.float32
    ) * (1.0 / math.sqrt(HEAD_DIM))
    if keep is not None:
        scores = jnp.where(keep, scores, -jnp.inf)
    weights = jnp.exp(scores - jnp.max(scores, -1, keepdims=True))
    row_sum = jnp.sum(weights, -1, keepdims=True)
    blended = dot_f32(weights.astype(jnp.bfloat16), value)
    return (blended / row_sum).astype(jnp.bfloat16)


def project_heads(run, tokens, weights, scales, width, arrived, from_side, attend_camera):
    rows, depth = tokens.shape
    heads = width // HEAD_DIM
    out_width = width if attend_camera else 3 * width

    def kernel(pos, tokens_ref, *refs):
        weight_refs, scale_refs = refs[:3], refs[3:5]
        arrived_ref, *side_refs, out_ref = refs[5:]
        raws = []
        for i in range(3):
            at = slice(i * width, (i + 1) * width)
            raw = dot_f32(tokens_ref[...], weight_refs[i][...])
            raw = raw + arrived_ref[:, at].astype(jnp.float32)
            raws.append(raw + joined_rows(side_refs, at).astype(jnp.float32))
        if attend_camera:
            row_cam = lax.broadcasted_iota(jnp.int32, (rows, rows), 0) // TOK_CAM
            col_cam = lax.broadcasted_iota(jnp.int32, (rows, rows), 1) // TOK_CAM
            same = row_cam == col_cam
        for h in range(heads):
            at = slice(h * HEAD_DIM, (h + 1) * HEAD_DIM)
            query = unit_norm(raws[0][:, at], scale_refs[0][:, at])
            key = unit_norm(raws[1][:, at], scale_refs[1][:, at])
            value = raws[2][:, at].astype(jnp.bfloat16)
            if attend_camera:
                out_ref[:, at] = softmax_blend(query, key, value, same)
            else:
                out_ref[:, at] = query
                out_ref[:, width + h * HEAD_DIM : width + (h + 1) * HEAD_DIM] = key
                out_ref[:, 2 * width + h * HEAD_DIM : 2 * width + (h + 1) * HEAD_DIM] = value

    weight_spec = pl.BlockSpec((depth, width), lambda s, pos: (0, mine_of(pos)))
    scale_spec = pl.BlockSpec((1, width), lambda s, pos: (0, mine_of(pos)))
    return run(
        kernel,
        (1,),
        (tokens, *weights, *scales, arrived, *from_side),
        (
            whole(tokens),
            *[weight_spec] * 3,
            *[scale_spec] * 2,
            pl.BlockSpec((rows, 3 * width), lambda s, pos: (0, pos[1])),
            *[whole(piece) for piece in from_side],
        ),
        jax.ShapeDtypeStruct((rows, out_width), jnp.bfloat16),
        pl.BlockSpec((rows, out_width), lambda s, pos: (0, 0)),
    )


def contract(run, parts, weight, sub, first=0, start=None):
    rows = sum(piece.shape[0] for piece in parts[0])
    width = parts[0][0].shape[1]
    count, pieces = len(parts), len(parts[0])
    out_width = weight.shape[1]
    block = width // sub

    def kernel(pos, weight_ref, *refs):
        out_ref = refs[-1]
        step = pl.program_id(0)
        for i in range(count):

            @pl.when(step // sub == i)
            def _(i=i):
                part = joined_rows(refs[i * pieces : (i + 1) * pieces])
                term = dot_f32(part, weight_ref[...])
                if i > 0:
                    out_ref[...] += term
                elif sub == 1:
                    out_ref[...] = term if start is None else term + refs[-2][...]
                else:

                    @pl.when(step == 0)
                    def _():
                        out_ref[...] = term if start is None else term + refs[-2][...]

                    @pl.when(step > 0)
                    def _():
                        out_ref[...] += term

    def weight_block(s, pos):
        i = s // sub + first
        return (2 * (pos[0] ^ (i & 1)) + (pos[1] ^ (i >> 1))) * sub + s % sub, 0

    def part_spec(i):
        return pl.BlockSpec(
            (rows // pieces, block), lambda s, pos: (0, jnp.clip(s - i * sub, 0, sub - 1))
        )

    operands = [weight, *[piece for part in parts for piece in part]]
    in_specs = [pl.BlockSpec((block, out_width), weight_block)]
    in_specs += [part_spec(i) for i in range(count) for _ in range(pieces)]
    if start is not None:
        operands.append(start)
        in_specs.append(whole(start))
    return run(
        kernel,
        (count * sub,),
        operands,
        in_specs,
        jax.ShapeDtypeStruct((rows, out_width), jnp.float32),
        pl.BlockSpec((rows, out_width), lambda s, pos: (0, 0)),
    )


def join_blend(run, parts, kept, from_side, scales):
    rows = parts.shape[0] + kept.shape[0]
    heads = parts.shape[1] // 3 // HEAD_DIM

    def kernel(pos, *refs):
        part_refs, kept_refs, side_refs = refs[:3], refs[3:6], refs[6:9]
        *scale_refs, out_ref = refs[9:]
        raws = [k[...] + s[...].astype(jnp.float32) for k, s in zip(kept_refs, side_refs)]
        late = [unit_norm(raws[i], scale_refs[i][...]) for i in range(2)]
        late.append(raws[2].astype(jnp.bfloat16))
        query, key, value = (
            jnp.concatenate((part_refs[i][...], late[i])) for i in range(3)
        )
        out_ref[...] = softmax_blend(query, key, value)

    def specs(array):
        return [
            pl.BlockSpec((array.shape[0], HEAD_DIM), lambda h, pos, i=i: (0, i * heads + h))
            for i in range(3)
        ]

    scale_spec = pl.BlockSpec((1, HEAD_DIM), lambda h, pos: (0, mine_of(pos) * heads + h))
    return run(
        kernel,
        (heads,),
        (*[parts] * 3, *[kept] * 3, *[from_side] * 3, *scales),
        (*specs(parts), *specs(kept), *specs(from_side), *[scale_spec] * 2),
        jax.ShapeDtypeStruct((rows, heads * HEAD_DIM), jnp.bfloat16),
        pl.BlockSpec((rows, HEAD_DIM), lambda h, pos: (0, h)),
    )


def moment_pair(values):
    return jnp.stack((jnp.sum(values, 1), jnp.sum(values * values, 1)))


def moment_flips(pair):
    return pair, flip(pair, 1), flip(pair, 2), flip(pair, 3)


def moment_sum(pairs):
    return (pairs[0] + pairs[1]) + (pairs[2] + pairs[3])


def sent(array, shift):
    return row_shift(array.astype(jnp.bfloat16), shift)


def sent_on(before, after):
    half = before.shape[0] // 2
    return sent(before[:half], 1), sent(after[half:], -1)


def moment_shards(total):
    return total, row_shift(total, 1), row_shift(total, -1), row_shift(total, 2)


def normed_shards(shards, scales, totals):
    return jnp.concatenate(
        [normalize(x.astype(jnp.float32), scales, m) for x, m in zip(shards, totals)]
    )


def sync(*values):
    return lax.optimization_barrier(values)


def scatter_rows_long(terms):
    own, before, after, away = jnp.split(terms, 4)
    half = own.shape[0] // 2

    def send(array, shift):
        return row_shift(array.astype(jnp.bfloat16), shift).astype(jnp.float32)

    to_after = send(away[:half], 1)
    to_before = send(away[half:], -1)
    from_before = jnp.concatenate((send(after[:half] + to_after, 1), send(after[half:], 1)))
    from_after = jnp.concatenate((send(before[:half], -1), send(before[half:] + to_before, -1)))
    return own + from_before + from_after


def fast_body(
    camera_tokens,
    norm_gain,
    query_weight,
    key_weight,
    value_weight,
    query_gain,
    key_gain,
    out_weight,
    up_weight,
    up_bias,
    down_weight,
    down_bias,
    join_gain,
    join_query,
    join_key,
    join_value,
    join_query_gain,
    join_key_gain,
    join_out,
):
    half = TOK_CAM
    index = lax.axis_index("cols")
    run = Runner(jnp.stack((index & 1, index >> 1)).astype(jnp.int32))
    head_width = query_weight.shape[1] // 4
    unit_width = up_weight.shape[1] // 4
    sub = 3 if unit_width % (3 * 256) == 0 else 1
    heads_in = (query_weight, key_weight, value_weight)
    join_in = (join_query, join_key, join_value)
    scales = (query_gain[None], key_gain[None])
    join_scales = (join_query_gain[None], join_key_gain[None])
    bias = up_bias[None]

    def heads_send(tokens, weights):
        return project_send(run, tokens, weights, head_width, 1)

    def heads_across(tokens, weights, arrived, pieces=1):
        return project_across(run, tokens, weights, head_width, 1, arrived, pieces)

    def heads_out(parts, first=0, start=None):
        return contract(run, [(part,) for part in parts], out_weight, 1, first, start)

    def units_down(parts, first, start):
        return contract(run, parts, down_weight, 2, first, start)

    def units_send(tokens):
        return project_send(run, tokens, (up_weight,), unit_width, sub)

    def units_across(tokens, arrived, pieces):
        return project_across(run, tokens, (up_weight,), unit_width, sub, arrived, pieces)

    def units_end(tokens, arrived, side, at=0):
        return project_hidden(run, tokens, up_weight, bias, unit_width, sub, arrived, side, at)

    def layer_end(start, own, *arrived):
        total = own
        for term in arrived:
            total = total + term.astype(jnp.float32)
        return (start + total + down_bias).astype(jnp.bfloat16)

    start_f32 = camera_tokens.astype(jnp.float32)
    own_a, own_b = camera_tokens[:half], camera_tokens[half:]
    pairs = moment_flips(moment_pair(start_f32))
    own_a, own_b, a_before, a_after, *pairs = sync(
        own_a, own_b, sent(own_a, 1), sent(own_a, -1), *pairs
    )

    totals = moment_shards(moment_sum(pairs))
    own_a, own_b, a_before, a_after, a_away0, a_away1, *totals = sync(
        own_a, own_b, a_before, a_after, *sent_on(a_before, a_after), *totals
    )
    a_away = jnp.concatenate((a_away0, a_away1))
    totals_a = [total[:, :half] for total in totals]
    totals_b = [total[:, half:] for total in totals]

    b_before = sent(own_b, 1)
    tok_a = normed_shards((own_a, a_before, a_after, a_away), norm_gain, totals_a)
    qs_a = heads_send(tok_a, heads_in)
    tok_a, own_b, b_before, qs_a = sync(tok_a, own_b, b_before, qs_a)

    b_after, qc_a = sent(own_b, -1), core_swap(qs_a)
    us_a = units_send(tok_a)
    tok_a, own_b, b_after, qc_a, us_a = sync(tok_a, own_b, b_after, qc_a, us_a)

    uc_a = core_swap(us_a)
    (qx_a,) = heads_across(tok_a, heads_in, qc_a)
    tok_a, own_b, b_before, b_after, qc_a, uc_a, qx_a = sync(
        tok_a, own_b, b_before, b_after, qc_a, uc_a, qx_a
    )

    qy_a, b_away0, b_away1 = y_swap(qx_a), *sent_on(b_before, b_after)
    (ux_a,) = units_across(tok_a, uc_a, 1)
    tok_a, qc_a, uc_a, ux_a, qy_a, own_b, b_before, b_after, b_away0, b_away1 = sync(
        tok_a, qc_a, uc_a, ux_a, qy_a, own_b, b_before, b_after, b_away0, b_away1
    )
    b_away = jnp.concatenate((b_away0, b_away1))

    uy_a = y_swap(ux_a)
    tok_b = normed_shards((own_b, b_before, b_after, b_away), norm_gain, totals_b)
    qs_b = heads_send(tok_b, heads_in)
    us_b = units_send(tok_b)
    at_a = project_heads(run, tok_a, heads_in, scales, head_width, qc_a, (qy_a,), True)
    tok_a, tok_b, qs_b, us_b, at_a, uc_a, uy_a = sync(
        tok_a, tok_b, qs_b, us_b, at_a, uc_a, uy_a
    )

    at_ya, at_ca, qc_b, uc_b = y_swap(at_a), core_swap(at_a), core_swap(qs_b), core_swap(us_b)
    hd_a = units_end(tok_a, uc_a, uy_a)
    tok_b, at_a, at_ya, at_ca, qc_b, uc_b, hd_a = sync(
        tok_b, at_a, at_ya, at_ca, qc_b, uc_b, hd_a
    )

    hd_ya, hd_ca, at_fa = y_swap(hd_a), core_swap(hd_a), core_swap(at_ya)
    (qx_b,) = heads_across(tok_b, heads_in, qc_b)
    ux_b = units_across(tok_b, uc_b, 2)
    mixed_a = units_down(((hd_a,),), 0, heads_out((at_a, at_ca, at_ya)))
    tok_b, at_fa, hd_ya, hd_ca, qc_b, uc_b, qx_b, mixed_a, *ux_b = sync(
        tok_b, at_fa, hd_ya, hd_ca, qc_b, uc_b, qx_b, mixed_a, *ux_b
    )

    qy_b, hd_fa = y_swap(qx_b), core_swap(hd_ya)
    mixed_a = units_down(((hd_ca,),), 1, heads_out((at_fa,), 3, mixed_a))
    mixed_a = units_down(((hd_ya,), (hd_fa,)), 2, mixed_a)
    tok_b, mixed_a, qc_b, qy_b, uc_b, ux_b0, ux_b1 = sync(
        tok_b, mixed_a, qc_b, qy_b, uc_b, *ux_b
    )

    uy_b0 = y_swap(ux_b0)
    mine_a, before_a, after_a, away_a = jnp.split(mixed_a, 4)
    from_before, from_after = sent(after_a, 1), sent(before_a, -1)
    at_b = project_heads(run, tok_b, heads_in, scales, head_width, qc_b, (qy_b,), True)
    at_yb = y_swap(at_b)
    tok_b, uc_b, uy_b0, ux_b1, at_b, at_yb, mine_a, away_a, from_before, from_after = sync(
        tok_b, uc_b, uy_b0, ux_b1, at_b, at_yb, mine_a, away_a.astype(jnp.bfloat16),
        from_before, from_after,
    )

    uy_b1, from_away, at_cb, at_fb = (
        y_swap(ux_b1), sent(away_a, 2), core_swap(at_b), core_swap(at_yb)
    )
    hd_b0 = units_end(tok_b, uc_b, uy_b0)
    mixed_b = heads_out((at_b, at_cb, at_yb, at_fb))
    tok_b, uc_b, uy_b1, hd_b0, mixed_b, mine_a, *arrived = sync(
        tok_b, uc_b, uy_b1, hd_b0, mixed_b, mine_a, from_before, from_after, from_away
    )

    hd_yb0, hd_cb0 = y_swap(hd_b0), core_swap(hd_b0)
    layer_a = layer_end(start_f32[:half], mine_a, *arrived)
    pairs = moment_flips(moment_pair(layer_a.astype(jnp.float32)))
    hd_b1 = units_end(tok_b, uc_b, uy_b1, 1)
    hd_b0, hd_b1, hd_yb0, hd_cb0, mixed_b, layer_a, *pairs = sync(
        hd_b0, hd_b1, hd_yb0, hd_cb0, mixed_b, layer_a, *pairs
    )

    hd_yb1, hd_cb1, hd_fb0 = y_swap(hd_b1), core_swap(hd_b1), core_swap(hd_yb0)
    join_a = normalize(layer_a.astype(jnp.float32), join_gain, moment_sum(pairs))
    ja_before, ja_after = sent(join_a, 1), sent(join_a, -1)
    mixed_b = units_down(((hd_b0, hd_b1),), 0, mixed_b)
    hd_cb0, hd_cb1, hd_yb0, hd_yb1, hd_fb0, mixed_b, layer_a, join_a, ja_before, ja_after = sync(
        hd_cb0, hd_cb1, hd_yb0, hd_yb1, hd_fb0, mixed_b, layer_a, join_a, ja_before, ja_after
    )

    hd_fb1 = core_swap(hd_yb1)
    mixed_b = units_down(((hd_cb0, hd_cb1),), 1, mixed_b)
    hd_yb0, hd_yb1, hd_fb0, hd_fb1, mixed_b, join_a, ja_before, ja_after = sync(
        hd_yb0, hd_yb1, hd_fb0, hd_fb1, mixed_b, join_a, ja_before, ja_after
    )

    ja_away0, ja_away1 = sent_on(ja_before, ja_after)
    mixed_b = units_down(((hd_yb0, hd_yb1), (hd_fb0, hd_fb1)), 2, mixed_b)
    mixed_b, join_a, ja_before, ja_after, ja_away0, ja_away1 = sync(
        mixed_b, join_a, ja_before, ja_after, ja_away0, ja_away1
    )

    mine_b, before_b, after_b, away_b = jnp.split(mixed_b, 4)
    part = half // 2
    to_after, to_before = sent(away_b[:part], 1), sent(away_b[part:], -1)
    mine_b, before_b, after_b, to_after, to_before, join_a, *shards = sync(
        mine_b, before_b, after_b, to_after, to_before, join_a,
        ja_before, ja_after, ja_away0, ja_away1,
    )

    after_b = jnp.concatenate((after_b[:part] + to_after.astype(jnp.float32), after_b[part:]))
    before_b = jnp.concatenate((before_b[:part], before_b[part:] + to_before.astype(jnp.float32)))
    from_before, from_after = sent(after_b, 1), sent(before_b, -1)
    tok_ja = jnp.concatenate((join_a, *shards))
    js_a = heads_send(tok_ja, join_in)
    tok_ja, js_a, mine_b, *arrived = sync(tok_ja, js_a, mine_b, from_before, from_after)

    layer_b = layer_end(start_f32[half:], mine_b, *arrived)
    pairs = moment_flips(moment_pair(layer_b.astype(jnp.float32)))
    jb_before, jb_after, jc_a = sent(layer_b, 1), sent(layer_b, -1), core_swap(js_a)
    jx_a = heads_across(tok_ja, join_in, jc_a, 2)
    tok_ja, jc_a, jx_a0, jx_a1, layer_b, jb_before, jb_after, *pairs = sync(
        tok_ja, jc_a, *jx_a, layer_b, jb_before, jb_after, *pairs
    )

    totals = moment_shards(moment_sum(pairs))
    jb_away0, jb_away1 = sent_on(jb_before, jb_after)
    jy_a0 = y_swap(jx_a0)
    tok_ja, jc_a, jy_a0, jx_a1, layer_b, jb_before, jb_after, jb_away0, jb_away1, *totals = sync(
        tok_ja, jc_a, jy_a0, jx_a1, layer_b, jb_before, jb_after, jb_away0, jb_away1, *totals
    )

    jy_a1 = y_swap(jx_a1)
    jb_away = jnp.concatenate((jb_away0, jb_away1))
    tok_jb = normed_shards((layer_b, jb_before, jb_after, jb_away), join_gain, totals)
    jc_b = core_swap(heads_send(tok_jb, join_in))
    (jx_b,) = heads_across(tok_jb, join_in, jc_b)
    tok_ja, jc_a, jy_a0, jy_a1, tok_jb, jc_b, jx_b = sync(
        tok_ja, jc_a, jy_a0, jy_a1, tok_jb, jc_b, jx_b
    )

    jy_b = y_swap(jx_b)
    parts_a = project_heads(
        run, tok_ja, join_in, join_scales, head_width, jc_a, (jy_a0, jy_a1), False
    )
    kept_b = project_keep(run, tok_jb, join_in, head_width, jc_b)
    jy_b, parts_a, kept_b = sync(jy_b, parts_a, kept_b)

    joined = join_blend(run, parts_a, kept_b, jy_b, join_scales)
    joined = joined.reshape(2, 4, half, head_width).swapaxes(0, 1).reshape(8 * half, head_width)
    jo_y, jo_c = y_swap(joined), core_swap(joined)
    jo_f = core_swap(jo_y)
    result = contract(run, ((joined,), (jo_c,), (jo_y,), (jo_f,)), join_out, 1)
    summed = scatter_rows_long(result)
    layer_own = jnp.concatenate((layer_a, layer_b))
    return (layer_own.astype(jnp.float32) + summed).astype(jnp.bfloat16)


def layer(*arrays):
    own_rows, heads_width = arrays[0].shape[0], arrays[2].shape[1]
    fits = lax.axis_size("cols") == 4 and lax.axis_size("rows") == 4
    fits = fits and own_rows == 2 * TOK_CAM and heads_width % (4 * HEAD_DIM) == 0
    return (fast_body if fits else generic_body)(*arrays)


def solution(mesh):
    in_specs = (
        P(("groups", "rows"), "cols"),
        P("cols"),
        P("cols", "rows"),
        P("cols", "rows"),
        P("cols", "rows"),
        P("rows"),
        P("rows"),
        P("rows", "cols"),
        P("cols", "rows"),
        P("rows"),
        P("rows", "cols"),
        P("cols"),
        P("cols"),
        P("cols", "rows"),
        P("cols", "rows"),
        P("cols", "rows"),
        P("rows"),
        P("rows"),
        P("rows", "cols"),
    )
    out_specs = P(("groups", "rows"), "cols")
    return jax.shard_map(layer, mesh=mesh, in_specs=in_specs, out_specs=out_specs, check_vma=False)
```

```python
import math

import jax
import jax.numpy as jnp
from jax import lax
from jax.experimental import pallas as pl
from jax.experimental.pallas import tpu as pltpu
from jax.sharding import PartitionSpec as P

HEAD_DIM = 128
TOK_CAM = 64
D = 6144


EPS = 1e-06


def partner_2(array, axis, bit):
    return lax.ppermute(array, axis, [(i, i ^ 1 << bit) for i in range(lax.axis_size(axis))])


def normalize(values, scales, moments):
    row_mean = moments[0] / D
    row_var = moments[1] / D - row_mean * row_mean
    return ((values - row_mean[:, None]) * lax.rsqrt(row_var[:, None] + EPS) * scales).astype(
        jnp.bfloat16
    )


def shard_moments(values):
    return lax.psum((jnp.sum(values, 1), jnp.sum(values * values, 1)), "cols")


def head_norm(values, scales):
    row_count = values.shape[0]
    grouped = values.reshape(row_count, -1, HEAD_DIM)
    row_mean = jnp.mean(grouped, -1, keepdims=True)
    row_var = jnp.mean(grouped * grouped, -1, keepdims=True) - row_mean * row_mean
    normed = (grouped - row_mean) * lax.rsqrt(row_var + EPS)
    return (normed.reshape(row_count, -1) * scales).astype(jnp.bfloat16)


def attend(queries, key_rows, val_rows):
    inv_root = 1.0 / math.sqrt(HEAD_DIM)
    scores = (
        jnp.einsum("bqhd,bkhd->bhqk", queries, key_rows, preferred_element_type=jnp.float32)
        * inv_root
    )
    row_max = jnp.max(scores, -1, keepdims=True)
    weights = jnp.exp(scores - row_max)
    row_sum = jnp.sum(weights, -1)
    blended = jnp.einsum(
        "bhqk,bkhd->bqhd",
        weights.astype(jnp.bfloat16),
        val_rows,
        preferred_element_type=jnp.float32,
    )
    return blended / jnp.transpose(row_sum, (0, 2, 1))[..., None]


def to_heads(matrix, blocks):
    return matrix.reshape(blocks, -1, matrix.shape[1] // HEAD_DIM, HEAD_DIM)


def camera_attention(queries, key_rows, val_rows):
    local_rows = queries.shape[0]
    if local_rows >= TOK_CAM:
        blocks = local_rows // TOK_CAM
        result = attend(
            to_heads(queries, blocks), to_heads(key_rows, blocks), to_heads(val_rows, blocks)
        )
    else:
        cam_span = TOK_CAM // local_rows
        position = lax.axis_index("cols")
        key_value = jnp.stack((key_rows, val_rows))
        for which_bit in range(cam_span.bit_length() - 1):
            partner = partner_2(key_value, "cols", which_bit)
            is_lower = position >> which_bit & 1 == 0
            key_value = jnp.where(
                is_lower,
                jnp.concatenate((key_value, partner), 1),
                jnp.concatenate((partner, key_value), 1),
            )
        result = attend(to_heads(queries, 1), to_heads(key_value[0], 1), to_heads(key_value[1], 1))
    return result.reshape(local_rows, -1).astype(jnp.bfloat16)


def generic_body(
    camera_tokens,
    norm_gain,
    query_weight,
    key_weight,
    value_weight,
    query_gain,
    key_gain,
    out_weight,
    up_weight,
    up_bias,
    down_weight,
    down_bias,
    join_gain,
    join_query,
    join_key,
    join_value,
    join_query_gain,
    join_key_gain,
    join_out,
):
    own_rows = camera_tokens.shape[0]
    all_rows = own_rows * lax.axis_size("rows")
    col_rows = all_rows // lax.axis_size("cols")
    attn_width = query_weight.shape[1]
    start_f32 = camera_tokens.astype(jnp.float32)
    normed_all = lax.all_gather(
        normalize(start_f32, norm_gain, shard_moments(start_f32)), "rows", axis=0, tiled=True
    )
    joint_weight = jnp.concatenate((query_weight, key_weight, value_weight, up_weight), 1)
    joint = lax.psum_scatter(
        jnp.dot(normed_all, joint_weight, preferred_element_type=jnp.float32),
        "cols",
        scatter_dimension=0,
        tiled=True,
    )
    up_sum = joint[:, 3 * attn_width :]
    hidden = jax.nn.gelu(up_sum + up_bias, approximate=False).astype(jnp.bfloat16)
    attended = camera_attention(
        head_norm(joint[:, :attn_width], query_gain),
        head_norm(joint[:, attn_width : 2 * attn_width], key_gain),
        joint[:, 2 * attn_width : 3 * attn_width].astype(jnp.bfloat16),
    )
    attn_all, hidden_all = (
        lax.all_gather(attended, "cols", axis=0, tiled=True),
        lax.all_gather(hidden, "cols", axis=0, tiled=True),
    )
    mixed = lax.psum_scatter(
        jnp.dot(attn_all, out_weight, preferred_element_type=jnp.float32)
        + jnp.dot(hidden_all, down_weight, preferred_element_type=jnp.float32),
        "rows",
        scatter_dimension=0,
        tiled=True,
    )
    layer_own = (start_f32 + mixed + down_bias).astype(jnp.bfloat16)
    layer_f32 = layer_own.astype(jnp.float32)
    join_in = lax.all_gather(
        normalize(layer_f32, join_gain, shard_moments(layer_f32)), "rows", axis=0, tiled=True
    )
    join_weight = jnp.concatenate((join_query, join_key, join_value), 1)
    join_joint = lax.psum_scatter(
        jnp.dot(join_in, join_weight, preferred_element_type=jnp.float32),
        "cols",
        scatter_dimension=0,
        tiled=True,
    )
    join_q = head_norm(join_joint[:, :attn_width], join_query_gain)
    join_k = head_norm(join_joint[:, attn_width : 2 * attn_width], join_key_gain)
    join_v = join_joint[:, 2 * attn_width :].astype(jnp.bfloat16)
    heads_here = attn_width // HEAD_DIM
    query_heads = join_q.reshape(col_rows, heads_here, HEAD_DIM)
    inv_root = 1.0 / math.sqrt(HEAD_DIM)
    run_max = jnp.full((heads_here, col_rows), -jnp.inf, jnp.float32)
    run_sum = jnp.zeros((heads_here, col_rows), jnp.float32)
    accum = jnp.zeros((col_rows, heads_here, HEAD_DIM), jnp.float32)
    key_part = lax.all_gather(join_k, "cols", axis=0, tiled=True)
    val_part = lax.all_gather(join_v, "cols", axis=0, tiled=True)
    row_count = key_part.shape[0]
    key_heads = key_part.reshape(row_count, heads_here, HEAD_DIM)
    val_heads = val_part.reshape(row_count, heads_here, HEAD_DIM)
    scores = (
        jnp.einsum("qhd,khd->hqk", query_heads, key_heads, preferred_element_type=jnp.float32)
        * inv_root
    )
    new_max = jnp.max(scores, -1)
    factor = jnp.exp(run_max - new_max)
    weights = jnp.exp(scores - new_max[..., None])
    run_sum = run_sum * factor + jnp.sum(weights, -1)
    accum = accum * jnp.transpose(factor)[..., None] + jnp.einsum(
        "hqk,khd->qhd", weights.astype(jnp.bfloat16), val_heads, preferred_element_type=jnp.float32
    )
    run_max, run_sum, accum = (new_max, run_sum, accum)
    joined_attn = (
        (accum / jnp.transpose(run_sum)[..., None])
        .reshape(col_rows, attn_width)
        .astype(jnp.bfloat16)
    )
    joined_all = lax.all_gather(joined_attn, "cols", axis=0, tiled=True)
    result = lax.psum_scatter(
        jnp.dot(joined_all, join_out, preferred_element_type=jnp.float32),
        "rows",
        scatter_dimension=0,
        tiled=True,
    )
    return (layer_own.astype(jnp.float32) + result).astype(jnp.bfloat16)


VMEM_BYTES = 48 * 1024 * 1024


def flip(array, mask):
    size = lax.axis_size("cols")
    return lax.ppermute(array, "cols", [(i, i ^ mask) for i in range(size)])


def core_swap(array):
    return flip(array, 1)


def y_swap(array):
    return flip(array, 2)


def row_shift(array, shift):
    size = lax.axis_size("rows")
    return lax.ppermute(array, "rows", [(i, (i + shift) % size) for i in range(size)])


class Runner:
    def __init__(self, position):
        self.position = position

    def __call__(self, kernel, grid, operands, in_specs, out_shape, out_spec):
        return pl.pallas_call(
            kernel,
            out_shape=out_shape,
            grid_spec=pltpu.PrefetchScalarGridSpec(
                num_scalar_prefetch=1, grid=grid, in_specs=list(in_specs), out_specs=out_spec
            ),
            compiler_params=pltpu.CompilerParams(vmem_limit_bytes=VMEM_BYTES),
            cost_estimate=pl.CostEstimate(flops=1, bytes_accessed=1, transcendentals=0),
        )(self.position, *operands)


def joined_rows(refs, at=slice(None)):
    return jnp.concatenate([ref[:, at] for ref in refs])


def store_rows(refs, at, values):
    piece = values.shape[0] // len(refs)
    for j, ref in enumerate(refs):
        ref[:, at] = values[j * piece : (j + 1) * piece].astype(ref.dtype)


def whole(array):
    return pl.BlockSpec(array.shape, lambda s, pos: (0,) * array.ndim)


def mine_of(pos):
    return 2 * pos[0] + pos[1]


def across_of(pos):
    return 2 * pos[0] + 1 - pos[1]


def dot_f32(a, b):
    return jnp.dot(a, b, preferred_element_type=jnp.float32)


def project_send(run, tokens, weights, width, sub):
    rows, depth = tokens.shape
    block = width // sub
    wide = len(weights) * block

    def kernel(pos, tokens_ref, *refs):
        for i in range(len(weights)):
            refs[-1][:, i * block : (i + 1) * block] = dot_f32(
                tokens_ref[...], refs[i][...]
            ).astype(jnp.bfloat16)

    spec = pl.BlockSpec((depth, block), lambda s, pos: (0, 2 * (1 - pos[0]) * sub + s))
    return run(
        kernel,
        (2 * sub,),
        (tokens, *weights),
        (whole(tokens), *[spec] * len(weights)),
        jax.ShapeDtypeStruct((rows, 2 * sub * wide), jnp.bfloat16),
        pl.BlockSpec((rows, wide), lambda s, pos: (0, s)),
    )


def project_across(run, tokens, weights, width, sub, arrived, pieces=1):
    rows, depth = tokens.shape
    block = width // sub
    wide = len(weights) * block

    def kernel(pos, tokens_ref, *refs):
        for i in range(len(weights)):
            at = slice(i * block, (i + 1) * block)
            part = dot_f32(tokens_ref[...], refs[i][...])
            part = part + refs[len(weights)][:, at].astype(jnp.float32)
            store_rows(refs[len(weights) + 1 :], at, part)

    spec = pl.BlockSpec((depth, block), lambda s, pos: (0, across_of(pos) * sub + s))
    return run(
        kernel,
        (sub,),
        (tokens, *weights, arrived),
        (
            whole(tokens),
            *[spec] * len(weights),
            pl.BlockSpec((rows, wide), lambda s, pos: (0, (1 - pos[1]) * sub + s)),
        ),
        (jax.ShapeDtypeStruct((rows // pieces, sub * wide), jnp.bfloat16),) * pieces,
        (pl.BlockSpec((rows // pieces, wide), lambda s, pos: (0, s)),) * pieces,
    )


def project_hidden(run, tokens, weight, bias, width, sub, arrived, from_side, at=0):
    depth = tokens.shape[1]
    rows = from_side.shape[0]
    block = width // sub

    def kernel(pos, tokens_ref, weight_ref, bias_ref, arrived_ref, side_ref, out_ref):
        total = dot_f32(tokens_ref[...], weight_ref[...])
        total = total + arrived_ref[...].astype(jnp.float32) + side_ref[...].astype(jnp.float32)
        total = total + bias_ref[...]
        out_ref[...] = (total * (1.0 + lax.erf(total * math.sqrt(0.5))) * 0.5).astype(jnp.bfloat16)

    return run(
        kernel,
        (sub,),
        (tokens, weight, bias, arrived, from_side),
        (
            pl.BlockSpec((rows, depth), lambda s, pos: (at, 0)),
            pl.BlockSpec((depth, block), lambda s, pos: (0, mine_of(pos) * sub + s)),
            pl.BlockSpec((1, block), lambda s, pos: (0, mine_of(pos) * sub + s)),
            pl.BlockSpec((rows, block), lambda s, pos: (at, pos[1] * sub + s)),
            pl.BlockSpec((rows, block), lambda s, pos: (0, s)),
        ),
        jax.ShapeDtypeStruct((rows, width), jnp.bfloat16),
        pl.BlockSpec((rows, block), lambda s, pos: (0, s)),
    )


def project_keep(run, tokens, weights, width, arrived):
    rows, depth = tokens.shape
    wide = len(weights) * width

    def kernel(pos, tokens_ref, *refs):
        arrived_ref, out_ref = refs[len(weights) :]
        for i in range(len(weights)):
            at = slice(i * width, (i + 1) * width)
            part = dot_f32(tokens_ref[...], refs[i][...])
            out_ref[:, at] = part + arrived_ref[:, at].astype(jnp.float32)

    spec = pl.BlockSpec((depth, width), lambda s, pos: (0, mine_of(pos)))
    return run(
        kernel,
        (1,),
        (tokens, *weights, arrived),
        (
            whole(tokens),
            *[spec] * len(weights),
            pl.BlockSpec((rows, wide), lambda s, pos: (0, pos[1])),
        ),
        jax.ShapeDtypeStruct((rows, wide), jnp.float32),
        pl.BlockSpec((rows, wide), lambda s, pos: (0, 0)),
    )


def unit_norm(values, scales):
    row_mean = jnp.mean(values, -1, keepdims=True)
    row_var = jnp.mean(values * values, -1, keepdims=True) - row_mean * row_mean
    return ((values - row_mean) * lax.rsqrt(row_var + EPS) * scales).astype(jnp.bfloat16)


def softmax_blend(query, key, value, keep=None):
    scores = lax.dot_general(
        query, key, (((1,), (1,)), ((), ())), preferred_element_type=jnp.float32
    ) * (1.0 / math.sqrt(HEAD_DIM))
    if keep is not None:
        scores = jnp.where(keep, scores, -jnp.inf)
    weights = jnp.exp(scores - jnp.max(scores, -1, keepdims=True))
    row_sum = jnp.sum(weights, -1, keepdims=True)
    blended = dot_f32(weights.astype(jnp.bfloat16), value)
    return (blended / row_sum).astype(jnp.bfloat16)


def project_heads(run, tokens, weights, scales, width, arrived, from_side, attend_camera):
    rows, depth = tokens.shape
    heads = width // HEAD_DIM
    out_width = width if attend_camera else 3 * width

    def kernel(pos, tokens_ref, *refs):
        weight_refs, scale_refs = refs[:3], refs[3:5]
        arrived_ref, *side_refs, out_ref = refs[5:]
        raws = []
        for i in range(3):
            at = slice(i * width, (i + 1) * width)
            raw = dot_f32(tokens_ref[...], weight_refs[i][...])
            raw = raw + arrived_ref[:, at].astype(jnp.float32)
            raws.append(raw + joined_rows(side_refs, at).astype(jnp.float32))
        if attend_camera:
            row_cam = lax.broadcasted_iota(jnp.int32, (rows, rows), 0) // TOK_CAM
            col_cam = lax.broadcasted_iota(jnp.int32, (rows, rows), 1) // TOK_CAM
            same = row_cam == col_cam
        for h in range(heads):
            at = slice(h * HEAD_DIM, (h + 1) * HEAD_DIM)
            query = unit_norm(raws[0][:, at], scale_refs[0][:, at])
            key = unit_norm(raws[1][:, at], scale_refs[1][:, at])
            value = raws[2][:, at].astype(jnp.bfloat16)
            if attend_camera:
                out_ref[:, at] = softmax_blend(query, key, value, same)
            else:
                out_ref[:, at] = query
                out_ref[:, width + h * HEAD_DIM : width + (h + 1) * HEAD_DIM] = key
                out_ref[:, 2 * width + h * HEAD_DIM : 2 * width + (h + 1) * HEAD_DIM] = value

    weight_spec = pl.BlockSpec((depth, width), lambda s, pos: (0, mine_of(pos)))
    scale_spec = pl.BlockSpec((1, width), lambda s, pos: (0, mine_of(pos)))
    return run(
        kernel,
        (1,),
        (tokens, *weights, *scales, arrived, *from_side),
        (
            whole(tokens),
            *[weight_spec] * 3,
            *[scale_spec] * 2,
            pl.BlockSpec((rows, 3 * width), lambda s, pos: (0, pos[1])),
            *[whole(piece) for piece in from_side],
        ),
        jax.ShapeDtypeStruct((rows, out_width), jnp.bfloat16),
        pl.BlockSpec((rows, out_width), lambda s, pos: (0, 0)),
    )


def contract(run, parts, weight, sub, first=0, start=None):
    rows = sum(piece.shape[0] for piece in parts[0])
    width = parts[0][0].shape[1]
    count, pieces = len(parts), len(parts[0])
    out_width = weight.shape[1]
    block = width // sub

    def kernel(pos, weight_ref, *refs):
        out_ref = refs[-1]
        step = pl.program_id(0)
        for i in range(count):

            @pl.when(step // sub == i)
            def _(i=i):
                part = joined_rows(refs[i * pieces : (i + 1) * pieces])
                term = dot_f32(part, weight_ref[...])
                if i > 0:
                    out_ref[...] += term
                elif sub == 1:
                    out_ref[...] = term if start is None else term + refs[-2][...]
                else:

                    @pl.when(step == 0)
                    def _():
                        out_ref[...] = term if start is None else term + refs[-2][...]

                    @pl.when(step > 0)
                    def _():
                        out_ref[...] += term

    def weight_block(s, pos):
        i = s // sub + first
        return (2 * (pos[0] ^ (i & 1)) + (pos[1] ^ (i >> 1))) * sub + s % sub, 0

    def part_spec(i):
        return pl.BlockSpec(
            (rows // pieces, block), lambda s, pos: (0, jnp.clip(s - i * sub, 0, sub - 1))
        )

    operands = [weight, *[piece for part in parts for piece in part]]
    in_specs = [pl.BlockSpec((block, out_width), weight_block)]
    in_specs += [part_spec(i) for i in range(count) for _ in range(pieces)]
    if start is not None:
        operands.append(start)
        in_specs.append(whole(start))
    return run(
        kernel,
        (count * sub,),
        operands,
        in_specs,
        jax.ShapeDtypeStruct((rows, out_width), jnp.float32),
        pl.BlockSpec((rows, out_width), lambda s, pos: (0, 0)),
    )


def join_blend(run, parts, kept, from_side, scales):
    rows = parts.shape[0] + kept.shape[0]
    heads = parts.shape[1] // 3 // HEAD_DIM

    def kernel(pos, *refs):
        part_refs, kept_refs, side_refs = refs[:3], refs[3:6], refs[6:9]
        *scale_refs, out_ref = refs[9:]
        raws = [k[...] + s[...].astype(jnp.float32) for k, s in zip(kept_refs, side_refs)]
        late = [unit_norm(raws[i], scale_refs[i][...]) for i in range(2)]
        late.append(raws[2].astype(jnp.bfloat16))
        query, key, value = (
            jnp.concatenate((part_refs[i][...], late[i])) for i in range(3)
        )
        out_ref[...] = softmax_blend(query, key, value)

    def specs(array):
        return [
            pl.BlockSpec((array.shape[0], HEAD_DIM), lambda h, pos, i=i: (0, i * heads + h))
            for i in range(3)
        ]

    scale_spec = pl.BlockSpec((1, HEAD_DIM), lambda h, pos: (0, mine_of(pos) * heads + h))
    return run(
        kernel,
        (heads,),
        (*[parts] * 3, *[kept] * 3, *[from_side] * 3, *scales),
        (*specs(parts), *specs(kept), *specs(from_side), *[scale_spec] * 2),
        jax.ShapeDtypeStruct((rows, heads * HEAD_DIM), jnp.bfloat16),
        pl.BlockSpec((rows, HEAD_DIM), lambda h, pos: (0, h)),
    )


def moment_pair(values):
    return jnp.stack((jnp.sum(values, 1), jnp.sum(values * values, 1)))


def moment_flips(pair):
    return pair, flip(pair, 1), flip(pair, 2), flip(pair, 3)


def moment_sum(pairs):
    return (pairs[0] + pairs[1]) + (pairs[2] + pairs[3])


def sent(array, shift):
    return row_shift(array.astype(jnp.bfloat16), shift)


def sent_on(before, after):
    half = before.shape[0] // 2
    return sent(before[:half], 1), sent(after[half:], -1)


def moment_shards(total):
    return total, row_shift(total, 1), row_shift(total, -1), row_shift(total, 2)


def normed_shards(shards, scales, totals):
    return jnp.concatenate(
        [normalize(x.astype(jnp.float32), scales, m) for x, m in zip(shards, totals)]
    )


def sync(*values):
    return lax.optimization_barrier(values)


def scatter_rows_long(terms):
    own, before, after, away = jnp.split(terms, 4)
    half = own.shape[0] // 2

    def send(array, shift):
        return row_shift(array.astype(jnp.bfloat16), shift).astype(jnp.float32)

    to_after = send(away[:half], 1)
    to_before = send(away[half:], -1)
    from_before = jnp.concatenate((send(after[:half] + to_after, 1), send(after[half:], 1)))
    from_after = jnp.concatenate((send(before[:half], -1), send(before[half:] + to_before, -1)))
    return own + from_before + from_after


def fast_body(
    camera_tokens,
    norm_gain,
    query_weight,
    key_weight,
    value_weight,
    query_gain,
    key_gain,
    out_weight,
    up_weight,
    up_bias,
    down_weight,
    down_bias,
    join_gain,
    join_query,
    join_key,
    join_value,
    join_query_gain,
    join_key_gain,
    join_out,
):
    half = TOK_CAM
    index = lax.axis_index("cols")
    run = Runner(jnp.stack((index & 1, index >> 1)).astype(jnp.int32))
    head_width = query_weight.shape[1] // 4
    unit_width = up_weight.shape[1] // 4
    sub = 3 if unit_width % (3 * 256) == 0 else 1
    heads_in = (query_weight, key_weight, value_weight)
    join_in = (join_query, join_key, join_value)
    scales = (query_gain[None], key_gain[None])
    join_scales = (join_query_gain[None], join_key_gain[None])
    bias = up_bias[None]

    def heads_send(tokens, weights):
        return project_send(run, tokens, weights, head_width, 1)

    def heads_across(tokens, weights, arrived, pieces=1):
        return project_across(run, tokens, weights, head_width, 1, arrived, pieces)

    def heads_out(parts, first=0, start=None):
        return contract(run, [(part,) for part in parts], out_weight, 1, first, start)

    def units_down(parts, first, start):
        return contract(run, parts, down_weight, 2, first, start)

    def units_send(tokens):
        return project_send(run, tokens, (up_weight,), unit_width, sub)

    def units_across(tokens, arrived, pieces):
        return project_across(run, tokens, (up_weight,), unit_width, sub, arrived, pieces)

    def units_end(tokens, arrived, side, at=0):
        return project_hidden(run, tokens, up_weight, bias, unit_width, sub, arrived, side, at)

    def layer_end(start, own, *arrived):
        total = own
        for term in arrived:
            total = total + term.astype(jnp.float32)
        return (start + total + down_bias).astype(jnp.bfloat16)

    start_f32 = camera_tokens.astype(jnp.float32)
    own_a, own_b = camera_tokens[:half], camera_tokens[half:]
    pairs = moment_flips(moment_pair(start_f32))
    own_a, own_b, a_before, a_after, *pairs = sync(
        own_a, own_b, sent(own_a, 1), sent(own_a, -1), *pairs
    )

    totals = moment_shards(moment_sum(pairs))
    own_a, own_b, a_before, a_after, a_away0, a_away1, *totals = sync(
        own_a, own_b, a_before, a_after, *sent_on(a_before, a_after), *totals
    )
    a_away = jnp.concatenate((a_away0, a_away1))
    totals_a = [total[:, :half] for total in totals]
    totals_b = [total[:, half:] for total in totals]

    b_before = sent(own_b, 1)
    tok_a = normed_shards((own_a, a_before, a_after, a_away), norm_gain, totals_a)
    qs_a = heads_send(tok_a, heads_in)
    tok_a, own_b, b_before, qs_a = sync(tok_a, own_b, b_before, qs_a)

    b_after, qc_a = sent(own_b, -1), core_swap(qs_a)
    qx_a = heads_across(tok_a, heads_in, qc_a, 2)
    tok_a, own_b, b_before, b_after, qc_a, qx_a0, qx_a1 = sync(
        tok_a, own_b, b_before, b_after, qc_a, *qx_a
    )

    qy_a0 = y_swap(qx_a0)
    us_a = units_send(tok_a)
    tok_a, own_b, b_before, b_after, qc_a, us_a, qy_a0, qx_a1 = sync(
        tok_a, own_b, b_before, b_after, qc_a, us_a, qy_a0, qx_a1
    )

    uc_a, qy_a1, b_away0, b_away1 = (
        core_swap(us_a), y_swap(qx_a1), *sent_on(b_before, b_after)
    )
    (ux_a,) = units_across(tok_a, uc_a, 1)
    tok_a, qc_a, uc_a, ux_a, qy_a0, qy_a1, own_b, b_before, b_after, b_away0, b_away1 = sync(
        tok_a, qc_a, uc_a, ux_a, qy_a0, qy_a1, own_b, b_before, b_after, b_away0, b_away1
    )
    b_away = jnp.concatenate((b_away0, b_away1))

    uy_a = y_swap(ux_a)
    tok_b = normed_shards((own_b, b_before, b_after, b_away), norm_gain, totals_b)
    qs_b = heads_send(tok_b, heads_in)
    us_b = units_send(tok_b)
    at_a = project_heads(run, tok_a, heads_in, scales, head_width, qc_a, (qy_a0, qy_a1), True)
    tok_a, tok_b, qs_b, us_b, at_a, uc_a, uy_a = sync(
        tok_a, tok_b, qs_b, us_b, at_a, uc_a, uy_a
    )

    at_ya, at_ca, qc_b, uc_b = y_swap(at_a), core_swap(at_a), core_swap(qs_b), core_swap(us_b)
    hd_a = units_end(tok_a, uc_a, uy_a)
    tok_b, at_a, at_ya, at_ca, qc_b, uc_b, hd_a = sync(
        tok_b, at_a, at_ya, at_ca, qc_b, uc_b, hd_a
    )

    hd_ya, hd_ca, at_fa = y_swap(hd_a), core_swap(hd_a), core_swap(at_ya)
    (qx_b,) = heads_across(tok_b, heads_in, qc_b)
    ux_b = units_across(tok_b, uc_b, 2)
    mixed_a = units_down(((hd_a,),), 0, heads_out((at_a, at_ca, at_ya)))
    tok_b, at_fa, hd_ya, hd_ca, qc_b, uc_b, qx_b, mixed_a, *ux_b = sync(
        tok_b, at_fa, hd_ya, hd_ca, qc_b, uc_b, qx_b, mixed_a, *ux_b
    )

    qy_b, hd_fa = y_swap(qx_b), core_swap(hd_ya)
    mixed_a = heads_out((at_fa,), 3, mixed_a)
    mixed_a = units_down(((hd_ca,), (hd_ya,), (hd_fa,)), 1, mixed_a)
    tok_b, mixed_a, qc_b, qy_b, uc_b, ux_b0, ux_b1 = sync(
        tok_b, mixed_a, qc_b, qy_b, uc_b, *ux_b
    )

    uy_b0 = y_swap(ux_b0)
    mine_a, before_a, after_a, away_a = jnp.split(mixed_a, 4)
    from_before, from_after = sent(after_a, 1), sent(before_a, -1)
    at_b = project_heads(run, tok_b, heads_in, scales, head_width, qc_b, (qy_b,), True)
    at_yb = y_swap(at_b)
    tok_b, uc_b, uy_b0, ux_b1, at_b, at_yb, mine_a, away_a, from_before, from_after = sync(
        tok_b, uc_b, uy_b0, ux_b1, at_b, at_yb, mine_a, away_a.astype(jnp.bfloat16),
        from_before, from_after,
    )

    uy_b1, from_away, at_cb, at_fb = (
        y_swap(ux_b1), sent(away_a, 2), core_swap(at_b), core_swap(at_yb)
    )
    hd_b0 = units_end(tok_b, uc_b, uy_b0)
    mixed_b = heads_out((at_b, at_cb, at_yb, at_fb))
    tok_b, uc_b, uy_b1, hd_b0, mixed_b, mine_a, *arrived = sync(
        tok_b, uc_b, uy_b1, hd_b0, mixed_b, mine_a, from_before, from_after, from_away
    )

    hd_yb0, hd_cb0 = y_swap(hd_b0), core_swap(hd_b0)
    layer_a = layer_end(start_f32[:half], mine_a, *arrived)
    pairs = moment_flips(moment_pair(layer_a.astype(jnp.float32)))
    hd_b1 = units_end(tok_b, uc_b, uy_b1, 1)
    hd_b0, hd_b1, hd_yb0, hd_cb0, mixed_b, layer_a, *pairs = sync(
        hd_b0, hd_b1, hd_yb0, hd_cb0, mixed_b, layer_a, *pairs
    )

    hd_yb1, hd_cb1, hd_fb0 = y_swap(hd_b1), core_swap(hd_b1), core_swap(hd_yb0)
    join_a = normalize(layer_a.astype(jnp.float32), join_gain, moment_sum(pairs))
    ja_before, ja_after = sent(join_a, 1), sent(join_a, -1)
    mixed_b = units_down(((hd_b0, hd_b1),), 0, mixed_b)
    hd_cb0, hd_cb1, hd_yb0, hd_yb1, hd_fb0, mixed_b, layer_a, join_a, ja_before, ja_after = sync(
        hd_cb0, hd_cb1, hd_yb0, hd_yb1, hd_fb0, mixed_b, layer_a, join_a, ja_before, ja_after
    )

    hd_fb1 = core_swap(hd_yb1)
    mixed_b = units_down(((hd_cb0, hd_cb1),), 1, mixed_b)
    hd_yb0, hd_yb1, hd_fb0, hd_fb1, mixed_b, join_a, ja_before, ja_after = sync(
        hd_yb0, hd_yb1, hd_fb0, hd_fb1, mixed_b, join_a, ja_before, ja_after
    )

    ja_away0, ja_away1 = sent_on(ja_before, ja_after)
    mixed_b = units_down(((hd_yb0, hd_yb1), (hd_fb0, hd_fb1)), 2, mixed_b)
    mixed_b, join_a, ja_before, ja_after, ja_away0, ja_away1 = sync(
        mixed_b, join_a, ja_before, ja_after, ja_away0, ja_away1
    )

    mine_b, before_b, after_b, away_b = jnp.split(mixed_b, 4)
    part = half // 2
    to_after, to_before = sent(away_b[:part], 1), sent(away_b[part:], -1)
    mine_b, before_b, after_b, to_after, to_before, join_a, *shards = sync(
        mine_b, before_b, after_b, to_after, to_before, join_a,
        ja_before, ja_after, ja_away0, ja_away1,
    )

    after_b = jnp.concatenate((after_b[:part] + to_after.astype(jnp.float32), after_b[part:]))
    before_b = jnp.concatenate((before_b[:part], before_b[part:] + to_before.astype(jnp.float32)))
    from_before, from_after = sent(after_b, 1), sent(before_b, -1)
    tok_ja = jnp.concatenate((join_a, *shards))
    js_a = heads_send(tok_ja, join_in)
    jc_a = core_swap(js_a)
    tok_ja, jc_a, mine_b, *arrived = sync(tok_ja, jc_a, mine_b, from_before, from_after)

    layer_b = layer_end(start_f32[half:], mine_b, *arrived)
    totals = moment_shards(moment_sum(moment_flips(moment_pair(layer_b.astype(jnp.float32)))))
    jb_before, jb_after = sent(layer_b, 1), sent(layer_b, -1)
    jx_a = heads_across(tok_ja, join_in, jc_a, 2)
    tok_ja, jc_a, jx_a0, jx_a1, layer_b, jb_before, jb_after, *totals = sync(
        tok_ja, jc_a, *jx_a, layer_b, jb_before, jb_after, *totals
    )

    jb_away0, jb_away1 = sent_on(jb_before, jb_after)
    jy_a0 = y_swap(jx_a0)
    tok_ja, jc_a, jy_a0, jx_a1, layer_b, jb_before, jb_after, jb_away0, jb_away1, *totals = sync(
        tok_ja, jc_a, jy_a0, jx_a1, layer_b, jb_before, jb_after, jb_away0, jb_away1, *totals
    )

    jy_a1 = y_swap(jx_a1)
    jb_away = jnp.concatenate((jb_away0, jb_away1))
    tok_jb = normed_shards((layer_b, jb_before, jb_after, jb_away), join_gain, totals)
    jc_b = core_swap(heads_send(tok_jb, join_in))
    (jx_b,) = heads_across(tok_jb, join_in, jc_b)
    tok_ja, jc_a, jy_a0, jy_a1, tok_jb, jc_b, jx_b = sync(
        tok_ja, jc_a, jy_a0, jy_a1, tok_jb, jc_b, jx_b
    )

    jy_b = y_swap(jx_b)
    parts_a = project_heads(
        run, tok_ja, join_in, join_scales, head_width, jc_a, (jy_a0, jy_a1), False
    )
    kept_b = project_keep(run, tok_jb, join_in, head_width, jc_b)
    jy_b, parts_a, kept_b = sync(jy_b, parts_a, kept_b)

    joined = join_blend(run, parts_a, kept_b, jy_b, join_scales)
    joined = joined.reshape(2, 4, half, head_width).swapaxes(0, 1).reshape(8 * half, head_width)
    jo_y, jo_c = y_swap(joined), core_swap(joined)
    jo_f = core_swap(jo_y)
    result = contract(run, ((joined,), (jo_c,)), join_out, 1)
    result = contract(run, ((jo_y,), (jo_f,)), join_out, 1, 2, result)
    summed = scatter_rows_long(result)
    layer_own = jnp.concatenate((layer_a, layer_b))
    return (layer_own.astype(jnp.float32) + summed).astype(jnp.bfloat16)


def layer(*arrays):
    own_rows, heads_width = arrays[0].shape[0], arrays[2].shape[1]
    fits = lax.axis_size("cols") == 4 and lax.axis_size("rows") == 4
    fits = fits and own_rows == 2 * TOK_CAM and heads_width % (4 * HEAD_DIM) == 0
    return (fast_body if fits else generic_body)(*arrays)


def solution(mesh):
    in_specs = (
        P(("groups", "rows"), "cols"),
        P("cols"),
        P("cols", "rows"),
        P("cols", "rows"),
        P("cols", "rows"),
        P("rows"),
        P("rows"),
        P("rows", "cols"),
        P("cols", "rows"),
        P("rows"),
        P("rows", "cols"),
        P("cols"),
        P("cols"),
        P("cols", "rows"),
        P("cols", "rows"),
        P("cols", "rows"),
        P("rows"),
        P("rows"),
        P("rows", "cols"),
    )
    out_specs = P(("groups", "rows"), "cols")
    return jax.shard_map(layer, mesh=mesh, in_specs=in_specs, out_specs=out_specs, check_vma=False)
```

```python
import math

import jax
import jax.numpy as jnp
from jax import lax
from jax.experimental import pallas as pl
from jax.experimental.pallas import tpu as pltpu
from jax.sharding import PartitionSpec as P

HEAD_DIM = 128
TOK_CAM = 64
D = 6144


EPS = 1e-06


def partner_2(array, axis, bit):
    return lax.ppermute(array, axis, [(i, i ^ 1 << bit) for i in range(lax.axis_size(axis))])


def normalize(values, scales, moments):
    row_mean = moments[0] / D
    row_var = moments[1] / D - row_mean * row_mean
    return ((values - row_mean[:, None]) * lax.rsqrt(row_var[:, None] + EPS) * scales).astype(
        jnp.bfloat16
    )


def shard_moments(values):
    return lax.psum((jnp.sum(values, 1), jnp.sum(values * values, 1)), "cols")


def head_norm(values, scales):
    row_count = values.shape[0]
    grouped = values.reshape(row_count, -1, HEAD_DIM)
    row_mean = jnp.mean(grouped, -1, keepdims=True)
    row_var = jnp.mean(grouped * grouped, -1, keepdims=True) - row_mean * row_mean
    normed = (grouped - row_mean) * lax.rsqrt(row_var + EPS)
    return (normed.reshape(row_count, -1) * scales).astype(jnp.bfloat16)


def attend(queries, key_rows, val_rows):
    inv_root = 1.0 / math.sqrt(HEAD_DIM)
    scores = (
        jnp.einsum("bqhd,bkhd->bhqk", queries, key_rows, preferred_element_type=jnp.float32)
        * inv_root
    )
    row_max = jnp.max(scores, -1, keepdims=True)
    weights = jnp.exp(scores - row_max)
    row_sum = jnp.sum(weights, -1)
    blended = jnp.einsum(
        "bhqk,bkhd->bqhd",
        weights.astype(jnp.bfloat16),
        val_rows,
        preferred_element_type=jnp.float32,
    )
    return blended / jnp.transpose(row_sum, (0, 2, 1))[..., None]


def to_heads(matrix, blocks):
    return matrix.reshape(blocks, -1, matrix.shape[1] // HEAD_DIM, HEAD_DIM)


def camera_attention(queries, key_rows, val_rows):
    local_rows = queries.shape[0]
    if local_rows >= TOK_CAM:
        blocks = local_rows // TOK_CAM
        result = attend(
            to_heads(queries, blocks), to_heads(key_rows, blocks), to_heads(val_rows, blocks)
        )
    else:
        cam_span = TOK_CAM // local_rows
        position = lax.axis_index("cols")
        key_value = jnp.stack((key_rows, val_rows))
        for which_bit in range(cam_span.bit_length() - 1):
            partner = partner_2(key_value, "cols", which_bit)
            is_lower = position >> which_bit & 1 == 0
            key_value = jnp.where(
                is_lower,
                jnp.concatenate((key_value, partner), 1),
                jnp.concatenate((partner, key_value), 1),
            )
        result = attend(to_heads(queries, 1), to_heads(key_value[0], 1), to_heads(key_value[1], 1))
    return result.reshape(local_rows, -1).astype(jnp.bfloat16)


def generic_body(
    camera_tokens,
    norm_gain,
    query_weight,
    key_weight,
    value_weight,
    query_gain,
    key_gain,
    out_weight,
    up_weight,
    up_bias,
    down_weight,
    down_bias,
    join_gain,
    join_query,
    join_key,
    join_value,
    join_query_gain,
    join_key_gain,
    join_out,
):
    own_rows = camera_tokens.shape[0]
    all_rows = own_rows * lax.axis_size("rows")
    col_rows = all_rows // lax.axis_size("cols")
    attn_width = query_weight.shape[1]
    start_f32 = camera_tokens.astype(jnp.float32)
    normed_all = lax.all_gather(
        normalize(start_f32, norm_gain, shard_moments(start_f32)), "rows", axis=0, tiled=True
    )
    joint_weight = jnp.concatenate((query_weight, key_weight, value_weight, up_weight), 1)
    joint = lax.psum_scatter(
        jnp.dot(normed_all, joint_weight, preferred_element_type=jnp.float32),
        "cols",
        scatter_dimension=0,
        tiled=True,
    )
    up_sum = joint[:, 3 * attn_width :]
    hidden = jax.nn.gelu(up_sum + up_bias, approximate=False).astype(jnp.bfloat16)
    attended = camera_attention(
        head_norm(joint[:, :attn_width], query_gain),
        head_norm(joint[:, attn_width : 2 * attn_width], key_gain),
        joint[:, 2 * attn_width : 3 * attn_width].astype(jnp.bfloat16),
    )
    attn_all, hidden_all = (
        lax.all_gather(attended, "cols", axis=0, tiled=True),
        lax.all_gather(hidden, "cols", axis=0, tiled=True),
    )
    mixed = lax.psum_scatter(
        jnp.dot(attn_all, out_weight, preferred_element_type=jnp.float32)
        + jnp.dot(hidden_all, down_weight, preferred_element_type=jnp.float32),
        "rows",
        scatter_dimension=0,
        tiled=True,
    )
    layer_own = (start_f32 + mixed + down_bias).astype(jnp.bfloat16)
    layer_f32 = layer_own.astype(jnp.float32)
    join_in = lax.all_gather(
        normalize(layer_f32, join_gain, shard_moments(layer_f32)), "rows", axis=0, tiled=True
    )
    join_weight = jnp.concatenate((join_query, join_key, join_value), 1)
    join_joint = lax.psum_scatter(
        jnp.dot(join_in, join_weight, preferred_element_type=jnp.float32),
        "cols",
        scatter_dimension=0,
        tiled=True,
    )
    join_q = head_norm(join_joint[:, :attn_width], join_query_gain)
    join_k = head_norm(join_joint[:, attn_width : 2 * attn_width], join_key_gain)
    join_v = join_joint[:, 2 * attn_width :].astype(jnp.bfloat16)
    heads_here = attn_width // HEAD_DIM
    query_heads = join_q.reshape(col_rows, heads_here, HEAD_DIM)
    inv_root = 1.0 / math.sqrt(HEAD_DIM)
    run_max = jnp.full((heads_here, col_rows), -jnp.inf, jnp.float32)
    run_sum = jnp.zeros((heads_here, col_rows), jnp.float32)
    accum = jnp.zeros((col_rows, heads_here, HEAD_DIM), jnp.float32)
    key_part = lax.all_gather(join_k, "cols", axis=0, tiled=True)
    val_part = lax.all_gather(join_v, "cols", axis=0, tiled=True)
    row_count = key_part.shape[0]
    key_heads = key_part.reshape(row_count, heads_here, HEAD_DIM)
    val_heads = val_part.reshape(row_count, heads_here, HEAD_DIM)
    scores = (
        jnp.einsum("qhd,khd->hqk", query_heads, key_heads, preferred_element_type=jnp.float32)
        * inv_root
    )
    new_max = jnp.max(scores, -1)
    factor = jnp.exp(run_max - new_max)
    weights = jnp.exp(scores - new_max[..., None])
    run_sum = run_sum * factor + jnp.sum(weights, -1)
    accum = accum * jnp.transpose(factor)[..., None] + jnp.einsum(
        "hqk,khd->qhd", weights.astype(jnp.bfloat16), val_heads, preferred_element_type=jnp.float32
    )
    run_max, run_sum, accum = (new_max, run_sum, accum)
    joined_attn = (
        (accum / jnp.transpose(run_sum)[..., None])
        .reshape(col_rows, attn_width)
        .astype(jnp.bfloat16)
    )
    joined_all = lax.all_gather(joined_attn, "cols", axis=0, tiled=True)
    result = lax.psum_scatter(
        jnp.dot(joined_all, join_out, preferred_element_type=jnp.float32),
        "rows",
        scatter_dimension=0,
        tiled=True,
    )
    return (layer_own.astype(jnp.float32) + result).astype(jnp.bfloat16)


VMEM_BYTES = 48 * 1024 * 1024


def flip(array, mask):
    size = lax.axis_size("cols")
    return lax.ppermute(array, "cols", [(i, i ^ mask) for i in range(size)])


def core_swap(array):
    return flip(array, 1)


def y_swap(array):
    return flip(array, 2)


def row_shift(array, shift):
    size = lax.axis_size("rows")
    return lax.ppermute(array, "rows", [(i, (i + shift) % size) for i in range(size)])


class Runner:
    def __init__(self, position):
        self.position = position

    def __call__(self, kernel, grid, operands, in_specs, out_shape, out_spec):
        return pl.pallas_call(
            kernel,
            out_shape=out_shape,
            grid_spec=pltpu.PrefetchScalarGridSpec(
                num_scalar_prefetch=1, grid=grid, in_specs=list(in_specs), out_specs=out_spec
            ),
            compiler_params=pltpu.CompilerParams(vmem_limit_bytes=VMEM_BYTES),
            cost_estimate=pl.CostEstimate(flops=1, bytes_accessed=1, transcendentals=0),
        )(self.position, *operands)


def joined_rows(refs, at=slice(None)):
    return jnp.concatenate([ref[:, at] for ref in refs])


def store_rows(refs, at, values):
    piece = values.shape[0] // len(refs)
    for j, ref in enumerate(refs):
        ref[:, at] = values[j * piece : (j + 1) * piece].astype(ref.dtype)


def whole(array):
    return pl.BlockSpec(array.shape, lambda s, pos: (0,) * array.ndim)


def mine_of(pos):
    return 2 * pos[0] + pos[1]


def across_of(pos):
    return 2 * pos[0] + 1 - pos[1]


def dot_f32(a, b):
    return jnp.dot(a, b, preferred_element_type=jnp.float32)


def project_send(run, tokens, weights, width, sub):
    rows, depth = tokens.shape
    block = width // sub
    wide = len(weights) * block

    def kernel(pos, tokens_ref, *refs):
        for i in range(len(weights)):
            refs[-1][:, i * block : (i + 1) * block] = dot_f32(
                tokens_ref[...], refs[i][...]
            ).astype(jnp.bfloat16)

    spec = pl.BlockSpec((depth, block), lambda s, pos: (0, 2 * (1 - pos[0]) * sub + s))
    return run(
        kernel,
        (2 * sub,),
        (tokens, *weights),
        (whole(tokens), *[spec] * len(weights)),
        jax.ShapeDtypeStruct((rows, 2 * sub * wide), jnp.bfloat16),
        pl.BlockSpec((rows, wide), lambda s, pos: (0, s)),
    )


def project_across(run, tokens, weights, width, sub, arrived, pieces=1):
    rows, depth = tokens.shape
    block = width // sub
    wide = len(weights) * block

    def kernel(pos, tokens_ref, *refs):
        for i in range(len(weights)):
            at = slice(i * block, (i + 1) * block)
            part = dot_f32(tokens_ref[...], refs[i][...])
            part = part + refs[len(weights)][:, at].astype(jnp.float32)
            store_rows(refs[len(weights) + 1 :], at, part)

    spec = pl.BlockSpec((depth, block), lambda s, pos: (0, across_of(pos) * sub + s))
    return run(
        kernel,
        (sub,),
        (tokens, *weights, arrived),
        (
            whole(tokens),
            *[spec] * len(weights),
            pl.BlockSpec((rows, wide), lambda s, pos: (0, (1 - pos[1]) * sub + s)),
        ),
        (jax.ShapeDtypeStruct((rows // pieces, sub * wide), jnp.bfloat16),) * pieces,
        (pl.BlockSpec((rows // pieces, wide), lambda s, pos: (0, s)),) * pieces,
    )


def project_hidden(run, tokens, weight, bias, width, sub, arrived, from_side, at=0):
    depth = tokens.shape[1]
    rows = from_side.shape[0]
    block = width // sub

    def kernel(pos, tokens_ref, weight_ref, bias_ref, arrived_ref, side_ref, out_ref):
        total = dot_f32(tokens_ref[...], weight_ref[...])
        total = total + arrived_ref[...].astype(jnp.float32) + side_ref[...].astype(jnp.float32)
        total = total + bias_ref[...]
        out_ref[...] = (total * (1.0 + lax.erf(total * math.sqrt(0.5))) * 0.5).astype(jnp.bfloat16)

    return run(
        kernel,
        (sub,),
        (tokens, weight, bias, arrived, from_side),
        (
            pl.BlockSpec((rows, depth), lambda s, pos: (at, 0)),
            pl.BlockSpec((depth, block), lambda s, pos: (0, mine_of(pos) * sub + s)),
            pl.BlockSpec((1, block), lambda s, pos: (0, mine_of(pos) * sub + s)),
            pl.BlockSpec((rows, block), lambda s, pos: (at, pos[1] * sub + s)),
            pl.BlockSpec((rows, block), lambda s, pos: (0, s)),
        ),
        jax.ShapeDtypeStruct((rows, width), jnp.bfloat16),
        pl.BlockSpec((rows, block), lambda s, pos: (0, s)),
    )


def project_keep(run, tokens, weights, width, arrived):
    rows, depth = tokens.shape
    wide = len(weights) * width

    def kernel(pos, tokens_ref, *refs):
        arrived_ref, out_ref = refs[len(weights) :]
        for i in range(len(weights)):
            at = slice(i * width, (i + 1) * width)
            part = dot_f32(tokens_ref[...], refs[i][...])
            out_ref[:, at] = part + arrived_ref[:, at].astype(jnp.float32)

    spec = pl.BlockSpec((depth, width), lambda s, pos: (0, mine_of(pos)))
    return run(
        kernel,
        (1,),
        (tokens, *weights, arrived),
        (
            whole(tokens),
            *[spec] * len(weights),
            pl.BlockSpec((rows, wide), lambda s, pos: (0, pos[1])),
        ),
        jax.ShapeDtypeStruct((rows, wide), jnp.float32),
        pl.BlockSpec((rows, wide), lambda s, pos: (0, 0)),
    )


def unit_norm(values, scales):
    row_mean = jnp.mean(values, -1, keepdims=True)
    row_var = jnp.mean(values * values, -1, keepdims=True) - row_mean * row_mean
    return ((values - row_mean) * lax.rsqrt(row_var + EPS) * scales).astype(jnp.bfloat16)


def softmax_blend(query, key, value, keep=None):
    scores = lax.dot_general(
        query, key, (((1,), (1,)), ((), ())), preferred_element_type=jnp.float32
    ) * (1.0 / math.sqrt(HEAD_DIM))
    if keep is not None:
        scores = jnp.where(keep, scores, -jnp.inf)
    weights = jnp.exp(scores - jnp.max(scores, -1, keepdims=True))
    row_sum = jnp.sum(weights, -1, keepdims=True)
    blended = dot_f32(weights.astype(jnp.bfloat16), value)
    return (blended / row_sum).astype(jnp.bfloat16)


def project_heads(run, tokens, weights, scales, width, arrived, from_side, attend_camera):
    rows, depth = tokens.shape
    heads = width // HEAD_DIM
    out_width = width if attend_camera else 3 * width

    def kernel(pos, tokens_ref, *refs):
        weight_refs, scale_refs = refs[:3], refs[3:5]
        arrived_ref, *side_refs, out_ref = refs[5:]
        raws = []
        for i in range(3):
            at = slice(i * width, (i + 1) * width)
            raw = dot_f32(tokens_ref[...], weight_refs[i][...])
            raw = raw + arrived_ref[:, at].astype(jnp.float32)
            raws.append(raw + joined_rows(side_refs, at).astype(jnp.float32))
        if attend_camera:
            row_cam = lax.broadcasted_iota(jnp.int32, (rows, rows), 0) // TOK_CAM
            col_cam = lax.broadcasted_iota(jnp.int32, (rows, rows), 1) // TOK_CAM
            same = row_cam == col_cam
        for h in range(heads):
            at = slice(h * HEAD_DIM, (h + 1) * HEAD_DIM)
            query = unit_norm(raws[0][:, at], scale_refs[0][:, at])
            key = unit_norm(raws[1][:, at], scale_refs[1][:, at])
            value = raws[2][:, at].astype(jnp.bfloat16)
            if attend_camera:
                out_ref[:, at] = softmax_blend(query, key, value, same)
            else:
                out_ref[:, at] = query
                out_ref[:, width + h * HEAD_DIM : width + (h + 1) * HEAD_DIM] = key
                out_ref[:, 2 * width + h * HEAD_DIM : 2 * width + (h + 1) * HEAD_DIM] = value

    weight_spec = pl.BlockSpec((depth, width), lambda s, pos: (0, mine_of(pos)))
    scale_spec = pl.BlockSpec((1, width), lambda s, pos: (0, mine_of(pos)))
    return run(
        kernel,
        (1,),
        (tokens, *weights, *scales, arrived, *from_side),
        (
            whole(tokens),
            *[weight_spec] * 3,
            *[scale_spec] * 2,
            pl.BlockSpec((rows, 3 * width), lambda s, pos: (0, pos[1])),
            *[whole(piece) for piece in from_side],
        ),
        jax.ShapeDtypeStruct((rows, out_width), jnp.bfloat16),
        pl.BlockSpec((rows, out_width), lambda s, pos: (0, 0)),
    )


def contract(run, parts, weight, sub, first=0, start=None):
    rows = sum(piece.shape[0] for piece in parts[0])
    width = parts[0][0].shape[1]
    count, pieces = len(parts), len(parts[0])
    out_width = weight.shape[1]
    block = width // sub

    def kernel(pos, weight_ref, *refs):
        out_ref = refs[-1]
        step = pl.program_id(0)
        for i in range(count):

            @pl.when(step // sub == i)
            def _(i=i):
                part = joined_rows(refs[i * pieces : (i + 1) * pieces])
                term = dot_f32(part, weight_ref[...])
                if i > 0:
                    out_ref[...] += term
                elif sub == 1:
                    out_ref[...] = term if start is None else term + refs[-2][...]
                else:

                    @pl.when(step == 0)
                    def _():
                        out_ref[...] = term if start is None else term + refs[-2][...]

                    @pl.when(step > 0)
                    def _():
                        out_ref[...] += term

    def weight_block(s, pos):
        i = s // sub + first
        return (2 * (pos[0] ^ (i & 1)) + (pos[1] ^ (i >> 1))) * sub + s % sub, 0

    def part_spec(i):
        return pl.BlockSpec(
            (rows // pieces, block), lambda s, pos: (0, jnp.clip(s - i * sub, 0, sub - 1))
        )

    operands = [weight, *[piece for part in parts for piece in part]]
    in_specs = [pl.BlockSpec((block, out_width), weight_block)]
    in_specs += [part_spec(i) for i in range(count) for _ in range(pieces)]
    if start is not None:
        operands.append(start)
        in_specs.append(whole(start))
    return run(
        kernel,
        (count * sub,),
        operands,
        in_specs,
        jax.ShapeDtypeStruct((rows, out_width), jnp.float32),
        pl.BlockSpec((rows, out_width), lambda s, pos: (0, 0)),
    )


def join_blend(run, parts, kept, from_side, scales):
    rows = parts.shape[0] + kept.shape[0]
    heads = parts.shape[1] // 3 // HEAD_DIM

    def kernel(pos, *refs):
        part_refs, kept_refs, side_refs = refs[:3], refs[3:6], refs[6:9]
        *scale_refs, out_ref = refs[9:]
        raws = [k[...] + s[...].astype(jnp.float32) for k, s in zip(kept_refs, side_refs)]
        late = [unit_norm(raws[i], scale_refs[i][...]) for i in range(2)]
        late.append(raws[2].astype(jnp.bfloat16))
        query, key, value = (
            jnp.concatenate((part_refs[i][...], late[i])) for i in range(3)
        )
        out_ref[...] = softmax_blend(query, key, value)

    def specs(array):
        return [
            pl.BlockSpec((array.shape[0], HEAD_DIM), lambda h, pos, i=i: (0, i * heads + h))
            for i in range(3)
        ]

    scale_spec = pl.BlockSpec((1, HEAD_DIM), lambda h, pos: (0, mine_of(pos) * heads + h))
    return run(
        kernel,
        (heads,),
        (*[parts] * 3, *[kept] * 3, *[from_side] * 3, *scales),
        (*specs(parts), *specs(kept), *specs(from_side), *[scale_spec] * 2),
        jax.ShapeDtypeStruct((rows, heads * HEAD_DIM), jnp.bfloat16),
        pl.BlockSpec((rows, HEAD_DIM), lambda h, pos: (0, h)),
    )


def moment_pair(values):
    return jnp.stack((jnp.sum(values, 1), jnp.sum(values * values, 1)))


def moment_flips(pair):
    return pair, flip(pair, 1), flip(pair, 2), flip(pair, 3)


def moment_sum(pairs):
    return (pairs[0] + pairs[1]) + (pairs[2] + pairs[3])


def sent(array, shift):
    return row_shift(array.astype(jnp.bfloat16), shift)


def moment_shards(total):
    return total, row_shift(total, 1), row_shift(total, -1), row_shift(total, 2)


def normed_shards(shards, scales, totals):
    return jnp.concatenate(
        [normalize(x.astype(jnp.float32), scales, m) for x, m in zip(shards, totals)]
    )


def sync(*values):
    return lax.optimization_barrier(values)


def scatter_rows(terms):
    own, before, after, away = jnp.split(terms, 4)
    to_after, from_after = sent(away, 1), sent(before, -1)
    from_before = sent(after + to_after.astype(jnp.float32), 1)
    return own + from_before.astype(jnp.float32) + from_after.astype(jnp.float32)


def fast_body(
    camera_tokens,
    norm_gain,
    query_weight,
    key_weight,
    value_weight,
    query_gain,
    key_gain,
    out_weight,
    up_weight,
    up_bias,
    down_weight,
    down_bias,
    join_gain,
    join_query,
    join_key,
    join_value,
    join_query_gain,
    join_key_gain,
    join_out,
):
    half = TOK_CAM
    index = lax.axis_index("cols")
    run = Runner(jnp.stack((index & 1, index >> 1)).astype(jnp.int32))
    head_width = query_weight.shape[1] // 4
    unit_width = up_weight.shape[1] // 4
    sub = 3 if unit_width % (3 * 256) == 0 else 1
    heads_in = (query_weight, key_weight, value_weight)
    join_in = (join_query, join_key, join_value)
    scales = (query_gain[None], key_gain[None])
    join_scales = (join_query_gain[None], join_key_gain[None])
    bias = up_bias[None]

    def heads_send(tokens, weights):
        return project_send(run, tokens, weights, head_width, 1)

    def heads_across(tokens, weights, arrived, pieces=1):
        return project_across(run, tokens, weights, head_width, 1, arrived, pieces)

    def heads_out(parts, first=0, start=None):
        return contract(run, [(part,) for part in parts], out_weight, 1, first, start)

    def units_down(parts, first, start):
        return contract(run, parts, down_weight, 2, first, start)

    def units_send(tokens):
        return project_send(run, tokens, (up_weight,), unit_width, sub)

    def units_across(tokens, arrived, pieces):
        return project_across(run, tokens, (up_weight,), unit_width, sub, arrived, pieces)

    def units_end(tokens, arrived, side, at=0):
        return project_hidden(run, tokens, up_weight, bias, unit_width, sub, arrived, side, at)

    def layer_end(start, own, *arrived):
        total = own
        for term in arrived:
            total = total + term.astype(jnp.float32)
        return (start + total + down_bias).astype(jnp.bfloat16)

    start_f32 = camera_tokens.astype(jnp.float32)
    own_a, own_b = camera_tokens[:half], camera_tokens[half:]
    pairs = moment_flips(moment_pair(start_f32))
    own_a, own_b, a_before, a_after, *pairs = sync(
        own_a, own_b, sent(own_a, 1), sent(own_a, -1), *pairs
    )

    totals = moment_shards(moment_sum(pairs))
    own_a, own_b, a_before, a_after, a_away, *totals = sync(
        own_a, own_b, a_before, a_after, sent(a_before, 1), *totals
    )
    totals_a = [total[:, :half] for total in totals]
    totals_b = [total[:, half:] for total in totals]

    b_before = sent(own_b, 1)
    tok_a = normed_shards((own_a, a_before, a_after, a_away), norm_gain, totals_a)
    qs_a = heads_send(tok_a, heads_in)
    tok_a, own_b, b_before, qs_a = sync(tok_a, own_b, b_before, qs_a)

    b_after, qc_a = sent(own_b, -1), core_swap(qs_a)
    qx_a = heads_across(tok_a, heads_in, qc_a, 2)
    tok_a, own_b, b_before, b_after, qc_a, qx_a0, qx_a1 = sync(
        tok_a, own_b, b_before, b_after, qc_a, *qx_a
    )

    qy_a0 = y_swap(qx_a0)
    us_a = units_send(tok_a)
    tok_a, own_b, b_before, b_after, qc_a, us_a, qy_a0, qx_a1 = sync(
        tok_a, own_b, b_before, b_after, qc_a, us_a, qy_a0, qx_a1
    )

    uc_a, qy_a1, b_away = core_swap(us_a), y_swap(qx_a1), sent(b_before, 1)
    (ux_a,) = units_across(tok_a, uc_a, 1)
    tok_a, qc_a, uc_a, ux_a, qy_a0, qy_a1, own_b, b_before, b_after, b_away = sync(
        tok_a, qc_a, uc_a, ux_a, qy_a0, qy_a1, own_b, b_before, b_after, b_away
    )

    uy_a = y_swap(ux_a)
    tok_b = normed_shards((own_b, b_before, b_after, b_away), norm_gain, totals_b)
    qs_b = heads_send(tok_b, heads_in)
    us_b = units_send(tok_b)
    at_a = project_heads(run, tok_a, heads_in, scales, head_width, qc_a, (qy_a0, qy_a1), True)
    tok_a, tok_b, qs_b, us_b, at_a, uc_a, uy_a = sync(
        tok_a, tok_b, qs_b, us_b, at_a, uc_a, uy_a
    )

    at_ya, at_ca, qc_b, uc_b = y_swap(at_a), core_swap(at_a), core_swap(qs_b), core_swap(us_b)
    hd_a = units_end(tok_a, uc_a, uy_a)
    tok_b, at_a, at_ya, at_ca, qc_b, uc_b, hd_a = sync(
        tok_b, at_a, at_ya, at_ca, qc_b, uc_b, hd_a
    )

    hd_ya, hd_ca, at_fa = y_swap(hd_a), core_swap(hd_a), core_swap(at_ya)
    (qx_b,) = heads_across(tok_b, heads_in, qc_b)
    ux_b = units_across(tok_b, uc_b, 2)
    mixed_a = units_down(((hd_a,),), 0, heads_out((at_a, at_ca, at_ya)))
    tok_b, at_fa, hd_ya, hd_ca, qc_b, uc_b, qx_b, mixed_a, *ux_b = sync(
        tok_b, at_fa, hd_ya, hd_ca, qc_b, uc_b, qx_b, mixed_a, *ux_b
    )

    qy_b, hd_fa = y_swap(qx_b), core_swap(hd_ya)
    mixed_a = heads_out((at_fa,), 3, mixed_a)
    mixed_a = units_down(((hd_ca,), (hd_ya,), (hd_fa,)), 1, mixed_a)
    tok_b, mixed_a, qc_b, qy_b, uc_b, ux_b0, ux_b1 = sync(
        tok_b, mixed_a, qc_b, qy_b, uc_b, *ux_b
    )

    uy_b0 = y_swap(ux_b0)
    mine_a, before_a, after_a, away_a = jnp.split(mixed_a, 4)
    to_after, from_after = sent(away_a, 1), sent(before_a, -1)
    at_b = project_heads(run, tok_b, heads_in, scales, head_width, qc_b, (qy_b,), True)
    tok_b, uc_b, uy_b0, ux_b1, at_b, mine_a, after_a, to_after, from_after = sync(
        tok_b, uc_b, uy_b0, ux_b1, at_b, mine_a, after_a, to_after, from_after
    )

    from_before = sent(after_a + to_after.astype(jnp.float32), 1)
    uy_b1, at_yb, at_cb = y_swap(ux_b1), y_swap(at_b), core_swap(at_b)
    hd_b0 = units_end(tok_b, uc_b, uy_b0)
    mixed_b = heads_out((at_b, at_cb))
    tok_b, uc_b, uy_b1, hd_b0, at_yb, mixed_b, mine_a, *arrived = sync(
        tok_b, uc_b, uy_b1, hd_b0, at_yb, mixed_b, mine_a, from_before, from_after
    )

    hd_yb0, at_fb = y_swap(hd_b0), core_swap(at_yb)
    layer_a = layer_end(start_f32[:half], mine_a, *arrived)
    pairs = moment_flips(moment_pair(layer_a.astype(jnp.float32)))
    hd_b1 = units_end(tok_b, uc_b, uy_b1, 1)
    mixed_b = heads_out((at_yb, at_fb), 2, mixed_b)
    hd_b0, hd_b1, hd_yb0, mixed_b, layer_a, *pairs = sync(
        hd_b0, hd_b1, hd_yb0, mixed_b, layer_a, *pairs
    )

    hd_yb1, hd_cb0, hd_cb1 = y_swap(hd_b1), core_swap(hd_b0), core_swap(hd_b1)
    join_a = normalize(layer_a.astype(jnp.float32), join_gain, moment_sum(pairs))
    ja_before, ja_after = sent(join_a, 1), sent(join_a, -1)
    mixed_b = units_down(((hd_b0, hd_b1),), 0, mixed_b)
    hd_cb0, hd_cb1, hd_yb0, hd_yb1, mixed_b, layer_a, join_a, ja_before, ja_after = sync(
        hd_cb0, hd_cb1, hd_yb0, hd_yb1, mixed_b, layer_a, join_a, ja_before, ja_after
    )

    hd_fb0 = core_swap(hd_yb0)
    hd_fb1 = core_swap(hd_yb1)
    mixed_b = units_down(((hd_cb0, hd_cb1),), 1, mixed_b)
    hd_yb0, hd_yb1, hd_fb0, hd_fb1, mixed_b, join_a, ja_before, ja_after = sync(
        hd_yb0, hd_yb1, hd_fb0, hd_fb1, mixed_b, join_a, ja_before, ja_after
    )

    ja_away = sent(ja_before, 1)
    mixed_b = units_down(((hd_yb0, hd_yb1), (hd_fb0, hd_fb1)), 2, mixed_b)
    mixed_b, join_a, ja_before, ja_after, ja_away = sync(
        mixed_b, join_a, ja_before, ja_after, ja_away
    )

    mine_b, before_b, after_b, away_b = jnp.split(mixed_b, 4)
    to_after, from_after = sent(away_b, 1), sent(before_b, -1)
    tok_ja = jnp.concatenate((join_a, ja_before, ja_after, ja_away))
    js_a = heads_send(tok_ja, join_in)
    mine_b, after_b, to_after, from_after, tok_ja, js_a = sync(
        mine_b, after_b, to_after, from_after, tok_ja, js_a
    )

    from_before, jc_a = sent(after_b + to_after.astype(jnp.float32), 1), core_swap(js_a)
    jx_a = heads_across(tok_ja, join_in, jc_a, 2)
    tok_ja, jc_a, jx_a0, jx_a1, mine_b, *arrived = sync(
        tok_ja, jc_a, *jx_a, mine_b, from_before, from_after
    )

    layer_b = layer_end(start_f32[half:], mine_b, *arrived)
    totals = moment_shards(moment_sum(moment_flips(moment_pair(layer_b.astype(jnp.float32)))))
    jb_before, jb_after = sent(layer_b, 1), sent(layer_b, -1)
    tok_ja, jc_a, jx_a0, jx_a1, layer_b, jb_before, jb_after, *totals = sync(
        tok_ja, jc_a, jx_a0, jx_a1, layer_b, jb_before, jb_after, *totals
    )

    jb_away = sent(jb_before, 1)
    jy_a0 = y_swap(jx_a0)
    tok_ja, jc_a, jy_a0, jx_a1, layer_b, jb_before, jb_after, jb_away, *totals = sync(
        tok_ja, jc_a, jy_a0, jx_a1, layer_b, jb_before, jb_after, jb_away, *totals
    )

    jy_a1 = y_swap(jx_a1)
    tok_jb = normed_shards((layer_b, jb_before, jb_after, jb_away), join_gain, totals)
    jc_b = core_swap(heads_send(tok_jb, join_in))
    (jx_b,) = heads_across(tok_jb, join_in, jc_b)
    tok_ja, jc_a, jy_a0, jy_a1, tok_jb, jc_b, jx_b = sync(
        tok_ja, jc_a, jy_a0, jy_a1, tok_jb, jc_b, jx_b
    )

    jy_b = y_swap(jx_b)
    parts_a = project_heads(
        run, tok_ja, join_in, join_scales, head_width, jc_a, (jy_a0, jy_a1), False
    )
    kept_b = project_keep(run, tok_jb, join_in, head_width, jc_b)
    jy_b, parts_a, kept_b = sync(jy_b, parts_a, kept_b)

    joined = join_blend(run, parts_a, kept_b, jy_b, join_scales)
    joined = joined.reshape(2, 4, half, head_width).swapaxes(0, 1).reshape(8 * half, head_width)
    jo_y, jo_c = y_swap(joined), core_swap(joined)
    jo_f = core_swap(jo_y)
    result = contract(run, ((joined,), (jo_c,), (jo_y,), (jo_f,)), join_out, 1)
    summed = scatter_rows(result)
    layer_own = jnp.concatenate((layer_a, layer_b))
    return (layer_own.astype(jnp.float32) + summed).astype(jnp.bfloat16)


def layer(*arrays):
    own_rows, heads_width = arrays[0].shape[0], arrays[2].shape[1]
    fits = lax.axis_size("cols") == 4 and lax.axis_size("rows") == 4
    fits = fits and own_rows == 2 * TOK_CAM and heads_width % (4 * HEAD_DIM) == 0
    return (fast_body if fits else generic_body)(*arrays)


def solution(mesh):
    in_specs = (
        P(("groups", "rows"), "cols"),
        P("cols"),
        P("cols", "rows"),
        P("cols", "rows"),
        P("cols", "rows"),
        P("rows"),
        P("rows"),
        P("rows", "cols"),
        P("cols", "rows"),
        P("rows"),
        P("rows", "cols"),
        P("cols"),
        P("cols"),
        P("cols", "rows"),
        P("cols", "rows"),
        P("cols", "rows"),
        P("rows"),
        P("rows"),
        P("rows", "cols"),
    )
    out_specs = P(("groups", "rows"), "cols")
    return jax.shard_map(layer, mesh=mesh, in_specs=in_specs, out_specs=out_specs, check_vma=False)
```

```python
import math

import jax
import jax.numpy as jnp
from jax import lax
from jax.experimental import pallas as pl
from jax.experimental.pallas import tpu as pltpu
from jax.sharding import PartitionSpec as P

HEAD_DIM = 128
TOK_CAM = 64
D = 6144


EPS = 1e-06


def partner_2(array, axis, bit):
    return lax.ppermute(array, axis, [(i, i ^ 1 << bit) for i in range(lax.axis_size(axis))])


def normalize(values, scales, moments):
    row_mean = moments[0] / D
    row_var = moments[1] / D - row_mean * row_mean
    return ((values - row_mean[:, None]) * lax.rsqrt(row_var[:, None] + EPS) * scales).astype(
        jnp.bfloat16
    )


def shard_moments(values):
    return lax.psum((jnp.sum(values, 1), jnp.sum(values * values, 1)), "cols")


def head_norm(values, scales):
    row_count = values.shape[0]
    grouped = values.reshape(row_count, -1, HEAD_DIM)
    row_mean = jnp.mean(grouped, -1, keepdims=True)
    row_var = jnp.mean(grouped * grouped, -1, keepdims=True) - row_mean * row_mean
    normed = (grouped - row_mean) * lax.rsqrt(row_var + EPS)
    return (normed.reshape(row_count, -1) * scales).astype(jnp.bfloat16)


def attend(queries, key_rows, val_rows):
    inv_root = 1.0 / math.sqrt(HEAD_DIM)
    scores = (
        jnp.einsum("bqhd,bkhd->bhqk", queries, key_rows, preferred_element_type=jnp.float32)
        * inv_root
    )
    row_max = jnp.max(scores, -1, keepdims=True)
    weights = jnp.exp(scores - row_max)
    row_sum = jnp.sum(weights, -1)
    blended = jnp.einsum(
        "bhqk,bkhd->bqhd",
        weights.astype(jnp.bfloat16),
        val_rows,
        preferred_element_type=jnp.float32,
    )
    return blended / jnp.transpose(row_sum, (0, 2, 1))[..., None]


def to_heads(matrix, blocks):
    return matrix.reshape(blocks, -1, matrix.shape[1] // HEAD_DIM, HEAD_DIM)


def camera_attention(queries, key_rows, val_rows):
    local_rows = queries.shape[0]
    if local_rows >= TOK_CAM:
        blocks = local_rows // TOK_CAM
        result = attend(
            to_heads(queries, blocks), to_heads(key_rows, blocks), to_heads(val_rows, blocks)
        )
    else:
        cam_span = TOK_CAM // local_rows
        position = lax.axis_index("cols")
        key_value = jnp.stack((key_rows, val_rows))
        for which_bit in range(cam_span.bit_length() - 1):
            partner = partner_2(key_value, "cols", which_bit)
            is_lower = position >> which_bit & 1 == 0
            key_value = jnp.where(
                is_lower,
                jnp.concatenate((key_value, partner), 1),
                jnp.concatenate((partner, key_value), 1),
            )
        result = attend(to_heads(queries, 1), to_heads(key_value[0], 1), to_heads(key_value[1], 1))
    return result.reshape(local_rows, -1).astype(jnp.bfloat16)


def generic_body(
    camera_tokens,
    norm_gain,
    query_weight,
    key_weight,
    value_weight,
    query_gain,
    key_gain,
    out_weight,
    up_weight,
    up_bias,
    down_weight,
    down_bias,
    join_gain,
    join_query,
    join_key,
    join_value,
    join_query_gain,
    join_key_gain,
    join_out,
):
    own_rows = camera_tokens.shape[0]
    all_rows = own_rows * lax.axis_size("rows")
    col_rows = all_rows // lax.axis_size("cols")
    attn_width = query_weight.shape[1]
    start_f32 = camera_tokens.astype(jnp.float32)
    normed_all = lax.all_gather(
        normalize(start_f32, norm_gain, shard_moments(start_f32)), "rows", axis=0, tiled=True
    )
    joint_weight = jnp.concatenate((query_weight, key_weight, value_weight, up_weight), 1)
    joint = lax.psum_scatter(
        jnp.dot(normed_all, joint_weight, preferred_element_type=jnp.float32),
        "cols",
        scatter_dimension=0,
        tiled=True,
    )
    up_sum = joint[:, 3 * attn_width :]
    hidden = jax.nn.gelu(up_sum + up_bias, approximate=False).astype(jnp.bfloat16)
    attended = camera_attention(
        head_norm(joint[:, :attn_width], query_gain),
        head_norm(joint[:, attn_width : 2 * attn_width], key_gain),
        joint[:, 2 * attn_width : 3 * attn_width].astype(jnp.bfloat16),
    )
    attn_all, hidden_all = (
        lax.all_gather(attended, "cols", axis=0, tiled=True),
        lax.all_gather(hidden, "cols", axis=0, tiled=True),
    )
    mixed = lax.psum_scatter(
        jnp.dot(attn_all, out_weight, preferred_element_type=jnp.float32)
        + jnp.dot(hidden_all, down_weight, preferred_element_type=jnp.float32),
        "rows",
        scatter_dimension=0,
        tiled=True,
    )
    layer_own = (start_f32 + mixed + down_bias).astype(jnp.bfloat16)
    layer_f32 = layer_own.astype(jnp.float32)
    join_in = lax.all_gather(
        normalize(layer_f32, join_gain, shard_moments(layer_f32)), "rows", axis=0, tiled=True
    )
    join_weight = jnp.concatenate((join_query, join_key, join_value), 1)
    join_joint = lax.psum_scatter(
        jnp.dot(join_in, join_weight, preferred_element_type=jnp.float32),
        "cols",
        scatter_dimension=0,
        tiled=True,
    )
    join_q = head_norm(join_joint[:, :attn_width], join_query_gain)
    join_k = head_norm(join_joint[:, attn_width : 2 * attn_width], join_key_gain)
    join_v = join_joint[:, 2 * attn_width :].astype(jnp.bfloat16)
    heads_here = attn_width // HEAD_DIM
    query_heads = join_q.reshape(col_rows, heads_here, HEAD_DIM)
    inv_root = 1.0 / math.sqrt(HEAD_DIM)
    run_max = jnp.full((heads_here, col_rows), -jnp.inf, jnp.float32)
    run_sum = jnp.zeros((heads_here, col_rows), jnp.float32)
    accum = jnp.zeros((col_rows, heads_here, HEAD_DIM), jnp.float32)
    key_part = lax.all_gather(join_k, "cols", axis=0, tiled=True)
    val_part = lax.all_gather(join_v, "cols", axis=0, tiled=True)
    row_count = key_part.shape[0]
    key_heads = key_part.reshape(row_count, heads_here, HEAD_DIM)
    val_heads = val_part.reshape(row_count, heads_here, HEAD_DIM)
    scores = (
        jnp.einsum("qhd,khd->hqk", query_heads, key_heads, preferred_element_type=jnp.float32)
        * inv_root
    )
    new_max = jnp.max(scores, -1)
    factor = jnp.exp(run_max - new_max)
    weights = jnp.exp(scores - new_max[..., None])
    run_sum = run_sum * factor + jnp.sum(weights, -1)
    accum = accum * jnp.transpose(factor)[..., None] + jnp.einsum(
        "hqk,khd->qhd", weights.astype(jnp.bfloat16), val_heads, preferred_element_type=jnp.float32
    )
    run_max, run_sum, accum = (new_max, run_sum, accum)
    joined_attn = (
        (accum / jnp.transpose(run_sum)[..., None])
        .reshape(col_rows, attn_width)
        .astype(jnp.bfloat16)
    )
    joined_all = lax.all_gather(joined_attn, "cols", axis=0, tiled=True)
    result = lax.psum_scatter(
        jnp.dot(joined_all, join_out, preferred_element_type=jnp.float32),
        "rows",
        scatter_dimension=0,
        tiled=True,
    )
    return (layer_own.astype(jnp.float32) + result).astype(jnp.bfloat16)


VMEM_BYTES = 48 * 1024 * 1024


def flip(array, mask):
    size = lax.axis_size("cols")
    return lax.ppermute(array, "cols", [(i, i ^ mask) for i in range(size)])


def core_swap(array):
    return flip(array, 1)


def y_swap(array):
    return flip(array, 2)


def row_shift(array, shift):
    size = lax.axis_size("rows")
    return lax.ppermute(array, "rows", [(i, (i + shift) % size) for i in range(size)])


class Runner:
    def __init__(self, position):
        self.position = position

    def __call__(self, kernel, grid, operands, in_specs, out_shape, out_spec):
        return pl.pallas_call(
            kernel,
            out_shape=out_shape,
            grid_spec=pltpu.PrefetchScalarGridSpec(
                num_scalar_prefetch=1, grid=grid, in_specs=list(in_specs), out_specs=out_spec
            ),
            compiler_params=pltpu.CompilerParams(vmem_limit_bytes=VMEM_BYTES),
            cost_estimate=pl.CostEstimate(flops=1, bytes_accessed=1, transcendentals=0),
        )(self.position, *operands)


def joined_rows(refs, at=slice(None)):
    return jnp.concatenate([ref[:, at] for ref in refs])


def store_rows(refs, at, values):
    piece = values.shape[0] // len(refs)
    for j, ref in enumerate(refs):
        ref[:, at] = values[j * piece : (j + 1) * piece].astype(ref.dtype)


def whole(array):
    return pl.BlockSpec(array.shape, lambda s, pos: (0,) * array.ndim)


def mine_of(pos):
    return 2 * pos[0] + pos[1]


def across_of(pos):
    return 2 * pos[0] + 1 - pos[1]


def dot_f32(a, b):
    return jnp.dot(a, b, preferred_element_type=jnp.float32)


def project_send(run, tokens, weights, width, sub):
    rows, depth = tokens.shape
    block = width // sub
    wide = len(weights) * block

    def kernel(pos, tokens_ref, *refs):
        for i in range(len(weights)):
            refs[-1][:, i * block : (i + 1) * block] = dot_f32(
                tokens_ref[...], refs[i][...]
            ).astype(jnp.bfloat16)

    spec = pl.BlockSpec((depth, block), lambda s, pos: (0, 2 * (1 - pos[0]) * sub + s))
    return run(
        kernel,
        (2 * sub,),
        (tokens, *weights),
        (whole(tokens), *[spec] * len(weights)),
        jax.ShapeDtypeStruct((rows, 2 * sub * wide), jnp.bfloat16),
        pl.BlockSpec((rows, wide), lambda s, pos: (0, s)),
    )


def project_across(run, tokens, weights, width, sub, arrived, pieces=1):
    rows, depth = tokens.shape
    block = width // sub
    wide = len(weights) * block

    def kernel(pos, tokens_ref, *refs):
        for i in range(len(weights)):
            at = slice(i * block, (i + 1) * block)
            part = dot_f32(tokens_ref[...], refs[i][...])
            part = part + refs[len(weights)][:, at].astype(jnp.float32)
            store_rows(refs[len(weights) + 1 :], at, part)

    spec = pl.BlockSpec((depth, block), lambda s, pos: (0, across_of(pos) * sub + s))
    return run(
        kernel,
        (sub,),
        (tokens, *weights, arrived),
        (
            whole(tokens),
            *[spec] * len(weights),
            pl.BlockSpec((rows, wide), lambda s, pos: (0, (1 - pos[1]) * sub + s)),
        ),
        (jax.ShapeDtypeStruct((rows // pieces, sub * wide), jnp.bfloat16),) * pieces,
        (pl.BlockSpec((rows // pieces, wide), lambda s, pos: (0, s)),) * pieces,
    )


def project_hidden(run, tokens, weight, bias, width, sub, arrived, from_side, at=0):
    depth = tokens.shape[1]
    rows = from_side.shape[0]
    block = width // sub

    def kernel(pos, tokens_ref, weight_ref, bias_ref, arrived_ref, side_ref, out_ref):
        total = dot_f32(tokens_ref[...], weight_ref[...])
        total = total + arrived_ref[...].astype(jnp.float32) + side_ref[...].astype(jnp.float32)
        total = total + bias_ref[...]
        out_ref[...] = (total * (1.0 + lax.erf(total * math.sqrt(0.5))) * 0.5).astype(jnp.bfloat16)

    return run(
        kernel,
        (sub,),
        (tokens, weight, bias, arrived, from_side),
        (
            pl.BlockSpec((rows, depth), lambda s, pos: (at, 0)),
            pl.BlockSpec((depth, block), lambda s, pos: (0, mine_of(pos) * sub + s)),
            pl.BlockSpec((1, block), lambda s, pos: (0, mine_of(pos) * sub + s)),
            pl.BlockSpec((rows, block), lambda s, pos: (at, pos[1] * sub + s)),
            pl.BlockSpec((rows, block), lambda s, pos: (0, s)),
        ),
        jax.ShapeDtypeStruct((rows, width), jnp.bfloat16),
        pl.BlockSpec((rows, block), lambda s, pos: (0, s)),
    )


def project_keep(run, tokens, weights, width, arrived):
    rows, depth = tokens.shape
    wide = len(weights) * width

    def kernel(pos, tokens_ref, *refs):
        arrived_ref, out_ref = refs[len(weights) :]
        for i in range(len(weights)):
            at = slice(i * width, (i + 1) * width)
            part = dot_f32(tokens_ref[...], refs[i][...])
            out_ref[:, at] = part + arrived_ref[:, at].astype(jnp.float32)

    spec = pl.BlockSpec((depth, width), lambda s, pos: (0, mine_of(pos)))
    return run(
        kernel,
        (1,),
        (tokens, *weights, arrived),
        (
            whole(tokens),
            *[spec] * len(weights),
            pl.BlockSpec((rows, wide), lambda s, pos: (0, pos[1])),
        ),
        jax.ShapeDtypeStruct((rows, wide), jnp.float32),
        pl.BlockSpec((rows, wide), lambda s, pos: (0, 0)),
    )


def unit_norm(values, scales):
    row_mean = jnp.mean(values, -1, keepdims=True)
    row_var = jnp.mean(values * values, -1, keepdims=True) - row_mean * row_mean
    return ((values - row_mean) * lax.rsqrt(row_var + EPS) * scales).astype(jnp.bfloat16)


def softmax_blend(query, key, value, keep=None):
    scores = lax.dot_general(
        query, key, (((1,), (1,)), ((), ())), preferred_element_type=jnp.float32
    ) * (1.0 / math.sqrt(HEAD_DIM))
    if keep is not None:
        scores = jnp.where(keep, scores, -jnp.inf)
    weights = jnp.exp(scores - jnp.max(scores, -1, keepdims=True))
    row_sum = jnp.sum(weights, -1, keepdims=True)
    blended = dot_f32(weights.astype(jnp.bfloat16), value)
    return (blended / row_sum).astype(jnp.bfloat16)


def project_heads(run, tokens, weights, scales, width, arrived, from_side, attend_camera):
    rows, depth = tokens.shape
    heads = width // HEAD_DIM
    out_width = width if attend_camera else 3 * width

    def kernel(pos, tokens_ref, *refs):
        weight_refs, scale_refs = refs[:3], refs[3:5]
        arrived_ref, *side_refs, out_ref = refs[5:]
        raws = []
        for i in range(3):
            at = slice(i * width, (i + 1) * width)
            raw = dot_f32(tokens_ref[...], weight_refs[i][...])
            raw = raw + arrived_ref[:, at].astype(jnp.float32)
            raws.append(raw + joined_rows(side_refs, at).astype(jnp.float32))
        if attend_camera:
            row_cam = lax.broadcasted_iota(jnp.int32, (rows, rows), 0) // TOK_CAM
            col_cam = lax.broadcasted_iota(jnp.int32, (rows, rows), 1) // TOK_CAM
            same = row_cam == col_cam
        for h in range(heads):
            at = slice(h * HEAD_DIM, (h + 1) * HEAD_DIM)
            query = unit_norm(raws[0][:, at], scale_refs[0][:, at])
            key = unit_norm(raws[1][:, at], scale_refs[1][:, at])
            value = raws[2][:, at].astype(jnp.bfloat16)
            if attend_camera:
                out_ref[:, at] = softmax_blend(query, key, value, same)
            else:
                out_ref[:, at] = query
                out_ref[:, width + h * HEAD_DIM : width + (h + 1) * HEAD_DIM] = key
                out_ref[:, 2 * width + h * HEAD_DIM : 2 * width + (h + 1) * HEAD_DIM] = value

    weight_spec = pl.BlockSpec((depth, width), lambda s, pos: (0, mine_of(pos)))
    scale_spec = pl.BlockSpec((1, width), lambda s, pos: (0, mine_of(pos)))
    return run(
        kernel,
        (1,),
        (tokens, *weights, *scales, arrived, *from_side),
        (
            whole(tokens),
            *[weight_spec] * 3,
            *[scale_spec] * 2,
            pl.BlockSpec((rows, 3 * width), lambda s, pos: (0, pos[1])),
            *[whole(piece) for piece in from_side],
        ),
        jax.ShapeDtypeStruct((rows, out_width), jnp.bfloat16),
        pl.BlockSpec((rows, out_width), lambda s, pos: (0, 0)),
    )


def contract(run, parts, weight, sub, first=0, start=None):
    rows = sum(piece.shape[0] for piece in parts[0])
    width = parts[0][0].shape[1]
    count, pieces = len(parts), len(parts[0])
    out_width = weight.shape[1]
    block = width // sub

    def kernel(pos, weight_ref, *refs):
        out_ref = refs[-1]
        step = pl.program_id(0)
        for i in range(count):

            @pl.when(step // sub == i)
            def _(i=i):
                part = joined_rows(refs[i * pieces : (i + 1) * pieces])
                term = dot_f32(part, weight_ref[...])
                if i > 0:
                    out_ref[...] += term
                elif sub == 1:
                    out_ref[...] = term if start is None else term + refs[-2][...]
                else:

                    @pl.when(step == 0)
                    def _():
                        out_ref[...] = term if start is None else term + refs[-2][...]

                    @pl.when(step > 0)
                    def _():
                        out_ref[...] += term

    def weight_block(s, pos):
        i = s // sub + first
        return (2 * (pos[0] ^ (i & 1)) + (pos[1] ^ (i >> 1))) * sub + s % sub, 0

    def part_spec(i):
        return pl.BlockSpec(
            (rows // pieces, block), lambda s, pos: (0, jnp.clip(s - i * sub, 0, sub - 1))
        )

    operands = [weight, *[piece for part in parts for piece in part]]
    in_specs = [pl.BlockSpec((block, out_width), weight_block)]
    in_specs += [part_spec(i) for i in range(count) for _ in range(pieces)]
    if start is not None:
        operands.append(start)
        in_specs.append(whole(start))
    return run(
        kernel,
        (count * sub,),
        operands,
        in_specs,
        jax.ShapeDtypeStruct((rows, out_width), jnp.float32),
        pl.BlockSpec((rows, out_width), lambda s, pos: (0, 0)),
    )


def join_blend(run, parts, kept, from_side, scales):
    rows = parts.shape[0] + kept.shape[0]
    heads = parts.shape[1] // 3 // HEAD_DIM

    def kernel(pos, *refs):
        part_refs, kept_refs, side_refs = refs[:3], refs[3:6], refs[6:9]
        *scale_refs, out_ref = refs[9:]
        raws = [k[...] + s[...].astype(jnp.float32) for k, s in zip(kept_refs, side_refs)]
        late = [unit_norm(raws[i], scale_refs[i][...]) for i in range(2)]
        late.append(raws[2].astype(jnp.bfloat16))
        query, key, value = (
            jnp.concatenate((part_refs[i][...], late[i])) for i in range(3)
        )
        out_ref[...] = softmax_blend(query, key, value)

    def specs(array):
        return [
            pl.BlockSpec((array.shape[0], HEAD_DIM), lambda h, pos, i=i: (0, i * heads + h))
            for i in range(3)
        ]

    scale_spec = pl.BlockSpec((1, HEAD_DIM), lambda h, pos: (0, mine_of(pos) * heads + h))
    return run(
        kernel,
        (heads,),
        (*[parts] * 3, *[kept] * 3, *[from_side] * 3, *scales),
        (*specs(parts), *specs(kept), *specs(from_side), *[scale_spec] * 2),
        jax.ShapeDtypeStruct((rows, heads * HEAD_DIM), jnp.bfloat16),
        pl.BlockSpec((rows, HEAD_DIM), lambda h, pos: (0, h)),
    )


def moment_pair(values):
    return jnp.stack((jnp.sum(values, 1), jnp.sum(values * values, 1)))


def moment_flips(pair):
    return pair, flip(pair, 1), flip(pair, 2), flip(pair, 3)


def moment_sum(pairs):
    return (pairs[0] + pairs[1]) + (pairs[2] + pairs[3])


def sent(array, shift):
    return row_shift(array.astype(jnp.bfloat16), shift)


def moment_shards(total):
    return total, row_shift(total, 1), row_shift(total, -1), row_shift(total, 2)


def normed_shards(shards, scales, totals):
    return jnp.concatenate(
        [normalize(x.astype(jnp.float32), scales, m) for x, m in zip(shards, totals)]
    )


def sync(*values):
    return lax.optimization_barrier(values)


def scatter_rows(terms):
    own, before, after, away = jnp.split(terms, 4)
    half = own.shape[0] // 2

    def send(array, shift):
        return sent(array, shift).astype(jnp.float32)

    to_after = send(away[:half], 1)
    to_before = send(away[half:], -1)
    from_before = jnp.concatenate((send(after[:half] + to_after, 1), send(after[half:], 1)))
    from_after = jnp.concatenate((send(before[:half], -1), send(before[half:] + to_before, -1)))
    return own + from_before + from_after


def fast_body(
    camera_tokens,
    norm_gain,
    query_weight,
    key_weight,
    value_weight,
    query_gain,
    key_gain,
    out_weight,
    up_weight,
    up_bias,
    down_weight,
    down_bias,
    join_gain,
    join_query,
    join_key,
    join_value,
    join_query_gain,
    join_key_gain,
    join_out,
):
    half = TOK_CAM
    index = lax.axis_index("cols")
    run = Runner(jnp.stack((index & 1, index >> 1)).astype(jnp.int32))
    head_width = query_weight.shape[1] // 4
    unit_width = up_weight.shape[1] // 4
    sub = 3 if unit_width % (3 * 256) == 0 else 1
    heads_in = (query_weight, key_weight, value_weight)
    join_in = (join_query, join_key, join_value)
    scales = (query_gain[None], key_gain[None])
    join_scales = (join_query_gain[None], join_key_gain[None])
    bias = up_bias[None]

    def heads_send(tokens, weights):
        return project_send(run, tokens, weights, head_width, 1)

    def heads_across(tokens, weights, arrived, pieces=1):
        return project_across(run, tokens, weights, head_width, 1, arrived, pieces)

    def heads_out(parts, first=0, start=None):
        return contract(run, [(part,) for part in parts], out_weight, 1, first, start)

    def units_down(parts, first, start):
        return contract(run, parts, down_weight, 2, first, start)

    def units_send(tokens):
        return project_send(run, tokens, (up_weight,), unit_width, sub)

    def units_across(tokens, arrived, pieces):
        return project_across(run, tokens, (up_weight,), unit_width, sub, arrived, pieces)

    def units_end(tokens, arrived, side, at=0):
        return project_hidden(run, tokens, up_weight, bias, unit_width, sub, arrived, side, at)

    def layer_end(start, own, *arrived):
        total = own
        for term in arrived:
            total = total + term.astype(jnp.float32)
        return (start + total + down_bias).astype(jnp.bfloat16)

    start_f32 = camera_tokens.astype(jnp.float32)
    own_a, own_b = camera_tokens[:half], camera_tokens[half:]
    pairs = moment_flips(moment_pair(start_f32))
    own_a, own_b, a_before, a_after, *pairs = sync(
        own_a, own_b, sent(own_a, 1), sent(own_a, -1), *pairs
    )

    totals = moment_shards(moment_sum(pairs))
    own_a, own_b, a_before, a_after, a_away, *totals = sync(
        own_a, own_b, a_before, a_after, sent(a_before, 1), *totals
    )
    totals_a = [total[:, :half] for total in totals]
    totals_b = [total[:, half:] for total in totals]

    b_before = sent(own_b, 1)
    tok_a = normed_shards((own_a, a_before, a_after, a_away), norm_gain, totals_a)
    qs_a = heads_send(tok_a, heads_in)
    tok_a, own_b, b_before, qs_a = sync(tok_a, own_b, b_before, qs_a)

    b_after, qc_a = sent(own_b, -1), core_swap(qs_a)
    qx_a = heads_across(tok_a, heads_in, qc_a, 2)
    tok_a, own_b, b_before, b_after, qc_a, qx_a0, qx_a1 = sync(
        tok_a, own_b, b_before, b_after, qc_a, *qx_a
    )

    qy_a0 = y_swap(qx_a0)
    us_a = units_send(tok_a)
    tok_a, own_b, b_before, b_after, qc_a, us_a, qy_a0, qx_a1 = sync(
        tok_a, own_b, b_before, b_after, qc_a, us_a, qy_a0, qx_a1
    )

    uc_a, qy_a1, b_away = core_swap(us_a), y_swap(qx_a1), sent(b_before, 1)
    (ux_a,) = units_across(tok_a, uc_a, 1)
    tok_a, qc_a, uc_a, ux_a, qy_a0, qy_a1, own_b, b_before, b_after, b_away = sync(
        tok_a, qc_a, uc_a, ux_a, qy_a0, qy_a1, own_b, b_before, b_after, b_away
    )

    uy_a = y_swap(ux_a)
    tok_b = normed_shards((own_b, b_before, b_after, b_away), norm_gain, totals_b)
    qs_b = heads_send(tok_b, heads_in)
    us_b = units_send(tok_b)
    at_a = project_heads(run, tok_a, heads_in, scales, head_width, qc_a, (qy_a0, qy_a1), True)
    tok_a, tok_b, qs_b, us_b, at_a, uc_a, uy_a = sync(
        tok_a, tok_b, qs_b, us_b, at_a, uc_a, uy_a
    )

    at_ya, at_ca, qc_b, uc_b = y_swap(at_a), core_swap(at_a), core_swap(qs_b), core_swap(us_b)
    hd_a = units_end(tok_a, uc_a, uy_a)
    tok_b, at_a, at_ya, at_ca, qc_b, uc_b, hd_a = sync(
        tok_b, at_a, at_ya, at_ca, qc_b, uc_b, hd_a
    )

    hd_ya, hd_ca, at_fa = y_swap(hd_a), core_swap(hd_a), core_swap(at_ya)
    (qx_b,) = heads_across(tok_b, heads_in, qc_b)
    ux_b = units_across(tok_b, uc_b, 2)
    mixed_a = units_down(((hd_a,),), 0, heads_out((at_a, at_ca, at_ya)))
    tok_b, at_fa, hd_ya, hd_ca, qc_b, uc_b, qx_b, mixed_a, *ux_b = sync(
        tok_b, at_fa, hd_ya, hd_ca, qc_b, uc_b, qx_b, mixed_a, *ux_b
    )

    qy_b, hd_fa = y_swap(qx_b), core_swap(hd_ya)
    mixed_a = heads_out((at_fa,), 3, mixed_a)
    mixed_a = units_down(((hd_ca,), (hd_ya,), (hd_fa,)), 1, mixed_a)
    tok_b, mixed_a, qc_b, qy_b, uc_b, ux_b0, ux_b1 = sync(
        tok_b, mixed_a, qc_b, qy_b, uc_b, *ux_b
    )

    uy_b0 = y_swap(ux_b0)
    mine_a, before_a, after_a, away_a = jnp.split(mixed_a, 4)
    to_after = sent(away_a, 1)
    at_b = project_heads(run, tok_b, heads_in, scales, head_width, qc_b, (qy_b,), True)
    tok_b, uc_b, uy_b0, ux_b1, at_b, mine_a, before_a, after_a, to_after = sync(
        tok_b, uc_b, uy_b0, ux_b1, at_b, mine_a, before_a, after_a, to_after
    )

    from_before = sent(after_a + to_after.astype(jnp.float32), 1)
    from_after = sent(before_a, -1)
    uy_b1, at_yb, at_cb = y_swap(ux_b1), y_swap(at_b), core_swap(at_b)
    hd_b0 = units_end(tok_b, uc_b, uy_b0)
    mixed_b = heads_out((at_b, at_cb))
    tok_b, uc_b, uy_b1, hd_b0, at_yb, mixed_b, mine_a, *arrived = sync(
        tok_b, uc_b, uy_b1, hd_b0, at_yb, mixed_b, mine_a, from_before, from_after
    )

    hd_yb0, at_fb = y_swap(hd_b0), core_swap(at_yb)
    layer_a = layer_end(start_f32[:half], mine_a, *arrived)
    pairs = moment_flips(moment_pair(layer_a.astype(jnp.float32)))
    hd_b1 = units_end(tok_b, uc_b, uy_b1, 1)
    mixed_b = heads_out((at_yb, at_fb), 2, mixed_b)
    hd_b0, hd_b1, hd_yb0, mixed_b, layer_a, *pairs = sync(
        hd_b0, hd_b1, hd_yb0, mixed_b, layer_a, *pairs
    )

    hd_yb1, hd_cb0, hd_cb1 = y_swap(hd_b1), core_swap(hd_b0), core_swap(hd_b1)
    join_a = normalize(layer_a.astype(jnp.float32), join_gain, moment_sum(pairs))
    ja_before, ja_after = sent(join_a, 1), sent(join_a, -1)
    mixed_b = units_down(((hd_b0, hd_b1),), 0, mixed_b)
    hd_cb0, hd_cb1, hd_yb0, hd_yb1, mixed_b, layer_a, join_a, ja_before, ja_after = sync(
        hd_cb0, hd_cb1, hd_yb0, hd_yb1, mixed_b, layer_a, join_a, ja_before, ja_after
    )

    hd_fb0 = core_swap(hd_yb0)
    hd_fb1 = core_swap(hd_yb1)
    mixed_b = units_down(((hd_cb0, hd_cb1),), 1, mixed_b)
    hd_yb0, hd_yb1, hd_fb0, hd_fb1, mixed_b, join_a, ja_before, ja_after = sync(
        hd_yb0, hd_yb1, hd_fb0, hd_fb1, mixed_b, join_a, ja_before, ja_after
    )

    ja_away = sent(ja_before, 1)
    mixed_b = units_down(((hd_yb0, hd_yb1), (hd_fb0, hd_fb1)), 2, mixed_b)
    mixed_b, join_a, ja_before, ja_after, ja_away = sync(
        mixed_b, join_a, ja_before, ja_after, ja_away
    )

    mine_b, before_b, after_b, away_b = jnp.split(mixed_b, 4)
    to_after = sent(away_b, 1)
    mine_b, before_b, after_b, to_after, join_a, ja_before, ja_after, ja_away = sync(
        mine_b, before_b, after_b, to_after, join_a, ja_before, ja_after, ja_away
    )

    from_before = sent(after_b + to_after.astype(jnp.float32), 1)
    from_after = sent(before_b, -1)
    tok_ja = jnp.concatenate((join_a, ja_before, ja_after, ja_away))
    js_a = heads_send(tok_ja, join_in)
    tok_ja, js_a, mine_b, *arrived = sync(tok_ja, js_a, mine_b, from_before, from_after)

    layer_b = layer_end(start_f32[half:], mine_b, *arrived)
    pairs = moment_flips(moment_pair(layer_b.astype(jnp.float32)))
    jb_before, jb_after, jc_a = sent(layer_b, 1), sent(layer_b, -1), core_swap(js_a)
    jx_a = heads_across(tok_ja, join_in, jc_a, 2)
    tok_ja, jc_a, jx_a0, jx_a1, layer_b, jb_before, jb_after, *pairs = sync(
        tok_ja, jc_a, *jx_a, layer_b, jb_before, jb_after, *pairs
    )

    totals = moment_shards(moment_sum(pairs))

    jb_away = sent(jb_before, 1)
    jy_a0 = y_swap(jx_a0)
    tok_ja, jc_a, jy_a0, jx_a1, layer_b, jb_before, jb_after, jb_away, *totals = sync(
        tok_ja, jc_a, jy_a0, jx_a1, layer_b, jb_before, jb_after, jb_away, *totals
    )

    jy_a1 = y_swap(jx_a1)
    tok_jb = normed_shards((layer_b, jb_before, jb_after, jb_away), join_gain, totals)
    jc_b = core_swap(heads_send(tok_jb, join_in))
    (jx_b,) = heads_across(tok_jb, join_in, jc_b)
    tok_ja, jc_a, jy_a0, jy_a1, tok_jb, jc_b, jx_b = sync(
        tok_ja, jc_a, jy_a0, jy_a1, tok_jb, jc_b, jx_b
    )

    jy_b = y_swap(jx_b)
    parts_a = project_heads(
        run, tok_ja, join_in, join_scales, head_width, jc_a, (jy_a0, jy_a1), False
    )
    kept_b = project_keep(run, tok_jb, join_in, head_width, jc_b)
    jy_b, parts_a, kept_b = sync(jy_b, parts_a, kept_b)

    joined = join_blend(run, parts_a, kept_b, jy_b, join_scales)
    joined = joined.reshape(2, 4, half, head_width).swapaxes(0, 1).reshape(8 * half, head_width)
    jo_y, jo_c = y_swap(joined), core_swap(joined)
    jo_f = core_swap(jo_y)
    result = contract(run, ((joined,), (jo_c,), (jo_y,), (jo_f,)), join_out, 1)
    summed = scatter_rows(result)
    layer_own = jnp.concatenate((layer_a, layer_b))
    return (layer_own.astype(jnp.float32) + summed).astype(jnp.bfloat16)


def layer(*arrays):
    own_rows, heads_width = arrays[0].shape[0], arrays[2].shape[1]
    fits = lax.axis_size("cols") == 4 and lax.axis_size("rows") == 4
    fits = fits and own_rows == 2 * TOK_CAM and heads_width % (4 * HEAD_DIM) == 0
    return (fast_body if fits else generic_body)(*arrays)


def solution(mesh):
    in_specs = (
        P(("groups", "rows"), "cols"),
        P("cols"),
        P("cols", "rows"),
        P("cols", "rows"),
        P("cols", "rows"),
        P("rows"),
        P("rows"),
        P("rows", "cols"),
        P("cols", "rows"),
        P("rows"),
        P("rows", "cols"),
        P("cols"),
        P("cols"),
        P("cols", "rows"),
        P("cols", "rows"),
        P("cols", "rows"),
        P("rows"),
        P("rows"),
        P("rows", "cols"),
    )
    out_specs = P(("groups", "rows"), "cols")
    return jax.shard_map(layer, mesh=mesh, in_specs=in_specs, out_specs=out_specs, check_vma=False)
```

```python
import math

import jax
import jax.numpy as jnp
from jax import lax
from jax.experimental import pallas as pl
from jax.experimental.pallas import tpu as pltpu
from jax.sharding import PartitionSpec as P

HEAD_DIM = 128
TOK_CAM = 64
D = 6144


EPS = 1e-06


def partner_2(array, axis, bit):
    return lax.ppermute(array, axis, [(i, i ^ 1 << bit) for i in range(lax.axis_size(axis))])


def normalize(values, scales, moments):
    row_mean = moments[0] / D
    row_var = moments[1] / D - row_mean * row_mean
    return ((values - row_mean[:, None]) * lax.rsqrt(row_var[:, None] + EPS) * scales).astype(
        jnp.bfloat16
    )


def shard_moments(values):
    return lax.psum((jnp.sum(values, 1), jnp.sum(values * values, 1)), "cols")


def head_norm(values, scales):
    row_count = values.shape[0]
    grouped = values.reshape(row_count, -1, HEAD_DIM)
    row_mean = jnp.mean(grouped, -1, keepdims=True)
    row_var = jnp.mean(grouped * grouped, -1, keepdims=True) - row_mean * row_mean
    normed = (grouped - row_mean) * lax.rsqrt(row_var + EPS)
    return (normed.reshape(row_count, -1) * scales).astype(jnp.bfloat16)


def attend(queries, key_rows, val_rows):
    inv_root = 1.0 / math.sqrt(HEAD_DIM)
    scores = (
        jnp.einsum("bqhd,bkhd->bhqk", queries, key_rows, preferred_element_type=jnp.float32)
        * inv_root
    )
    row_max = jnp.max(scores, -1, keepdims=True)
    weights = jnp.exp(scores - row_max)
    row_sum = jnp.sum(weights, -1)
    blended = jnp.einsum(
        "bhqk,bkhd->bqhd",
        weights.astype(jnp.bfloat16),
        val_rows,
        preferred_element_type=jnp.float32,
    )
    return blended / jnp.transpose(row_sum, (0, 2, 1))[..., None]


def to_heads(matrix, blocks):
    return matrix.reshape(blocks, -1, matrix.shape[1] // HEAD_DIM, HEAD_DIM)


def camera_attention(queries, key_rows, val_rows):
    local_rows = queries.shape[0]
    if local_rows >= TOK_CAM:
        blocks = local_rows // TOK_CAM
        result = attend(
            to_heads(queries, blocks), to_heads(key_rows, blocks), to_heads(val_rows, blocks)
        )
    else:
        cam_span = TOK_CAM // local_rows
        position = lax.axis_index("cols")
        key_value = jnp.stack((key_rows, val_rows))
        for which_bit in range(cam_span.bit_length() - 1):
            partner = partner_2(key_value, "cols", which_bit)
            is_lower = position >> which_bit & 1 == 0
            key_value = jnp.where(
                is_lower,
                jnp.concatenate((key_value, partner), 1),
                jnp.concatenate((partner, key_value), 1),
            )
        result = attend(to_heads(queries, 1), to_heads(key_value[0], 1), to_heads(key_value[1], 1))
    return result.reshape(local_rows, -1).astype(jnp.bfloat16)


def generic_body(
    camera_tokens,
    norm_gain,
    query_weight,
    key_weight,
    value_weight,
    query_gain,
    key_gain,
    out_weight,
    up_weight,
    up_bias,
    down_weight,
    down_bias,
    join_gain,
    join_query,
    join_key,
    join_value,
    join_query_gain,
    join_key_gain,
    join_out,
):
    own_rows = camera_tokens.shape[0]
    all_rows = own_rows * lax.axis_size("rows")
    col_rows = all_rows // lax.axis_size("cols")
    attn_width = query_weight.shape[1]
    start_f32 = camera_tokens.astype(jnp.float32)
    normed_all = lax.all_gather(
        normalize(start_f32, norm_gain, shard_moments(start_f32)), "rows", axis=0, tiled=True
    )
    joint_weight = jnp.concatenate((query_weight, key_weight, value_weight, up_weight), 1)
    joint = lax.psum_scatter(
        jnp.dot(normed_all, joint_weight, preferred_element_type=jnp.float32),
        "cols",
        scatter_dimension=0,
        tiled=True,
    )
    up_sum = joint[:, 3 * attn_width :]
    hidden = jax.nn.gelu(up_sum + up_bias, approximate=False).astype(jnp.bfloat16)
    attended = camera_attention(
        head_norm(joint[:, :attn_width], query_gain),
        head_norm(joint[:, attn_width : 2 * attn_width], key_gain),
        joint[:, 2 * attn_width : 3 * attn_width].astype(jnp.bfloat16),
    )
    attn_all, hidden_all = (
        lax.all_gather(attended, "cols", axis=0, tiled=True),
        lax.all_gather(hidden, "cols", axis=0, tiled=True),
    )
    mixed = lax.psum_scatter(
        jnp.dot(attn_all, out_weight, preferred_element_type=jnp.float32)
        + jnp.dot(hidden_all, down_weight, preferred_element_type=jnp.float32),
        "rows",
        scatter_dimension=0,
        tiled=True,
    )
    layer_own = (start_f32 + mixed + down_bias).astype(jnp.bfloat16)
    layer_f32 = layer_own.astype(jnp.float32)
    join_in = lax.all_gather(
        normalize(layer_f32, join_gain, shard_moments(layer_f32)), "rows", axis=0, tiled=True
    )
    join_weight = jnp.concatenate((join_query, join_key, join_value), 1)
    join_joint = lax.psum_scatter(
        jnp.dot(join_in, join_weight, preferred_element_type=jnp.float32),
        "cols",
        scatter_dimension=0,
        tiled=True,
    )
    join_q = head_norm(join_joint[:, :attn_width], join_query_gain)
    join_k = head_norm(join_joint[:, attn_width : 2 * attn_width], join_key_gain)
    join_v = join_joint[:, 2 * attn_width :].astype(jnp.bfloat16)
    heads_here = attn_width // HEAD_DIM
    query_heads = join_q.reshape(col_rows, heads_here, HEAD_DIM)
    inv_root = 1.0 / math.sqrt(HEAD_DIM)
    run_max = jnp.full((heads_here, col_rows), -jnp.inf, jnp.float32)
    run_sum = jnp.zeros((heads_here, col_rows), jnp.float32)
    accum = jnp.zeros((col_rows, heads_here, HEAD_DIM), jnp.float32)
    key_part = lax.all_gather(join_k, "cols", axis=0, tiled=True)
    val_part = lax.all_gather(join_v, "cols", axis=0, tiled=True)
    row_count = key_part.shape[0]
    key_heads = key_part.reshape(row_count, heads_here, HEAD_DIM)
    val_heads = val_part.reshape(row_count, heads_here, HEAD_DIM)
    scores = (
        jnp.einsum("qhd,khd->hqk", query_heads, key_heads, preferred_element_type=jnp.float32)
        * inv_root
    )
    new_max = jnp.max(scores, -1)
    factor = jnp.exp(run_max - new_max)
    weights = jnp.exp(scores - new_max[..., None])
    run_sum = run_sum * factor + jnp.sum(weights, -1)
    accum = accum * jnp.transpose(factor)[..., None] + jnp.einsum(
        "hqk,khd->qhd", weights.astype(jnp.bfloat16), val_heads, preferred_element_type=jnp.float32
    )
    run_max, run_sum, accum = (new_max, run_sum, accum)
    joined_attn = (
        (accum / jnp.transpose(run_sum)[..., None])
        .reshape(col_rows, attn_width)
        .astype(jnp.bfloat16)
    )
    joined_all = lax.all_gather(joined_attn, "cols", axis=0, tiled=True)
    result = lax.psum_scatter(
        jnp.dot(joined_all, join_out, preferred_element_type=jnp.float32),
        "rows",
        scatter_dimension=0,
        tiled=True,
    )
    return (layer_own.astype(jnp.float32) + result).astype(jnp.bfloat16)


VMEM_BYTES = 48 * 1024 * 1024


def flip(array, mask):
    size = lax.axis_size("cols")
    return lax.ppermute(array, "cols", [(i, i ^ mask) for i in range(size)])


def core_swap(array):
    return flip(array, 1)


def y_swap(array):
    return flip(array, 2)


def row_shift(array, shift):
    size = lax.axis_size("rows")
    return lax.ppermute(array, "rows", [(i, (i + shift) % size) for i in range(size)])


class Runner:
    def __init__(self, position):
        self.position = position

    def __call__(self, kernel, grid, operands, in_specs, out_shape, out_spec):
        return pl.pallas_call(
            kernel,
            out_shape=out_shape,
            grid_spec=pltpu.PrefetchScalarGridSpec(
                num_scalar_prefetch=1, grid=grid, in_specs=list(in_specs), out_specs=out_spec
            ),
            compiler_params=pltpu.CompilerParams(vmem_limit_bytes=VMEM_BYTES),
            cost_estimate=pl.CostEstimate(flops=1, bytes_accessed=1, transcendentals=0),
        )(self.position, *operands)


def joined_rows(refs, at=slice(None)):
    return jnp.concatenate([ref[:, at] for ref in refs])


def store_rows(refs, at, values):
    piece = values.shape[0] // len(refs)
    for j, ref in enumerate(refs):
        ref[:, at] = values[j * piece : (j + 1) * piece].astype(ref.dtype)


def whole(array):
    return pl.BlockSpec(array.shape, lambda s, pos: (0,) * array.ndim)


def mine_of(pos):
    return 2 * pos[0] + pos[1]


def across_of(pos):
    return 2 * pos[0] + 1 - pos[1]


def dot_f32(a, b):
    return jnp.dot(a, b, preferred_element_type=jnp.float32)


def project_send(run, tokens, weights, width, sub):
    rows, depth = tokens.shape
    block = width // sub
    wide = len(weights) * block

    def kernel(pos, tokens_ref, *refs):
        for i in range(len(weights)):
            refs[-1][:, i * block : (i + 1) * block] = dot_f32(
                tokens_ref[...], refs[i][...]
            ).astype(jnp.bfloat16)

    spec = pl.BlockSpec((depth, block), lambda s, pos: (0, 2 * (1 - pos[0]) * sub + s))
    return run(
        kernel,
        (2 * sub,),
        (tokens, *weights),
        (whole(tokens), *[spec] * len(weights)),
        jax.ShapeDtypeStruct((rows, 2 * sub * wide), jnp.bfloat16),
        pl.BlockSpec((rows, wide), lambda s, pos: (0, s)),
    )


def project_across(run, tokens, weights, width, sub, arrived, pieces=1):
    rows, depth = tokens.shape
    block = width // sub
    wide = len(weights) * block

    def kernel(pos, tokens_ref, *refs):
        for i in range(len(weights)):
            at = slice(i * block, (i + 1) * block)
            part = dot_f32(tokens_ref[...], refs[i][...])
            part = part + refs[len(weights)][:, at].astype(jnp.float32)
            store_rows(refs[len(weights) + 1 :], at, part)

    spec = pl.BlockSpec((depth, block), lambda s, pos: (0, across_of(pos) * sub + s))
    return run(
        kernel,
        (sub,),
        (tokens, *weights, arrived),
        (
            whole(tokens),
            *[spec] * len(weights),
            pl.BlockSpec((rows, wide), lambda s, pos: (0, (1 - pos[1]) * sub + s)),
        ),
        (jax.ShapeDtypeStruct((rows // pieces, sub * wide), jnp.bfloat16),) * pieces,
        (pl.BlockSpec((rows // pieces, wide), lambda s, pos: (0, s)),) * pieces,
    )


def project_hidden(run, tokens, weight, bias, width, sub, arrived, from_side, at=0):
    depth = tokens.shape[1]
    rows = from_side.shape[0]
    block = width // sub

    def kernel(pos, tokens_ref, weight_ref, bias_ref, arrived_ref, side_ref, out_ref):
        total = dot_f32(tokens_ref[...], weight_ref[...])
        total = total + arrived_ref[...].astype(jnp.float32) + side_ref[...].astype(jnp.float32)
        total = total + bias_ref[...]
        out_ref[...] = (total * (1.0 + lax.erf(total * math.sqrt(0.5))) * 0.5).astype(jnp.bfloat16)

    return run(
        kernel,
        (sub,),
        (tokens, weight, bias, arrived, from_side),
        (
            pl.BlockSpec((rows, depth), lambda s, pos: (at, 0)),
            pl.BlockSpec((depth, block), lambda s, pos: (0, mine_of(pos) * sub + s)),
            pl.BlockSpec((1, block), lambda s, pos: (0, mine_of(pos) * sub + s)),
            pl.BlockSpec((rows, block), lambda s, pos: (at, pos[1] * sub + s)),
            pl.BlockSpec((rows, block), lambda s, pos: (0, s)),
        ),
        jax.ShapeDtypeStruct((rows, width), jnp.bfloat16),
        pl.BlockSpec((rows, block), lambda s, pos: (0, s)),
    )


def project_keep(run, tokens, weights, width, arrived):
    rows, depth = tokens.shape
    wide = len(weights) * width

    def kernel(pos, tokens_ref, *refs):
        arrived_ref, out_ref = refs[len(weights) :]
        for i in range(len(weights)):
            at = slice(i * width, (i + 1) * width)
            part = dot_f32(tokens_ref[...], refs[i][...])
            out_ref[:, at] = part + arrived_ref[:, at].astype(jnp.float32)

    spec = pl.BlockSpec((depth, width), lambda s, pos: (0, mine_of(pos)))
    return run(
        kernel,
        (1,),
        (tokens, *weights, arrived),
        (
            whole(tokens),
            *[spec] * len(weights),
            pl.BlockSpec((rows, wide), lambda s, pos: (0, pos[1])),
        ),
        jax.ShapeDtypeStruct((rows, wide), jnp.float32),
        pl.BlockSpec((rows, wide), lambda s, pos: (0, 0)),
    )


def unit_norm(values, scales):
    row_mean = jnp.mean(values, -1, keepdims=True)
    row_var = jnp.mean(values * values, -1, keepdims=True) - row_mean * row_mean
    return ((values - row_mean) * lax.rsqrt(row_var + EPS) * scales).astype(jnp.bfloat16)


def softmax_blend(query, key, value, keep=None):
    scores = lax.dot_general(
        query, key, (((1,), (1,)), ((), ())), preferred_element_type=jnp.float32
    ) * (1.0 / math.sqrt(HEAD_DIM))
    if keep is not None:
        scores = jnp.where(keep, scores, -jnp.inf)
    weights = jnp.exp(scores - jnp.max(scores, -1, keepdims=True))
    row_sum = jnp.sum(weights, -1, keepdims=True)
    blended = dot_f32(weights.astype(jnp.bfloat16), value)
    return (blended / row_sum).astype(jnp.bfloat16)


def project_heads(run, tokens, weights, scales, width, arrived, from_side, attend_camera):
    rows, depth = tokens.shape
    heads = width // HEAD_DIM
    out_width = width if attend_camera else 3 * width

    def kernel(pos, tokens_ref, *refs):
        weight_refs, scale_refs = refs[:3], refs[3:5]
        arrived_ref, *side_refs, out_ref = refs[5:]
        raws = []
        for i in range(3):
            at = slice(i * width, (i + 1) * width)
            raw = dot_f32(tokens_ref[...], weight_refs[i][...])
            raw = raw + arrived_ref[:, at].astype(jnp.float32)
            raws.append(raw + joined_rows(side_refs, at).astype(jnp.float32))
        if attend_camera:
            row_cam = lax.broadcasted_iota(jnp.int32, (rows, rows), 0) // TOK_CAM
            col_cam = lax.broadcasted_iota(jnp.int32, (rows, rows), 1) // TOK_CAM
            same = row_cam == col_cam
        for h in range(heads):
            at = slice(h * HEAD_DIM, (h + 1) * HEAD_DIM)
            query = unit_norm(raws[0][:, at], scale_refs[0][:, at])
            key = unit_norm(raws[1][:, at], scale_refs[1][:, at])
            value = raws[2][:, at].astype(jnp.bfloat16)
            if attend_camera:
                out_ref[:, at] = softmax_blend(query, key, value, same)
            else:
                out_ref[:, at] = query
                out_ref[:, width + h * HEAD_DIM : width + (h + 1) * HEAD_DIM] = key
                out_ref[:, 2 * width + h * HEAD_DIM : 2 * width + (h + 1) * HEAD_DIM] = value

    weight_spec = pl.BlockSpec((depth, width), lambda s, pos: (0, mine_of(pos)))
    scale_spec = pl.BlockSpec((1, width), lambda s, pos: (0, mine_of(pos)))
    return run(
        kernel,
        (1,),
        (tokens, *weights, *scales, arrived, *from_side),
        (
            whole(tokens),
            *[weight_spec] * 3,
            *[scale_spec] * 2,
            pl.BlockSpec((rows, 3 * width), lambda s, pos: (0, pos[1])),
            *[whole(piece) for piece in from_side],
        ),
        jax.ShapeDtypeStruct((rows, out_width), jnp.bfloat16),
        pl.BlockSpec((rows, out_width), lambda s, pos: (0, 0)),
    )


def contract(run, parts, weight, sub, first=0, start=None):
    rows = sum(piece.shape[0] for piece in parts[0])
    width = parts[0][0].shape[1]
    count, pieces = len(parts), len(parts[0])
    out_width = weight.shape[1]
    block = width // sub

    def kernel(pos, weight_ref, *refs):
        out_ref = refs[-1]
        step = pl.program_id(0)
        for i in range(count):

            @pl.when(step // sub == i)
            def _(i=i):
                part = joined_rows(refs[i * pieces : (i + 1) * pieces])
                term = dot_f32(part, weight_ref[...])
                if i > 0:
                    out_ref[...] += term
                elif sub == 1:
                    out_ref[...] = term if start is None else term + refs[-2][...]
                else:

                    @pl.when(step == 0)
                    def _():
                        out_ref[...] = term if start is None else term + refs[-2][...]

                    @pl.when(step > 0)
                    def _():
                        out_ref[...] += term

    def weight_block(s, pos):
        i = s // sub + first
        return (2 * (pos[0] ^ (i & 1)) + (pos[1] ^ (i >> 1))) * sub + s % sub, 0

    def part_spec(i):
        return pl.BlockSpec(
            (rows // pieces, block), lambda s, pos: (0, jnp.clip(s - i * sub, 0, sub - 1))
        )

    operands = [weight, *[piece for part in parts for piece in part]]
    in_specs = [pl.BlockSpec((block, out_width), weight_block)]
    in_specs += [part_spec(i) for i in range(count) for _ in range(pieces)]
    if start is not None:
        operands.append(start)
        in_specs.append(whole(start))
    return run(
        kernel,
        (count * sub,),
        operands,
        in_specs,
        jax.ShapeDtypeStruct((rows, out_width), jnp.float32),
        pl.BlockSpec((rows, out_width), lambda s, pos: (0, 0)),
    )


def join_blend(run, parts, kept, from_side, scales):
    rows = parts.shape[0] + kept.shape[0]
    heads = parts.shape[1] // 3 // HEAD_DIM

    def kernel(pos, *refs):
        part_refs, kept_refs, side_refs = refs[:3], refs[3:6], refs[6:9]
        *scale_refs, out_ref = refs[9:]
        raws = [k[...] + s[...].astype(jnp.float32) for k, s in zip(kept_refs, side_refs)]
        late = [unit_norm(raws[i], scale_refs[i][...]) for i in range(2)]
        late.append(raws[2].astype(jnp.bfloat16))
        query, key, value = (
            jnp.concatenate((part_refs[i][...], late[i])) for i in range(3)
        )
        out_ref[...] = softmax_blend(query, key, value)

    def specs(array):
        return [
            pl.BlockSpec((array.shape[0], HEAD_DIM), lambda h, pos, i=i: (0, i * heads + h))
            for i in range(3)
        ]

    scale_spec = pl.BlockSpec((1, HEAD_DIM), lambda h, pos: (0, mine_of(pos) * heads + h))
    return run(
        kernel,
        (heads,),
        (*[parts] * 3, *[kept] * 3, *[from_side] * 3, *scales),
        (*specs(parts), *specs(kept), *specs(from_side), *[scale_spec] * 2),
        jax.ShapeDtypeStruct((rows, heads * HEAD_DIM), jnp.bfloat16),
        pl.BlockSpec((rows, HEAD_DIM), lambda h, pos: (0, h)),
    )


def moment_pair(values):
    return jnp.stack((jnp.sum(values, 1), jnp.sum(values * values, 1)))


def moment_flips(pair):
    return pair, flip(pair, 1), flip(pair, 2), flip(pair, 3)


def moment_sum(pairs):
    return (pairs[0] + pairs[1]) + (pairs[2] + pairs[3])


def sent(array, shift):
    return row_shift(array.astype(jnp.bfloat16), shift)


def moment_shards(total):
    return total, row_shift(total, 1), row_shift(total, -1), row_shift(total, 2)


def normed_shards(shards, scales, totals):
    return jnp.concatenate(
        [normalize(x.astype(jnp.float32), scales, m) for x, m in zip(shards, totals)]
    )


def sync(*values):
    return lax.optimization_barrier(values)


def scatter_rows(terms):
    own, before, after, away = jnp.split(terms, 4)
    half = own.shape[0] // 2

    def send(array, shift):
        return sent(array, shift).astype(jnp.float32)

    to_after = send(away[:half], 1)
    to_before = send(away[half:], -1)
    from_before = jnp.concatenate((send(after[:half] + to_after, 1), send(after[half:], 1)))
    from_after = jnp.concatenate((send(before[:half], -1), send(before[half:] + to_before, -1)))
    return own + from_before + from_after


def fast_body(
    camera_tokens,
    norm_gain,
    query_weight,
    key_weight,
    value_weight,
    query_gain,
    key_gain,
    out_weight,
    up_weight,
    up_bias,
    down_weight,
    down_bias,
    join_gain,
    join_query,
    join_key,
    join_value,
    join_query_gain,
    join_key_gain,
    join_out,
):
    half = TOK_CAM
    index = lax.axis_index("cols")
    run = Runner(jnp.stack((index & 1, index >> 1)).astype(jnp.int32))
    head_width = query_weight.shape[1] // 4
    unit_width = up_weight.shape[1] // 4
    sub = 2 if unit_width % 256 == 0 else 1
    heads_in = (query_weight, key_weight, value_weight)
    join_in = (join_query, join_key, join_value)
    scales = (query_gain[None], key_gain[None])
    join_scales = (join_query_gain[None], join_key_gain[None])
    bias = up_bias[None]

    def heads_send(tokens, weights):
        return project_send(run, tokens, weights, head_width, 1)

    def heads_across(tokens, weights, arrived, pieces=1):
        return project_across(run, tokens, weights, head_width, 1, arrived, pieces)

    def heads_out(parts, first=0, start=None):
        return contract(run, [(part,) for part in parts], out_weight, 1, first, start)

    def units_down(parts, first, start):
        return contract(run, parts, down_weight, 1 if len(parts) > 1 else 2, first, start)

    def units_send(tokens):
        return project_send(run, tokens, (up_weight,), unit_width, 1)

    def units_across(tokens, arrived, pieces):
        return project_across(run, tokens, (up_weight,), unit_width, sub, arrived, pieces)

    def units_end(tokens, arrived, side, at=0):
        return project_hidden(run, tokens, up_weight, bias, unit_width, sub, arrived, side, at)

    def layer_end(start, own, *arrived):
        total = own
        for term in arrived:
            total = total + term.astype(jnp.float32)
        return (start + total + down_bias).astype(jnp.bfloat16)

    start_f32 = camera_tokens.astype(jnp.float32)
    own_a, own_b = camera_tokens[:half], camera_tokens[half:]
    pairs = moment_flips(moment_pair(start_f32))
    own_a, own_b, a_before, a_after, *pairs = sync(
        own_a, own_b, sent(own_a, 1), sent(own_a, -1), *pairs
    )

    totals = moment_shards(moment_sum(pairs))
    own_a, own_b, a_before, a_after, a_away, *totals = sync(
        own_a, own_b, a_before, a_after, sent(a_before, 1), *totals
    )
    totals_a = [total[:, :half] for total in totals]
    totals_b = [total[:, half:] for total in totals]

    b_before = sent(own_b, 1)
    tok_a = normed_shards((own_a, a_before, a_after, a_away), norm_gain, totals_a)
    qs_a = heads_send(tok_a, heads_in)
    tok_a, own_b, b_before, qs_a = sync(tok_a, own_b, b_before, qs_a)

    b_after, qc_a = sent(own_b, -1), core_swap(qs_a)
    qx_a = heads_across(tok_a, heads_in, qc_a, 2)
    tok_a, own_b, b_before, b_after, qc_a, qx_a0, qx_a1 = sync(
        tok_a, own_b, b_before, b_after, qc_a, *qx_a
    )

    qy_a0 = y_swap(qx_a0)
    us_a = units_send(tok_a)
    tok_a, own_b, b_before, b_after, qc_a, us_a, qy_a0, qx_a1 = sync(
        tok_a, own_b, b_before, b_after, qc_a, us_a, qy_a0, qx_a1
    )

    uc_a, qy_a1, b_away = core_swap(us_a), y_swap(qx_a1), sent(b_before, 1)
    (ux_a,) = units_across(tok_a, uc_a, 1)
    tok_a, qc_a, uc_a, ux_a, qy_a0, qy_a1, own_b, b_before, b_after, b_away = sync(
        tok_a, qc_a, uc_a, ux_a, qy_a0, qy_a1, own_b, b_before, b_after, b_away
    )

    uy_a = y_swap(ux_a)
    tok_b = normed_shards((own_b, b_before, b_after, b_away), norm_gain, totals_b)
    qs_b = heads_send(tok_b, heads_in)
    us_b = units_send(tok_b)
    at_a = project_heads(run, tok_a, heads_in, scales, head_width, qc_a, (qy_a0, qy_a1), True)
    tok_a, tok_b, qs_b, us_b, at_a, uc_a, uy_a = sync(
        tok_a, tok_b, qs_b, us_b, at_a, uc_a, uy_a
    )

    at_ya, at_ca, qc_b, uc_b = y_swap(at_a), core_swap(at_a), core_swap(qs_b), core_swap(us_b)
    hd_a = units_end(tok_a, uc_a, uy_a)
    tok_b, at_a, at_ya, at_ca, qc_b, uc_b, hd_a = sync(
        tok_b, at_a, at_ya, at_ca, qc_b, uc_b, hd_a
    )

    hd_ya, hd_ca, at_fa = y_swap(hd_a), core_swap(hd_a), core_swap(at_ya)
    (qx_b,) = heads_across(tok_b, heads_in, qc_b)
    ux_b = units_across(tok_b, uc_b, 2)
    mixed_a = units_down(((hd_a,),), 0, heads_out((at_a, at_ca, at_ya)))
    tok_b, at_fa, hd_ya, hd_ca, qc_b, uc_b, qx_b, mixed_a, *ux_b = sync(
        tok_b, at_fa, hd_ya, hd_ca, qc_b, uc_b, qx_b, mixed_a, *ux_b
    )

    qy_b, hd_fa = y_swap(qx_b), core_swap(hd_ya)
    mixed_a = heads_out((at_fa,), 3, mixed_a)
    mixed_a = units_down(((hd_ca,), (hd_ya,), (hd_fa,)), 1, mixed_a)
    tok_b, mixed_a, qc_b, qy_b, uc_b, ux_b0, ux_b1 = sync(
        tok_b, mixed_a, qc_b, qy_b, uc_b, *ux_b
    )

    uy_b0 = y_swap(ux_b0)
    mine_a, before_a, after_a, away_a = jnp.split(mixed_a, 4)
    to_after = sent(away_a, 1)
    at_b = project_heads(run, tok_b, heads_in, scales, head_width, qc_b, (qy_b,), True)
    tok_b, uc_b, uy_b0, ux_b1, at_b, mine_a, before_a, after_a, to_after = sync(
        tok_b, uc_b, uy_b0, ux_b1, at_b, mine_a, before_a, after_a, to_after
    )

    from_before = sent(after_a + to_after.astype(jnp.float32), 1)
    from_after = sent(before_a, -1)
    uy_b1, at_yb, at_cb = y_swap(ux_b1), y_swap(at_b), core_swap(at_b)
    hd_b0 = units_end(tok_b, uc_b, uy_b0)
    mixed_b = heads_out((at_b, at_cb))
    tok_b, uc_b, uy_b1, hd_b0, at_yb, mixed_b, mine_a, *arrived = sync(
        tok_b, uc_b, uy_b1, hd_b0, at_yb, mixed_b, mine_a, from_before, from_after
    )

    hd_yb0, at_fb = y_swap(hd_b0), core_swap(at_yb)
    layer_a = layer_end(start_f32[:half], mine_a, *arrived)
    pairs = moment_flips(moment_pair(layer_a.astype(jnp.float32)))
    hd_b1 = units_end(tok_b, uc_b, uy_b1, 1)
    mixed_b = heads_out((at_yb, at_fb), 2, mixed_b)
    hd_b0, hd_b1, hd_yb0, mixed_b, layer_a, *pairs = sync(
        hd_b0, hd_b1, hd_yb0, mixed_b, layer_a, *pairs
    )

    hd_yb1, hd_cb0, hd_cb1 = y_swap(hd_b1), core_swap(hd_b0), core_swap(hd_b1)
    join_a = normalize(layer_a.astype(jnp.float32), join_gain, moment_sum(pairs))
    ja_before, ja_after = sent(join_a, 1), sent(join_a, -1)
    mixed_b = units_down(((hd_b0, hd_b1),), 0, mixed_b)
    hd_cb0, hd_cb1, hd_yb0, hd_yb1, mixed_b, layer_a, join_a, ja_before, ja_after = sync(
        hd_cb0, hd_cb1, hd_yb0, hd_yb1, mixed_b, layer_a, join_a, ja_before, ja_after
    )

    hd_fb0 = core_swap(hd_yb0)
    hd_fb1 = core_swap(hd_yb1)
    mixed_b = units_down(((hd_cb0, hd_cb1),), 1, mixed_b)
    hd_yb0, hd_yb1, hd_fb0, hd_fb1, mixed_b, join_a, ja_before, ja_after = sync(
        hd_yb0, hd_yb1, hd_fb0, hd_fb1, mixed_b, join_a, ja_before, ja_after
    )

    ja_away = sent(ja_before, 1)
    mixed_b = units_down(((hd_yb0, hd_yb1), (hd_fb0, hd_fb1)), 2, mixed_b)
    mixed_b, join_a, ja_before, ja_after, ja_away = sync(
        mixed_b, join_a, ja_before, ja_after, ja_away
    )

    mine_b, before_b, after_b, away_b = jnp.split(mixed_b, 4)
    to_after = sent(away_b, 1)
    mine_b, before_b, after_b, to_after, join_a, ja_before, ja_after, ja_away = sync(
        mine_b, before_b, after_b, to_after, join_a, ja_before, ja_after, ja_away
    )

    from_before = sent(after_b + to_after.astype(jnp.float32), 1)
    from_after = sent(before_b, -1)
    tok_ja = jnp.concatenate((join_a, ja_before, ja_after, ja_away))
    js_a = heads_send(tok_ja, join_in)
    tok_ja, js_a, mine_b, *arrived = sync(tok_ja, js_a, mine_b, from_before, from_after)

    layer_b = layer_end(start_f32[half:], mine_b, *arrived)
    pairs = moment_flips(moment_pair(layer_b.astype(jnp.float32)))
    jb_before, jb_after, jc_a = sent(layer_b, 1), sent(layer_b, -1), core_swap(js_a)
    jx_a = heads_across(tok_ja, join_in, jc_a, 2)
    tok_ja, jc_a, jx_a0, jx_a1, layer_b, jb_before, jb_after, *pairs = sync(
        tok_ja, jc_a, *jx_a, layer_b, jb_before, jb_after, *pairs
    )

    totals = moment_shards(moment_sum(pairs))

    jb_away = sent(jb_before, 1)
    jy_a0 = y_swap(jx_a0)
    tok_ja, jc_a, jy_a0, jx_a1, layer_b, jb_before, jb_after, jb_away, *totals = sync(
        tok_ja, jc_a, jy_a0, jx_a1, layer_b, jb_before, jb_after, jb_away, *totals
    )

    jy_a1 = y_swap(jx_a1)
    tok_jb = normed_shards((layer_b, jb_before, jb_after, jb_away), join_gain, totals)
    jc_b = core_swap(heads_send(tok_jb, join_in))
    (jx_b,) = heads_across(tok_jb, join_in, jc_b)
    tok_ja, jc_a, jy_a0, jy_a1, tok_jb, jc_b, jx_b = sync(
        tok_ja, jc_a, jy_a0, jy_a1, tok_jb, jc_b, jx_b
    )

    jy_b = y_swap(jx_b)
    parts_a = project_heads(
        run, tok_ja, join_in, join_scales, head_width, jc_a, (jy_a0, jy_a1), False
    )
    kept_b = project_keep(run, tok_jb, join_in, head_width, jc_b)
    jy_b, parts_a, kept_b = sync(jy_b, parts_a, kept_b)

    joined = join_blend(run, parts_a, kept_b, jy_b, join_scales)
    joined = joined.reshape(2, 4, half, head_width).swapaxes(0, 1).reshape(8 * half, head_width)
    jo_y, jo_c = y_swap(joined), core_swap(joined)
    jo_f = core_swap(jo_y)
    result = contract(run, ((joined,), (jo_c,), (jo_y,), (jo_f,)), join_out, 1)
    summed = scatter_rows(result)
    layer_own = jnp.concatenate((layer_a, layer_b))
    return (layer_own.astype(jnp.float32) + summed).astype(jnp.bfloat16)


def layer(*arrays):
    own_rows, heads_width = arrays[0].shape[0], arrays[2].shape[1]
    fits = lax.axis_size("cols") == 4 and lax.axis_size("rows") == 4
    fits = fits and own_rows == 2 * TOK_CAM and heads_width % (4 * HEAD_DIM) == 0
    return (fast_body if fits else generic_body)(*arrays)


def solution(mesh):
    in_specs = (
        P(("groups", "rows"), "cols"),
        P("cols"),
        P("cols", "rows"),
        P("cols", "rows"),
        P("cols", "rows"),
        P("rows"),
        P("rows"),
        P("rows", "cols"),
        P("cols", "rows"),
        P("rows"),
        P("rows", "cols"),
        P("cols"),
        P("cols"),
        P("cols", "rows"),
        P("cols", "rows"),
        P("cols", "rows"),
        P("rows"),
        P("rows"),
        P("rows", "cols"),
    )
    out_specs = P(("groups", "rows"), "cols")
    return jax.shard_map(layer, mesh=mesh, in_specs=in_specs, out_specs=out_specs, check_vma=False)
```

```python
import math

import jax
import jax.numpy as jnp
from jax import lax
from jax.experimental import pallas as pl
from jax.experimental.pallas import tpu as pltpu
from jax.sharding import PartitionSpec as P

HEAD_DIM = 128
TOK_CAM = 64
D = 6144


EPS = 1e-06


def partner_2(array, axis, bit):
    return lax.ppermute(array, axis, [(i, i ^ 1 << bit) for i in range(lax.axis_size(axis))])


def normalize(values, scales, moments):
    row_mean = moments[0] / D
    row_var = moments[1] / D - row_mean * row_mean
    return ((values - row_mean[:, None]) * lax.rsqrt(row_var[:, None] + EPS) * scales).astype(
        jnp.bfloat16
    )


def shard_moments(values):
    return lax.psum((jnp.sum(values, 1), jnp.sum(values * values, 1)), "cols")


def head_norm(values, scales):
    row_count = values.shape[0]
    grouped = values.reshape(row_count, -1, HEAD_DIM)
    row_mean = jnp.mean(grouped, -1, keepdims=True)
    row_var = jnp.mean(grouped * grouped, -1, keepdims=True) - row_mean * row_mean
    normed = (grouped - row_mean) * lax.rsqrt(row_var + EPS)
    return (normed.reshape(row_count, -1) * scales).astype(jnp.bfloat16)


def attend(queries, key_rows, val_rows):
    inv_root = 1.0 / math.sqrt(HEAD_DIM)
    scores = (
        jnp.einsum("bqhd,bkhd->bhqk", queries, key_rows, preferred_element_type=jnp.float32)
        * inv_root
    )
    row_max = jnp.max(scores, -1, keepdims=True)
    weights = jnp.exp(scores - row_max)
    row_sum = jnp.sum(weights, -1)
    blended = jnp.einsum(
        "bhqk,bkhd->bqhd",
        weights.astype(jnp.bfloat16),
        val_rows,
        preferred_element_type=jnp.float32,
    )
    return blended / jnp.transpose(row_sum, (0, 2, 1))[..., None]


def to_heads(matrix, blocks):
    return matrix.reshape(blocks, -1, matrix.shape[1] // HEAD_DIM, HEAD_DIM)


def camera_attention(queries, key_rows, val_rows):
    local_rows = queries.shape[0]
    if local_rows >= TOK_CAM:
        blocks = local_rows // TOK_CAM
        result = attend(
            to_heads(queries, blocks), to_heads(key_rows, blocks), to_heads(val_rows, blocks)
        )
    else:
        cam_span = TOK_CAM // local_rows
        position = lax.axis_index("cols")
        key_value = jnp.stack((key_rows, val_rows))
        for which_bit in range(cam_span.bit_length() - 1):
            partner = partner_2(key_value, "cols", which_bit)
            is_lower = position >> which_bit & 1 == 0
            key_value = jnp.where(
                is_lower,
                jnp.concatenate((key_value, partner), 1),
                jnp.concatenate((partner, key_value), 1),
            )
        result = attend(to_heads(queries, 1), to_heads(key_value[0], 1), to_heads(key_value[1], 1))
    return result.reshape(local_rows, -1).astype(jnp.bfloat16)


def generic_body(
    camera_tokens,
    norm_gain,
    query_weight,
    key_weight,
    value_weight,
    query_gain,
    key_gain,
    out_weight,
    up_weight,
    up_bias,
    down_weight,
    down_bias,
    join_gain,
    join_query,
    join_key,
    join_value,
    join_query_gain,
    join_key_gain,
    join_out,
):
    own_rows = camera_tokens.shape[0]
    all_rows = own_rows * lax.axis_size("rows")
    col_rows = all_rows // lax.axis_size("cols")
    attn_width = query_weight.shape[1]
    start_f32 = camera_tokens.astype(jnp.float32)
    normed_all = lax.all_gather(
        normalize(start_f32, norm_gain, shard_moments(start_f32)), "rows", axis=0, tiled=True
    )
    joint_weight = jnp.concatenate((query_weight, key_weight, value_weight, up_weight), 1)
    joint = lax.psum_scatter(
        jnp.dot(normed_all, joint_weight, preferred_element_type=jnp.float32),
        "cols",
        scatter_dimension=0,
        tiled=True,
    )
    up_sum = joint[:, 3 * attn_width :]
    hidden = jax.nn.gelu(up_sum + up_bias, approximate=False).astype(jnp.bfloat16)
    attended = camera_attention(
        head_norm(joint[:, :attn_width], query_gain),
        head_norm(joint[:, attn_width : 2 * attn_width], key_gain),
        joint[:, 2 * attn_width : 3 * attn_width].astype(jnp.bfloat16),
    )
    attn_all, hidden_all = (
        lax.all_gather(attended, "cols", axis=0, tiled=True),
        lax.all_gather(hidden, "cols", axis=0, tiled=True),
    )
    mixed = lax.psum_scatter(
        jnp.dot(attn_all, out_weight, preferred_element_type=jnp.float32)
        + jnp.dot(hidden_all, down_weight, preferred_element_type=jnp.float32),
        "rows",
        scatter_dimension=0,
        tiled=True,
    )
    layer_own = (start_f32 + mixed + down_bias).astype(jnp.bfloat16)
    layer_f32 = layer_own.astype(jnp.float32)
    join_in = lax.all_gather(
        normalize(layer_f32, join_gain, shard_moments(layer_f32)), "rows", axis=0, tiled=True
    )
    join_weight = jnp.concatenate((join_query, join_key, join_value), 1)
    join_joint = lax.psum_scatter(
        jnp.dot(join_in, join_weight, preferred_element_type=jnp.float32),
        "cols",
        scatter_dimension=0,
        tiled=True,
    )
    join_q = head_norm(join_joint[:, :attn_width], join_query_gain)
    join_k = head_norm(join_joint[:, attn_width : 2 * attn_width], join_key_gain)
    join_v = join_joint[:, 2 * attn_width :].astype(jnp.bfloat16)
    heads_here = attn_width // HEAD_DIM
    query_heads = join_q.reshape(col_rows, heads_here, HEAD_DIM)
    inv_root = 1.0 / math.sqrt(HEAD_DIM)
    run_max = jnp.full((heads_here, col_rows), -jnp.inf, jnp.float32)
    run_sum = jnp.zeros((heads_here, col_rows), jnp.float32)
    accum = jnp.zeros((col_rows, heads_here, HEAD_DIM), jnp.float32)
    key_part = lax.all_gather(join_k, "cols", axis=0, tiled=True)
    val_part = lax.all_gather(join_v, "cols", axis=0, tiled=True)
    row_count = key_part.shape[0]
    key_heads = key_part.reshape(row_count, heads_here, HEAD_DIM)
    val_heads = val_part.reshape(row_count, heads_here, HEAD_DIM)
    scores = (
        jnp.einsum("qhd,khd->hqk", query_heads, key_heads, preferred_element_type=jnp.float32)
        * inv_root
    )
    new_max = jnp.max(scores, -1)
    factor = jnp.exp(run_max - new_max)
    weights = jnp.exp(scores - new_max[..., None])
    run_sum = run_sum * factor + jnp.sum(weights, -1)
    accum = accum * jnp.transpose(factor)[..., None] + jnp.einsum(
        "hqk,khd->qhd", weights.astype(jnp.bfloat16), val_heads, preferred_element_type=jnp.float32
    )
    run_max, run_sum, accum = (new_max, run_sum, accum)
    joined_attn = (
        (accum / jnp.transpose(run_sum)[..., None])
        .reshape(col_rows, attn_width)
        .astype(jnp.bfloat16)
    )
    joined_all = lax.all_gather(joined_attn, "cols", axis=0, tiled=True)
    result = lax.psum_scatter(
        jnp.dot(joined_all, join_out, preferred_element_type=jnp.float32),
        "rows",
        scatter_dimension=0,
        tiled=True,
    )
    return (layer_own.astype(jnp.float32) + result).astype(jnp.bfloat16)


VMEM_BYTES = 48 * 1024 * 1024


def flip(array, mask):
    size = lax.axis_size("cols")
    return lax.ppermute(array, "cols", [(i, i ^ mask) for i in range(size)])


def core_swap(array):
    return flip(array, 1)


def y_swap(array):
    return flip(array, 2)


def row_shift(array, shift):
    size = lax.axis_size("rows")
    return lax.ppermute(array, "rows", [(i, (i + shift) % size) for i in range(size)])


class Runner:
    def __init__(self, position):
        self.position = position

    def __call__(self, kernel, grid, operands, in_specs, out_shape, out_spec):
        return pl.pallas_call(
            kernel,
            out_shape=out_shape,
            grid_spec=pltpu.PrefetchScalarGridSpec(
                num_scalar_prefetch=1, grid=grid, in_specs=list(in_specs), out_specs=out_spec
            ),
            compiler_params=pltpu.CompilerParams(vmem_limit_bytes=VMEM_BYTES),
            cost_estimate=pl.CostEstimate(flops=1, bytes_accessed=1, transcendentals=0),
        )(self.position, *operands)


def joined_rows(refs, at=slice(None)):
    return jnp.concatenate([ref[:, at] for ref in refs])


def store_rows(refs, at, values):
    piece = values.shape[0] // len(refs)
    for j, ref in enumerate(refs):
        ref[:, at] = values[j * piece : (j + 1) * piece].astype(ref.dtype)


def whole(array):
    return pl.BlockSpec(array.shape, lambda s, pos: (0,) * array.ndim)


def mine_of(pos):
    return 2 * pos[0] + pos[1]


def across_of(pos):
    return 2 * pos[0] + 1 - pos[1]


def dot_f32(a, b):
    return jnp.dot(a, b, preferred_element_type=jnp.float32)


def project_send(run, tokens, weights, width, sub):
    rows, depth = tokens.shape
    block = width // sub
    wide = len(weights) * block

    def kernel(pos, tokens_ref, *refs):
        for i in range(len(weights)):
            refs[-1][:, i * block : (i + 1) * block] = dot_f32(
                tokens_ref[...], refs[i][...]
            ).astype(jnp.bfloat16)

    spec = pl.BlockSpec((depth, block), lambda s, pos: (0, 2 * (1 - pos[0]) * sub + s))
    return run(
        kernel,
        (2 * sub,),
        (tokens, *weights),
        (whole(tokens), *[spec] * len(weights)),
        jax.ShapeDtypeStruct((rows, 2 * sub * wide), jnp.bfloat16),
        pl.BlockSpec((rows, wide), lambda s, pos: (0, s)),
    )


def project_across(run, tokens, weights, width, sub, arrived, pieces=1):
    rows, depth = tokens.shape
    block = width // sub
    wide = len(weights) * block

    def kernel(pos, tokens_ref, *refs):
        for i in range(len(weights)):
            at = slice(i * block, (i + 1) * block)
            part = dot_f32(tokens_ref[...], refs[i][...])
            part = part + refs[len(weights)][:, at].astype(jnp.float32)
            store_rows(refs[len(weights) + 1 :], at, part)

    spec = pl.BlockSpec((depth, block), lambda s, pos: (0, across_of(pos) * sub + s))
    return run(
        kernel,
        (sub,),
        (tokens, *weights, arrived),
        (
            whole(tokens),
            *[spec] * len(weights),
            pl.BlockSpec((rows, wide), lambda s, pos: (0, (1 - pos[1]) * sub + s)),
        ),
        (jax.ShapeDtypeStruct((rows // pieces, sub * wide), jnp.bfloat16),) * pieces,
        (pl.BlockSpec((rows // pieces, wide), lambda s, pos: (0, s)),) * pieces,
    )


def project_hidden(run, tokens, weight, bias, width, sub, arrived, from_side, at=0):
    depth = tokens.shape[1]
    rows = from_side.shape[0]
    block = width // sub

    def kernel(pos, tokens_ref, weight_ref, bias_ref, arrived_ref, side_ref, out_ref):
        total = dot_f32(tokens_ref[...], weight_ref[...])
        total = total + arrived_ref[...].astype(jnp.float32) + side_ref[...].astype(jnp.float32)
        total = total + bias_ref[...]
        out_ref[...] = (total * (1.0 + lax.erf(total * math.sqrt(0.5))) * 0.5).astype(jnp.bfloat16)

    return run(
        kernel,
        (sub,),
        (tokens, weight, bias, arrived, from_side),
        (
            pl.BlockSpec((rows, depth), lambda s, pos: (at, 0)),
            pl.BlockSpec((depth, block), lambda s, pos: (0, mine_of(pos) * sub + s)),
            pl.BlockSpec((1, block), lambda s, pos: (0, mine_of(pos) * sub + s)),
            pl.BlockSpec((rows, block), lambda s, pos: (at, pos[1] * sub + s)),
            pl.BlockSpec((rows, block), lambda s, pos: (0, s)),
        ),
        jax.ShapeDtypeStruct((rows, width), jnp.bfloat16),
        pl.BlockSpec((rows, block), lambda s, pos: (0, s)),
    )


def project_keep(run, tokens, weights, width, arrived):
    rows, depth = tokens.shape
    wide = len(weights) * width

    def kernel(pos, tokens_ref, *refs):
        arrived_ref, out_ref = refs[len(weights) :]
        for i in range(len(weights)):
            at = slice(i * width, (i + 1) * width)
            part = dot_f32(tokens_ref[...], refs[i][...])
            out_ref[:, at] = part + arrived_ref[:, at].astype(jnp.float32)

    spec = pl.BlockSpec((depth, width), lambda s, pos: (0, mine_of(pos)))
    return run(
        kernel,
        (1,),
        (tokens, *weights, arrived),
        (
            whole(tokens),
            *[spec] * len(weights),
            pl.BlockSpec((rows, wide), lambda s, pos: (0, pos[1])),
        ),
        jax.ShapeDtypeStruct((rows, wide), jnp.float32),
        pl.BlockSpec((rows, wide), lambda s, pos: (0, 0)),
    )


def unit_norm(values, scales):
    row_mean = jnp.mean(values, -1, keepdims=True)
    row_var = jnp.mean(values * values, -1, keepdims=True) - row_mean * row_mean
    return ((values - row_mean) * lax.rsqrt(row_var + EPS) * scales).astype(jnp.bfloat16)


def softmax_blend(query, key, value, keep=None):
    scores = lax.dot_general(
        query, key, (((1,), (1,)), ((), ())), preferred_element_type=jnp.float32
    ) * (1.0 / math.sqrt(HEAD_DIM))
    if keep is not None:
        scores = jnp.where(keep, scores, -jnp.inf)
    weights = jnp.exp(scores - jnp.max(scores, -1, keepdims=True))
    row_sum = jnp.sum(weights, -1, keepdims=True)
    blended = dot_f32(weights.astype(jnp.bfloat16), value)
    return (blended / row_sum).astype(jnp.bfloat16)


def project_heads(run, tokens, weights, scales, width, arrived, from_side, attend_camera):
    rows, depth = tokens.shape
    heads = width // HEAD_DIM
    out_width = width if attend_camera else 3 * width

    def kernel(pos, tokens_ref, *refs):
        weight_refs, scale_refs = refs[:3], refs[3:5]
        arrived_ref, *side_refs, out_ref = refs[5:]
        raws = []
        for i in range(3):
            at = slice(i * width, (i + 1) * width)
            raw = dot_f32(tokens_ref[...], weight_refs[i][...])
            raw = raw + arrived_ref[:, at].astype(jnp.float32)
            raws.append(raw + joined_rows(side_refs, at).astype(jnp.float32))
        if attend_camera:
            row_cam = lax.broadcasted_iota(jnp.int32, (rows, rows), 0) // TOK_CAM
            col_cam = lax.broadcasted_iota(jnp.int32, (rows, rows), 1) // TOK_CAM
            same = row_cam == col_cam
        for h in range(heads):
            at = slice(h * HEAD_DIM, (h + 1) * HEAD_DIM)
            query = unit_norm(raws[0][:, at], scale_refs[0][:, at])
            key = unit_norm(raws[1][:, at], scale_refs[1][:, at])
            value = raws[2][:, at].astype(jnp.bfloat16)
            if attend_camera:
                out_ref[:, at] = softmax_blend(query, key, value, same)
            else:
                out_ref[:, at] = query
                out_ref[:, width + h * HEAD_DIM : width + (h + 1) * HEAD_DIM] = key
                out_ref[:, 2 * width + h * HEAD_DIM : 2 * width + (h + 1) * HEAD_DIM] = value

    weight_spec = pl.BlockSpec((depth, width), lambda s, pos: (0, mine_of(pos)))
    scale_spec = pl.BlockSpec((1, width), lambda s, pos: (0, mine_of(pos)))
    return run(
        kernel,
        (1,),
        (tokens, *weights, *scales, arrived, *from_side),
        (
            whole(tokens),
            *[weight_spec] * 3,
            *[scale_spec] * 2,
            pl.BlockSpec((rows, 3 * width), lambda s, pos: (0, pos[1])),
            *[whole(piece) for piece in from_side],
        ),
        jax.ShapeDtypeStruct((rows, out_width), jnp.bfloat16),
        pl.BlockSpec((rows, out_width), lambda s, pos: (0, 0)),
    )


def contract(run, parts, weight, sub, first=0, start=None):
    rows = sum(piece.shape[0] for piece in parts[0])
    width = parts[0][0].shape[1]
    count, pieces = len(parts), len(parts[0])
    out_width = weight.shape[1]
    block = width // sub

    def kernel(pos, weight_ref, *refs):
        out_ref = refs[-1]
        step = pl.program_id(0)
        for i in range(count):

            @pl.when(step // sub == i)
            def _(i=i):
                part = joined_rows(refs[i * pieces : (i + 1) * pieces])
                term = dot_f32(part, weight_ref[...])
                if i > 0:
                    out_ref[...] += term
                elif sub == 1:
                    out_ref[...] = term if start is None else term + refs[-2][...]
                else:

                    @pl.when(step == 0)
                    def _():
                        out_ref[...] = term if start is None else term + refs[-2][...]

                    @pl.when(step > 0)
                    def _():
                        out_ref[...] += term

    def weight_block(s, pos):
        i = s // sub + first
        return (2 * (pos[0] ^ (i & 1)) + (pos[1] ^ (i >> 1))) * sub + s % sub, 0

    def part_spec(i):
        return pl.BlockSpec(
            (rows // pieces, block), lambda s, pos: (0, jnp.clip(s - i * sub, 0, sub - 1))
        )

    operands = [weight, *[piece for part in parts for piece in part]]
    in_specs = [pl.BlockSpec((block, out_width), weight_block)]
    in_specs += [part_spec(i) for i in range(count) for _ in range(pieces)]
    if start is not None:
        operands.append(start)
        in_specs.append(whole(start))
    return run(
        kernel,
        (count * sub,),
        operands,
        in_specs,
        jax.ShapeDtypeStruct((rows, out_width), jnp.float32),
        pl.BlockSpec((rows, out_width), lambda s, pos: (0, 0)),
    )


def join_blend(run, parts, kept, from_side, scales):
    rows = parts.shape[0] + kept.shape[0]
    heads = parts.shape[1] // 3 // HEAD_DIM

    def kernel(pos, *refs):
        part_refs, kept_refs, side_refs = refs[:3], refs[3:6], refs[6:9]
        *scale_refs, out_ref = refs[9:]
        raws = [k[...] + s[...].astype(jnp.float32) for k, s in zip(kept_refs, side_refs)]
        late = [unit_norm(raws[i], scale_refs[i][...]) for i in range(2)]
        late.append(raws[2].astype(jnp.bfloat16))
        query, key, value = (
            jnp.concatenate((part_refs[i][...], late[i])) for i in range(3)
        )
        out_ref[...] = softmax_blend(query, key, value)

    def specs(array):
        return [
            pl.BlockSpec((array.shape[0], HEAD_DIM), lambda h, pos, i=i: (0, i * heads + h))
            for i in range(3)
        ]

    scale_spec = pl.BlockSpec((1, HEAD_DIM), lambda h, pos: (0, mine_of(pos) * heads + h))
    return run(
        kernel,
        (heads,),
        (*[parts] * 3, *[kept] * 3, *[from_side] * 3, *scales),
        (*specs(parts), *specs(kept), *specs(from_side), *[scale_spec] * 2),
        jax.ShapeDtypeStruct((rows, heads * HEAD_DIM), jnp.bfloat16),
        pl.BlockSpec((rows, HEAD_DIM), lambda h, pos: (0, h)),
    )


def moment_pair(values):
    return jnp.stack((jnp.sum(values, 1), jnp.sum(values * values, 1)))


def moment_flips(pair):
    return pair, flip(pair, 1), flip(pair, 2), flip(pair, 3)


def moment_sum(pairs):
    return (pairs[0] + pairs[1]) + (pairs[2] + pairs[3])


def sent(array, shift):
    return row_shift(array.astype(jnp.bfloat16), shift)


def moment_shards(total):
    return total, row_shift(total, 1), row_shift(total, -1), row_shift(total, 2)


def normed_shards(shards, scales, totals):
    return jnp.concatenate(
        [normalize(x.astype(jnp.float32), scales, m) for x, m in zip(shards, totals)]
    )


def sync(*values):
    return lax.optimization_barrier(values)


def scatter_rows(terms):
    own, before, after, away = jnp.split(terms, 4)
    half = own.shape[0] // 2

    def send(array, shift):
        return sent(array, shift).astype(jnp.float32)

    to_after = send(away[:half], 1)
    to_before = send(away[half:], -1)
    from_before = jnp.concatenate((send(after[:half] + to_after, 1), send(after[half:], 1)))
    from_after = jnp.concatenate((send(before[:half], -1), send(before[half:] + to_before, -1)))
    return own + from_before + from_after


def fast_body(
    camera_tokens,
    norm_gain,
    query_weight,
    key_weight,
    value_weight,
    query_gain,
    key_gain,
    out_weight,
    up_weight,
    up_bias,
    down_weight,
    down_bias,
    join_gain,
    join_query,
    join_key,
    join_value,
    join_query_gain,
    join_key_gain,
    join_out,
):
    half = TOK_CAM
    index = lax.axis_index("cols")
    run = Runner(jnp.stack((index & 1, index >> 1)).astype(jnp.int32))
    head_width = query_weight.shape[1] // 4
    unit_width = up_weight.shape[1] // 4
    sub = 2 if unit_width % 256 == 0 else 1
    heads_in = (query_weight, key_weight, value_weight)
    join_in = (join_query, join_key, join_value)
    scales = (query_gain[None], key_gain[None])
    join_scales = (join_query_gain[None], join_key_gain[None])
    bias = up_bias[None]

    def heads_send(tokens, weights):
        return project_send(run, tokens, weights, head_width, 1)

    def heads_across(tokens, weights, arrived, pieces=1):
        return project_across(run, tokens, weights, head_width, 1, arrived, pieces)

    def heads_out(parts, first=0, start=None):
        return contract(run, [(part,) for part in parts], out_weight, 1, first, start)

    def units_down(parts, first, start):
        return contract(run, parts, down_weight, 1 if len(parts) > 1 else 2, first, start)

    def units_send(tokens):
        return project_send(run, tokens, (up_weight,), unit_width, 1)

    def units_across(tokens, arrived, pieces):
        return project_across(run, tokens, (up_weight,), unit_width, sub, arrived, pieces)

    def units_end(tokens, arrived, side, at=0):
        return project_hidden(run, tokens, up_weight, bias, unit_width, sub, arrived, side, at)

    def layer_end(start, own, *arrived):
        total = own
        for term in arrived:
            total = total + term.astype(jnp.float32)
        return (start + total + down_bias).astype(jnp.bfloat16)

    start_f32 = camera_tokens.astype(jnp.float32)
    own_a, own_b = camera_tokens[:half], camera_tokens[half:]
    pairs = moment_flips(moment_pair(start_f32))
    own_a, own_b, a_before, a_after, *pairs = sync(
        own_a, own_b, sent(own_a, 1), sent(own_a, -1), *pairs
    )

    totals = moment_shards(moment_sum(pairs))
    own_a, own_b, a_before, a_after, a_away, *totals = sync(
        own_a, own_b, a_before, a_after, sent(a_before, 1), *totals
    )
    totals_a = [total[:, :half] for total in totals]
    totals_b = [total[:, half:] for total in totals]

    b_before = sent(own_b, 1)
    tok_a = normed_shards((own_a, a_before, a_after, a_away), norm_gain, totals_a)
    qs_a = heads_send(tok_a, heads_in)
    tok_a, own_b, b_before, qs_a = sync(tok_a, own_b, b_before, qs_a)

    b_after, qc_a = sent(own_b, -1), core_swap(qs_a)
    qx_a = heads_across(tok_a, heads_in, qc_a, 2)
    tok_a, own_b, b_before, b_after, qc_a, qx_a0, qx_a1 = sync(
        tok_a, own_b, b_before, b_after, qc_a, *qx_a
    )

    qy_a0 = y_swap(qx_a0)
    us_a = units_send(tok_a)
    tok_a, own_b, b_before, b_after, qc_a, us_a, qy_a0, qx_a1 = sync(
        tok_a, own_b, b_before, b_after, qc_a, us_a, qy_a0, qx_a1
    )

    uc_a, qy_a1, b_away = core_swap(us_a), y_swap(qx_a1), sent(b_before, 1)
    (ux_a,) = units_across(tok_a, uc_a, 1)
    tok_a, qc_a, uc_a, ux_a, qy_a0, qy_a1, own_b, b_before, b_after, b_away = sync(
        tok_a, qc_a, uc_a, ux_a, qy_a0, qy_a1, own_b, b_before, b_after, b_away
    )

    uy_a = y_swap(ux_a)
    tok_b = normed_shards((own_b, b_before, b_after, b_away), norm_gain, totals_b)
    qs_b = heads_send(tok_b, heads_in)
    us_b = units_send(tok_b)
    at_a = project_heads(run, tok_a, heads_in, scales, head_width, qc_a, (qy_a0, qy_a1), True)
    tok_a, tok_b, qs_b, us_b, at_a, uc_a, uy_a = sync(
        tok_a, tok_b, qs_b, us_b, at_a, uc_a, uy_a
    )

    at_ya, at_ca, qc_b, uc_b = y_swap(at_a), core_swap(at_a), core_swap(qs_b), core_swap(us_b)
    hd_a = units_end(tok_a, uc_a, uy_a)
    tok_b, at_a, at_ya, at_ca, qc_b, uc_b, hd_a = sync(
        tok_b, at_a, at_ya, at_ca, qc_b, uc_b, hd_a
    )

    hd_ya, hd_ca, at_fa = y_swap(hd_a), core_swap(hd_a), core_swap(at_ya)
    (qx_b,) = heads_across(tok_b, heads_in, qc_b)
    ux_b = units_across(tok_b, uc_b, 2)
    mixed_a = units_down(((hd_a,),), 0, heads_out((at_a, at_ca, at_ya)))
    tok_b, at_fa, hd_ya, hd_ca, qc_b, uc_b, qx_b, mixed_a, *ux_b = sync(
        tok_b, at_fa, hd_ya, hd_ca, qc_b, uc_b, qx_b, mixed_a, *ux_b
    )

    qy_b, hd_fa = y_swap(qx_b), core_swap(hd_ya)
    mixed_a = heads_out((at_fa,), 3, mixed_a)
    mixed_a = units_down(((hd_ca,), (hd_ya,), (hd_fa,)), 1, mixed_a)
    tok_b, mixed_a, qc_b, qy_b, uc_b, ux_b0, ux_b1 = sync(
        tok_b, mixed_a, qc_b, qy_b, uc_b, *ux_b
    )

    uy_b0 = y_swap(ux_b0)
    mine_a, before_a, after_a, away_a = jnp.split(mixed_a, 4)
    to_after = sent(away_a, 1)
    at_b = project_heads(run, tok_b, heads_in, scales, head_width, qc_b, (qy_b,), True)
    tok_b, uc_b, uy_b0, ux_b1, at_b, mine_a, before_a, after_a, to_after = sync(
        tok_b, uc_b, uy_b0, ux_b1, at_b, mine_a, before_a, after_a, to_after
    )

    from_before = sent(after_a + to_after.astype(jnp.float32), 1)
    from_after = sent(before_a, -1)
    uy_b1, at_yb, at_cb = y_swap(ux_b1), y_swap(at_b), core_swap(at_b)
    hd_b0 = units_end(tok_b, uc_b, uy_b0)
    mixed_b = heads_out((at_b, at_cb))
    tok_b, uc_b, uy_b1, hd_b0, at_yb, mixed_b, mine_a, *arrived = sync(
        tok_b, uc_b, uy_b1, hd_b0, at_yb, mixed_b, mine_a, from_before, from_after
    )

    hd_yb0, at_fb = y_swap(hd_b0), core_swap(at_yb)
    layer_a = layer_end(start_f32[:half], mine_a, *arrived)
    pairs = moment_flips(moment_pair(layer_a.astype(jnp.float32)))
    hd_b1 = units_end(tok_b, uc_b, uy_b1, 1)
    mixed_b = heads_out((at_yb, at_fb), 2, mixed_b)
    hd_b0, hd_b1, hd_yb0, mixed_b, layer_a, *pairs = sync(
        hd_b0, hd_b1, hd_yb0, mixed_b, layer_a, *pairs
    )

    hd_yb1, hd_cb0, hd_cb1 = y_swap(hd_b1), core_swap(hd_b0), core_swap(hd_b1)
    join_a = normalize(layer_a.astype(jnp.float32), join_gain, moment_sum(pairs))
    ja_before, ja_after = sent(join_a, 1), sent(join_a, -1)
    mixed_b = units_down(((hd_b0, hd_b1),), 0, mixed_b)
    hd_cb0, hd_cb1, hd_yb0, hd_yb1, mixed_b, layer_a, join_a, ja_before, ja_after = sync(
        hd_cb0, hd_cb1, hd_yb0, hd_yb1, mixed_b, layer_a, join_a, ja_before, ja_after
    )

    hd_fb0 = core_swap(hd_yb0)
    hd_fb1 = core_swap(hd_yb1)
    mixed_b = units_down(((hd_cb0, hd_cb1),), 1, mixed_b)
    hd_yb0, hd_yb1, hd_fb0, hd_fb1, mixed_b, join_a, ja_before, ja_after = sync(
        hd_yb0, hd_yb1, hd_fb0, hd_fb1, mixed_b, join_a, ja_before, ja_after
    )

    ja_away = sent(ja_before, 1)
    mixed_b = units_down(((hd_yb0, hd_yb1), (hd_fb0, hd_fb1)), 2, mixed_b)
    mixed_b, join_a, ja_before, ja_after, ja_away = sync(
        mixed_b, join_a, ja_before, ja_after, ja_away
    )

    mine_b, before_b, after_b, away_b = jnp.split(mixed_b, 4)
    to_after = sent(away_b, 1)
    tok_ja = jnp.concatenate((join_a, ja_before, ja_after, ja_away))
    js_a = heads_send(tok_ja, join_in)
    mine_b, before_b, after_b, to_after, tok_ja, js_a = sync(
        mine_b, before_b, after_b, to_after, tok_ja, js_a
    )

    from_before = sent(after_b + to_after.astype(jnp.float32), 1)
    from_after, jc_a = sent(before_b, -1), core_swap(js_a)
    jx_a = heads_across(tok_ja, join_in, jc_a, 2)
    tok_ja, jc_a, jx_a0, jx_a1, mine_b, *arrived = sync(
        tok_ja, jc_a, *jx_a, mine_b, from_before, from_after
    )

    layer_b = layer_end(start_f32[half:], mine_b, *arrived)
    pair = moment_pair(layer_b.astype(jnp.float32))
    pair = pair + flip(pair, 1)
    jb_before, jb_after, jy_a0 = sent(layer_b, 1), sent(layer_b, -1), y_swap(jx_a0)
    tok_ja, jc_a, jy_a0, jx_a1, layer_b, jb_before, jb_after, *pairs = sync(
        tok_ja, jc_a, jy_a0, jx_a1, layer_b, jb_before, jb_after, pair, flip(pair, 2)
    )

    totals = moment_shards(pairs[0] + pairs[1])
    jb_away = sent(jb_before, 1)
    jy_a1 = y_swap(jx_a1)
    tok_ja, jc_a, jy_a0, jy_a1, layer_b, jb_before, jb_after, jb_away, *totals = sync(
        tok_ja, jc_a, jy_a0, jy_a1, layer_b, jb_before, jb_after, jb_away, *totals
    )

    tok_jb = normed_shards((layer_b, jb_before, jb_after, jb_away), join_gain, totals)
    jc_b = core_swap(heads_send(tok_jb, join_in))
    (jx_b,) = heads_across(tok_jb, join_in, jc_b)
    tok_ja, jc_a, jy_a0, jy_a1, tok_jb, jc_b, jx_b = sync(
        tok_ja, jc_a, jy_a0, jy_a1, tok_jb, jc_b, jx_b
    )

    jy_b = y_swap(jx_b)
    parts_a = project_heads(
        run, tok_ja, join_in, join_scales, head_width, jc_a, (jy_a0, jy_a1), False
    )
    kept_b = project_keep(run, tok_jb, join_in, head_width, jc_b)
    jy_b, parts_a, kept_b = sync(jy_b, parts_a, kept_b)

    joined = join_blend(run, parts_a, kept_b, jy_b, join_scales)
    joined = joined.reshape(2, 4, half, head_width).swapaxes(0, 1).reshape(8 * half, head_width)
    jo_y, jo_c = y_swap(joined), core_swap(joined)
    jo_f = core_swap(jo_y)
    result = contract(run, ((joined,), (jo_c,), (jo_y,), (jo_f,)), join_out, 1)
    summed = scatter_rows(result)
    layer_own = jnp.concatenate((layer_a, layer_b))
    return (layer_own.astype(jnp.float32) + summed).astype(jnp.bfloat16)


def layer(*arrays):
    own_rows, heads_width = arrays[0].shape[0], arrays[2].shape[1]
    fits = lax.axis_size("cols") == 4 and lax.axis_size("rows") == 4
    fits = fits and own_rows == 2 * TOK_CAM and heads_width % (4 * HEAD_DIM) == 0
    return (fast_body if fits else generic_body)(*arrays)


def solution(mesh):
    in_specs = (
        P(("groups", "rows"), "cols"),
        P("cols"),
        P("cols", "rows"),
        P("cols", "rows"),
        P("cols", "rows"),
        P("rows"),
        P("rows"),
        P("rows", "cols"),
        P("cols", "rows"),
        P("rows"),
        P("rows", "cols"),
        P("cols"),
        P("cols"),
        P("cols", "rows"),
        P("cols", "rows"),
        P("cols", "rows"),
        P("rows"),
        P("rows"),
        P("rows", "cols"),
    )
    out_specs = P(("groups", "rows"), "cols")
    return jax.shard_map(layer, mesh=mesh, in_specs=in_specs, out_specs=out_specs, check_vma=False)
```
